256 devices in a mesh: ctx: 32 (over y, z), tp: 8 (over x, core).
Axes of the slice: x: 4, y: 4, z: 8, core: 2. Of those that a mesh axis runs over, the one named last changes fastest.
Arguments:
- context_queries: bfloat16 [24576, 8192], P('ctx', 'tp'), may hold values from -160 to 160
- context_keys: bfloat16 [24576, 1024], P('ctx', 'tp'), may hold values from -5 to 5
- context_values: bfloat16 [24576, 1024], P('ctx', 'tp'), may hold values from -6 to 6
- block_length: int32 [32], P('ctx'), may hold values from 1 to 768, 18432 in all
- question_queries: bfloat16 [256, 8192], P('ctx', 'tp'), may hold values from -160 to 160
- question_keys: bfloat16 [256, 1024], P('ctx', 'tp'), may hold values from -6 to 6
- question_values: bfloat16 [256, 1024], P('ctx', 'tp'), may hold values from -6 to 6
- query_position: int32 [256], P('ctx'), may hold values from 0 to 255, each once
- out_weight: bfloat16 [8192, 8192], P('tp', 'ctx'), may hold values from -0.0625 to 0.0625
Outputs:
- block_output: bfloat16 [24576, 8192], P('ctx', 'tp')
- answer: bfloat16 [256, 8192], P(None, 'ctx')
The draws below stay inside these ranges and needn't reach their ends.
Inputs may be any that keep to these rules, and one draw needn't show every extreme that they name: `block_length`: the largest entry equals 768; the entries sum to 18432. `query_position`: A permutation.
All inputs are finite; a program needn't handle non-finite values. No bound on the sum of `block_length` on one device may be relied on, other than what follows from the above.
Results may differ from the reference program's by a relative error of at most 0.008.
Values may be sent and summed in bfloat16 or wider, within the bound.
A program may use at most 192 MiB of HBM per device.

```python
import math
import jax
import jax.numpy as jnp
import numpy as np
from jax import lax

D = 8192
QUERY_HEADS = 64
KEY_VALUE_HEADS = 8
HEAD_SIZE = 128
BLOCK_TOKENS = 768
QUERY_ROW_COUNT = 256
CONTEXT_TOKENS = 24576
QUERY_ROWS_LOCAL = 8
N_CTX = 32


def shared_keys(key):
    return jax.random.truncated_normal(key, -5.0, 5.0, (CONTEXT_TOKENS, KEY_VALUE_HEADS * HEAD_SIZE), jnp.float32)


def draw_context_keys(key, part):
    base = shared_keys(key)
    return base.astype(jnp.bfloat16)


def draw_context_queries(key, part):
    key = jax.random.fold_in(key, 2)
    query_matrix = 2.5 * jax.random.truncated_normal(key, -6.0, 6.0, (CONTEXT_TOKENS, QUERY_HEADS * HEAD_SIZE), jnp.float32)
    return query_matrix.astype(jnp.bfloat16)


def draw_question_queries(key, part):
    key = jax.random.fold_in(key, 3)
    query_matrix = 2.5 * jax.random.truncated_normal(key, -6.0, 6.0, (QUERY_ROW_COUNT, QUERY_HEADS * HEAD_SIZE), jnp.float32)
    return query_matrix.astype(jnp.bfloat16)


def block_scale(rng, extent, shards, smallest, high):
    loudness = 1.0
    for dim, blocks in shards:
        steps = jax.random.uniform(jax.random.fold_in(jax.random.fold_in(rng, 6), dim), (blocks,), jnp.float32, smallest / len(shards), high / len(shards))
        loudness = loudness * jnp.repeat(jnp.exp(steps), extent[dim] // blocks).reshape((-1,) + (1,) * (len(extent) - 1 - dim))
    return loudness


def split_up(amount, total, limit, slope):
    portions = [(1 << 20) // math.isqrt(rank ** slope) + 1 for rank in range(2, amount + 1)]
    rest, counts = total - limit - (amount - 1), [1] * (amount - 1)
    while rest > 0:
        free = [i for i in range(amount - 1) if counts[i] < limit]
        mass, budget = sum([portions[i] for i in free]), rest
        for i in free:
            extra = min(limit - counts[i], max(1, budget * portions[i] // mass), rest)
            counts[i] = counts[i] + extra
            rest = rest - extra
    return np.array([limit] + counts)


def ragged(stream_key, amount, total, most, slope):
    if amount == 2:
        one = jax.random.randint(stream_key, (), max(1, total - most), min(most, total - 1) + 1)
        return jnp.stack([one, total - one])
    lengths = jnp.asarray(split_up(amount, total, most, slope), jnp.int32)
    twos = (amount - 1) // 2
    source_of, sink = lengths[1:1 + 2 * twos:2], lengths[2:2 + 2 * twos:2]
    room = jnp.minimum(source_of - 1, most - sink)
    moved = jax.random.randint(jax.random.fold_in(stream_key, 1), (twos,), 0, 1 << 20) % (room + 1)
    lengths = lengths.at[1:1 + 2 * twos:2].set(source_of - moved).at[2:2 + 2 * twos:2].set(sink + moved)
    return lengths[jax.random.permutation(jax.random.fold_in(stream_key, 2), amount)]


def centred(key, extent, scale, reach, cuts=(), kind=jnp.bfloat16):
    drawn = jax.random.normal(key, extent, jnp.float32) * scale
    if len(cuts) > 0:
        drawn = block_scale(key, extent, cuts, -0.22, 0.18) * drawn
    return jnp.clip(drawn, min=-reach, max=reach).astype(kind)


def setup_inputs(seed: int = 0) -> dict:
    key_of = jax.random.split(jax.random.key(seed), 10)
    context_queries = draw_context_queries(jax.random.fold_in(key_of[9], 71), 0)
    context_keys = draw_context_keys(jax.random.fold_in(key_of[9], 71), 0)
    context_values = centred(key_of[2], (CONTEXT_TOKENS, KEY_VALUE_HEADS * HEAD_SIZE), 1.0, 6.0, ((0, 32), (1, 8)))
    block_length = ragged(key_of[3], N_CTX, CONTEXT_TOKENS * 3 // 4, BLOCK_TOKENS, 1).astype(jnp.int32)
    question_queries = draw_question_queries(jax.random.fold_in(key_of[9], 71), 0)
    question_keys = centred(key_of[5], (QUERY_ROW_COUNT, KEY_VALUE_HEADS * HEAD_SIZE), 1.0, 6.0, ((0, 32), (1, 8)))
    question_values = centred(key_of[6], (QUERY_ROW_COUNT, KEY_VALUE_HEADS * HEAD_SIZE), 1.0, 6.0, ((0, 32), (1, 8)))
    query_position = jax.random.permutation(key_of[7], QUERY_ROW_COUNT).astype(jnp.int32)
    out_weight = centred(key_of[8], (QUERY_HEADS * HEAD_SIZE, D), (QUERY_HEADS * HEAD_SIZE) ** -0.5, 0.0625, ((0, 8), (1, 32)))
    return dict(context_queries=context_queries, context_keys=context_keys, context_values=context_values, block_length=block_length, question_queries=question_queries, question_keys=question_keys, question_values=question_values, query_position=query_position, out_weight=out_weight)


NEG = -1e+30

def softmax_parts(scores, visible, value_rows):
    masked = jnp.where(visible, scores, NEG)
    highest = lax.optimization_barrier(jnp.max(masked, axis=-1))
    weights = jnp.where(visible, jnp.exp(masked - highest[..., None]), 0.0)
    total = lax.optimization_barrier(jnp.sum(weights, axis=-1))
    rounded = weights.astype(jnp.bfloat16).astype(jnp.float32)
    return (highest, total, rounded, value_rows.astype(jnp.float32))

def encode_head(query_matrix, key_rows, value_rows, anchor_keys, anchor_values, own_length, anchor_length, uses_anchor):
    rows = query_matrix.shape[0]
    row_index = lax.broadcasted_iota(jnp.int32, (rows, rows), 0)
    col_index = lax.broadcasted_iota(jnp.int32, (rows, rows), 1)
    anchor_seen = (col_index < anchor_length) & uses_anchor
    own_seen = (col_index <= row_index) & (col_index < own_length)
    visible = jnp.concatenate([anchor_seen, own_seen], axis=1)
    keys_all = jnp.concatenate([anchor_keys, key_rows], axis=0)
    values_all = jnp.concatenate([anchor_values, value_rows], axis=0)
    scores = jnp.einsum('rgd,kd->grk', query_matrix.astype(jnp.float32), keys_all.astype(jnp.float32)) / math.sqrt(HEAD_SIZE)
    highest, total, rounded, values_wide = softmax_parts(scores, visible[None], values_all)
    summed = jnp.einsum('grk,kd->grd', rounded, values_wide)
    return jnp.transpose((summed / total[..., None]).astype(jnp.bfloat16), (1, 0, 2))

def combine(first, second):
    top = jnp.maximum(first[0], second[0])
    scale_a = jnp.exp(first[0] - top)
    scale_b = jnp.exp(second[0] - top)
    return (top, first[1] * scale_a + second[1] * scale_b, first[2] * scale_a[..., None] + second[2] * scale_b[..., None])

def reference(context_queries, context_keys, context_values, block_length, question_queries, question_keys, question_values, query_position, out_weight):
    head_group = QUERY_HEADS // KEY_VALUE_HEADS
    query_matrix = context_queries.reshape(N_CTX, BLOCK_TOKENS, KEY_VALUE_HEADS, head_group, HEAD_SIZE)
    key_rows = context_keys.reshape(N_CTX, BLOCK_TOKENS, KEY_VALUE_HEADS, HEAD_SIZE)
    value_rows = context_values.reshape(N_CTX, BLOCK_TOKENS, KEY_VALUE_HEADS, HEAD_SIZE)
    anchor_keys = key_rows[0]
    anchor_values = value_rows[0]
    anchor_length = block_length[0]

    def encode_block(packed):
        block_q, block_k, block_v, own_length, place = packed

        def per_head(head_pack):
            head_q, head_k, head_v, head_ak, head_av = head_pack
            return encode_head(head_q, head_k, head_v, head_ak, head_av, own_length, anchor_length, place != 0)
        outputs = lax.map(per_head, (jnp.transpose(block_q, (1, 0, 2, 3)), jnp.transpose(block_k, (1, 0, 2)), jnp.transpose(block_v, (1, 0, 2)), jnp.transpose(anchor_keys, (1, 0, 2)), jnp.transpose(anchor_values, (1, 0, 2))))
        return jnp.transpose(outputs, (1, 0, 2, 3)).reshape(BLOCK_TOKENS, QUERY_HEADS * HEAD_SIZE)
    places = jnp.arange(N_CTX, dtype=jnp.int32)
    block_output = lax.map(encode_block, (query_matrix, key_rows, value_rows, block_length, places)).reshape(CONTEXT_TOKENS, QUERY_HEADS * HEAD_SIZE)
    asked_rows = question_queries.reshape(QUERY_ROW_COUNT, KEY_VALUE_HEADS, head_group, HEAD_SIZE).astype(jnp.float32)
    local_keys = question_keys.reshape(N_CTX, QUERY_ROWS_LOCAL, KEY_VALUE_HEADS, HEAD_SIZE)
    local_values = question_values.reshape(N_CTX, QUERY_ROWS_LOCAL, KEY_VALUE_HEADS, HEAD_SIZE)
    own_position = query_position.reshape(N_CTX, QUERY_ROWS_LOCAL)

    def phase_two(carry, packed):
        block_k, block_v, own_length, q_keys, q_values, q_position = packed
        keys_all = jnp.concatenate([block_k, q_keys], axis=0).astype(jnp.float32)
        values_all = jnp.concatenate([block_v, q_values], axis=0)
        context_seen = jnp.broadcast_to(jnp.arange(BLOCK_TOKENS, dtype=jnp.int32)[None, :] < own_length, (QUERY_ROW_COUNT, BLOCK_TOKENS))
        query_seen = q_position[None, :] <= query_position[:, None]
        visible = jnp.concatenate([context_seen, query_seen], axis=1)
        scores = jnp.einsum('qhgd,khd->hgqk', asked_rows, keys_all) / math.sqrt(HEAD_SIZE)
        highest, total, rounded, values_wide = softmax_parts(scores, visible[None, None], values_all)
        summed = jnp.einsum('hgqk,khd->hgqd', rounded, values_wide)
        part = (highest.reshape(QUERY_HEADS, QUERY_ROW_COUNT), total.reshape(QUERY_HEADS, QUERY_ROW_COUNT), summed.reshape(QUERY_HEADS, QUERY_ROW_COUNT, HEAD_SIZE))
        return (combine(carry, part), None)
    start = (jnp.full((QUERY_HEADS, QUERY_ROW_COUNT), NEG, jnp.float32), jnp.zeros((QUERY_HEADS, QUERY_ROW_COUNT), jnp.float32), jnp.zeros((QUERY_HEADS, QUERY_ROW_COUNT, HEAD_SIZE), jnp.float32))
    final, _ = lax.scan(phase_two, start, (key_rows, value_rows, block_length, local_keys, local_values, own_position))
    attention = (final[2] / final[1][..., None]).astype(jnp.bfloat16)
    weight = out_weight.reshape(QUERY_HEADS, HEAD_SIZE, D)
    answer = jnp.einsum('hqd,hde->qe', attention.astype(jnp.float32), weight.astype(jnp.float32))
    return (block_output, answer.astype(jnp.bfloat16))
```

```python
import functools
import math

import jax
import jax.numpy as jnp
from jax import lax
from jax.experimental import pallas as pl
from jax.experimental.pallas import tpu as pltpu
from jax.sharding import PartitionSpec as P

MESH = pl.DeviceIdType.MESH
NT = (((1,), (1,)), ((), ()))
BF = jnp.bfloat16
F32 = jnp.float32
NEG = -1e30
HD = 128
HEADS = 8
NY, NZ, TP = 4, 8, 8
ROWS = 768
QROWS = 8
TILE = 256
NRB = ROWS // TILE
SL = ROWS * 2 // (NY * NZ)
QUARTER = SL * NZ
SCALE = math.log2(math.e) / math.sqrt(HD)
LOG2E = math.log2(math.e)
ZORDER = (1, 7, 2, 6, 3, 5, 4)
YORDER = (1, 3, 2)
HG = 4

S_Q, S_SM, S_KV, S_AA, S_AB, S_AC, S_AD = 0, 7, 10, 16, 23, 26, 33
S_PZ, S_TZ, S_TY, S_RX, S_GX = 36, 43, 50, 74, 81
N_SEM = 88


def live_keys(live, keys, kk, values, va, rows):
    kk[rows, :] = keys
    va[rows, :HD] = jnp.where(live, values, jnp.zeros_like(values))
    va[rows, HD:] = jnp.where(live, 1.0, 0.0).astype(BF)


def kernel(
    cq, ck, cv, blen, qq, qk, qv, qpos, w,
    out, ans,
    cqv, wv, kvb, kk, va, akk, ava, bias,
    mo, acco, obuf,
    qbuf, sml, rst, ast, akv,
    p2kk, p2va, m2, acc2,
    cmsg, crecv, abuf, pown, psend, prec, ansb,
    ss, rs, ls,
):
    ctx = lax.axis_index("ctx")
    t = lax.axis_index("tp")
    y, z = ctx // NZ, lax.rem(ctx, NZ)

    def at_z(d):
        return lax.rem(z + d + NZ, NZ)

    def at_y(d):
        return lax.rem(y + d + NY, NY)

    def at_t(d):
        return lax.rem(t + d + TP, TP)

    def dev(yy, zz, tt):
        return (yy * NZ + zz, tt)

    def remote(src, dst, si, ri, device):
        return pltpu.make_async_remote_copy(
            src_ref=src, dst_ref=dst, send_sem=ss.at[si], recv_sem=rs.at[ri],
            device_id=device, device_id_type=MESH,
        )

    def recv(dst, ri):
        remote(dst, dst, ri, ri, dev(at_y(1), z, t)).wait_recv()

    sends = []

    def send(src, dst, si, device):
        copy = remote(src, dst, si, si, device)
        copy.start()
        sends.append(copy)

    barrier = pltpu.get_barrier_semaphore()
    peers = (
        [dev(y, at_z(d), t) for d in range(1, NZ)]
        + [dev(at_y(d), z, t) for d in range(1, NY)]
        + [dev(y, z, at_t(d)) for d in range(1, TP)]
    )
    for peer in peers:
        pl.semaphore_signal(barrier, inc=1, device_id=peer, device_id_type=MESH)
    loads = [
        pltpu.make_async_copy(src.at[pl.ds(i * QUARTER, QUARTER)], kvb.at[y, 2 * n + i], ls.at[2 * n + i])
        for n, src in enumerate((ck, cv)) for i in range(2)
    ]
    for copy in loads:
        copy.start()
    load_q = pltpu.make_async_copy(cq, cqv, ls.at[4])
    load_q.start()
    load_w = pltpu.make_async_copy(w, wv, ls.at[5])
    load_w.start()

    row8 = lax.broadcasted_iota(jnp.int32, (8, HD), 0)
    lane8 = lax.broadcasted_iota(jnp.int32, (8, HD), 1)
    qf = qq[...].astype(F32)
    qbuf[z, 0:64, :] = jnp.concatenate([qf[:, h * HD:(h + 1) * HD] for h in range(HEADS)], axis=0).astype(BF)
    pos = jnp.zeros((8, HD), jnp.int32)
    key_pos = jnp.full((8, HD), 512, jnp.int32)
    for r in range(QROWS):
        pos = jnp.where(row8 == r, qpos[r], pos)
        key_pos = jnp.where(lane8 == y * QROWS + r, qpos[r], key_pos)
    pos = pos.astype(F32)
    key_pos = key_pos.astype(F32)
    qbuf[z, 64:80, :] = jnp.concatenate([pos, pos], axis=0).astype(BF)
    length = jnp.zeros((8, HD), jnp.int32) + blen[0]
    info = jnp.concatenate([length // 128, lax.rem(length, 128)], axis=0).astype(F32).astype(BF)
    sml[y, 0:16, :] = jnp.concatenate([qk[...].astype(F32), qv[...].astype(F32)], axis=0).astype(BF)
    sml[y, 16:32, :] = jnp.concatenate([key_pos, key_pos], axis=0).astype(BF)
    sml[y, 32:48, :] = info

    for copy in loads:
        copy.wait()
    pl.semaphore_wait(barrier, len(peers))

    for d in ZORDER:
        send(qbuf.at[z], qbuf.at[z], S_Q + d - 1, dev(y, at_z(d), t))
    up, down = dev(at_y(1), z, t), dev(at_y(3), z, t)
    keys, values = pl.ds(0, 2), pl.ds(2, 2)
    send(kvb.at[y, keys], kvb.at[y, keys], S_KV, up)
    send(kvb.at[y, values], kvb.at[y, values], S_KV + 2, down)
    for d in YORDER:
        send(sml.at[y], sml.at[y], S_SM + d - 1, dev(at_y(d), z, t))
    send(kvb.at[y, values], kvb.at[y, values], S_KV + 1, up)
    send(kvb.at[y, keys], kvb.at[y, keys], S_KV + 3, down)

    root = (y == 0) & (z == 0)

    @pl.when(root)
    def _():
        for j in range(NZ):
            for i in range(4):
                rst[j, i, 0:SL, :] = kvb[0, i, j * SL:(j + 1) * SL, :]
                rst[j, i, SL:SL + 16, :] = info
        ast[...] = rst[0]
        for j in range(1, NZ):
            remote(rst.at[j], ast, S_AA + j - 1, S_AA, dev(0, j, t)).start()

    row_of = lax.broadcasted_iota(jnp.int32, (QUARTER, HD), 0)
    for i in range(2):
        live = row_of + i * QUARTER < blen[0]
        live_keys(
            live, jnp.where(live, kvb[y, i], kvb[y, 0, 0:1, :]), kk, kvb[y, 2 + i], va,
            slice(i * QUARTER, (i + 1) * QUARTER),
        )
    rr = lax.broadcasted_iota(jnp.int32, (TILE, TILE), 0)
    cc = lax.broadcasted_iota(jnp.int32, (TILE, TILE), 1)
    bias[...] = jnp.where(cc <= rr, 0.0, NEG)
    load_q.wait()

    def own_step(rb, h):
        qt = cqv[rb * TILE:(rb + 1) * TILE, pl.ds(pl.multiple_of(h * HD, HD), HD)]
        diagonal = slice(rb * TILE, (rb + 1) * TILE)
        sd = lax.dot_general(qt, kk[diagonal], NT, preferred_element_type=F32) + bias[...]
        top = jnp.max(sd, axis=1, keepdims=True)
        if rb:
            so = lax.dot_general(qt, kk[0:rb * TILE], NT, preferred_element_type=F32)
            top = jnp.maximum(top, jnp.max(so, axis=1, keepdims=True))
        top_s = top * SCALE
        pd = jnp.exp2(sd * SCALE - top_s).astype(BF)
        acc = jnp.dot(pd, va[diagonal], preferred_element_type=F32)
        if rb:
            po = jnp.exp2(so * SCALE - top_s).astype(BF)
            acc = acc + jnp.dot(po, va[0:rb * TILE], preferred_element_type=F32)
        acco[rb * HEADS + h] = acc
        mo[rb * HEADS + h] = jnp.broadcast_to(top_s, (TILE, HD))

    def own_steps(rb):
        @pl.loop(0, HEADS // HG)
        def _(i):
            for u in range(HG):
                own_step(rb, i * HG + u)

    own_steps(0)
    own_steps(1)


    @pl.when(y == 0)
    def _():
        @pl.when(z != 0)
        def _():
            recv(ast, S_AA)
        akv[0, z] = ast[0]
        for d in range(1, NY):
            remote(ast.at[d], akv.at[d, z], S_AB + d - 1, S_AB, dev(d, z, t)).start()

    own_steps(2)

    below, above, opposite = at_y(3), at_y(1), at_y(2)
    recv(kvb.at[below, keys], S_KV)
    send(kvb.at[below, keys], kvb.at[below, keys], S_KV + 4, up)
    recv(kvb.at[above, values], S_KV + 2)
    send(kvb.at[above, values], kvb.at[above, values], S_KV + 5, down)

    @pl.when(y != 0)
    def _():
        recv(akv.at[y, z], S_AB)

    for d in ZORDER:
        send(akv.at[y, z], akv.at[y, z], S_AC + d - 1, dev(y, at_z(d), t))

    for d in range(1, NZ):
        recv(qbuf.at[at_z(-d)], S_Q + d - 1)
    for d in range(1, NY):
        recv(sml.at[at_y(-d)], S_SM + d - 1)
    half = NZ // 2 * 64

    def asked(i):
        return jnp.concatenate([qbuf[i * 4 + j, 0:64, :] for j in range(4)], axis=0)

    small = [sml[j].astype(F32) for j in range(NY)]
    zero96 = jnp.zeros((HD - NY * QROWS, HD), F32)
    ext_k = jnp.concatenate([s[0:8] for s in small] + [zero96], axis=0).astype(BF)
    ext_v = jnp.concatenate([s[8:16] for s in small] + [zero96], axis=0).astype(BF)
    ext_va = jnp.concatenate([ext_v, jnp.ones((HD, HD), BF)], axis=1)
    ext_pos = functools.reduce(jnp.minimum, [s[16:17] for s in small])

    for i in range(2):
        qt = asked(i)
        rows_pos = jnp.concatenate(
            [p for j in range(4) for p in [qbuf[i * 4 + j, 64:80, :].astype(F32)[0:8]] * HEADS], axis=0
        )
        se = lax.dot_general(qt, ext_k, NT, preferred_element_type=F32)
        se = jnp.where(ext_pos <= rows_pos, se, NEG)
        sa = lax.dot_general(qt, kk[...], NT, preferred_element_type=F32)
        top = jnp.maximum(jnp.max(se, axis=1, keepdims=True), jnp.max(sa, axis=1, keepdims=True)) * SCALE
        acc = jnp.dot(jnp.exp2(sa * SCALE - top).astype(BF), va[...], preferred_element_type=F32)
        acc = acc + jnp.dot(jnp.exp2(se * SCALE - top).astype(BF), ext_va, preferred_element_type=F32)
        m2[i * half:(i + 1) * half] = jnp.broadcast_to(top, (half, HD))
        acc2[i * half:(i + 1) * half] = acc

    def phase_two(slot):
        length = (sml[slot, 32:48, :].astype(F32))
        live_to = length[0:1] * 128.0 + length[8:9]
        for i in range(2):
            live = (row_of + i * QUARTER).astype(F32) < live_to
            live_keys(
                live, jnp.where(live, kvb[slot, i], kvb[slot, 0, 0:1, :]), p2kk, kvb[slot, 2 + i], p2va,
                slice(i * QUARTER, (i + 1) * QUARTER),
            )
        for i in range(2):
            part = slice(i * half, (i + 1) * half)
            sa = lax.dot_general(asked(i), p2kk[...], NT, preferred_element_type=F32)
            old = m2[part]
            top = jnp.maximum(jnp.max(sa, axis=1, keepdims=True) * SCALE, old)
            acc = jnp.dot(jnp.exp2(sa * SCALE - top[:, 0:1]).astype(BF), p2va[...], preferred_element_type=F32)
            keep = jnp.exp2(old - top)
            acc2[part] = acc + acc2[part] * jnp.concatenate([keep, keep], axis=1)
            m2[part] = top

    recv(kvb.at[below, values], S_KV + 1)
    phase_two(below)
    recv(kvb.at[above, keys], S_KV + 3)
    phase_two(above)

    for d in range(1, NZ):
        recv(akv.at[y, at_z(-d)], S_AC + d - 1)
    data = pl.ds(0, SL)
    for d in YORDER:
        send(akv.at[y, :, data], akv.at[y, :, data], S_AD + d - 1, dev(at_y(d), z, t))

    recv(kvb.at[opposite, keys], S_KV + 4)
    recv(kvb.at[opposite, values], S_KV + 5)
    phase_two(opposite)

    total = acc2[:, HD:]
    lse = m2[...] + jnp.log(total) * LOG2E
    part_out = acc2[:, :HD] / total
    for j in range(NZ):
        compact = jnp.zeros((8, HD), F32)
        for h in range(HEADS):
            compact = jnp.where(lane8 == h, lse[j * 64 + h * 8:j * 64 + h * 8 + 8], compact)
        first = compact.astype(BF).astype(F32)
        second = (compact - first).astype(BF).astype(F32)
        third = compact - first - second
        cmsg[j, 0:64, :] = part_out[j * 64:(j + 1) * 64].astype(BF)
        cmsg[j, 64:96, :] = jnp.concatenate([first, second, third, jnp.zeros((8, HD), F32)], axis=0).astype(BF)
    for d in ZORDER:
        send(cmsg.at[at_z(d)], crecv.at[z], S_PZ + d - 1, dev(y, at_z(d), t))

    for d in range(1, NY):
        recv(akv.at[at_y(-d), :, data], S_AD + d - 1)
    alen = akv[y, z, SL:SL + 16, :].astype(F32)
    alive_to = jnp.where(ctx == 0, 0.0, alen[0:1] * 128.0 + alen[8:9])
    for i in range(2):
        live = (row_of + i * QUARTER).astype(F32) < alive_to
        live_keys(
            live,
            jnp.where(live, akv[i, :, 0:SL, :].reshape(QUARTER, HD), akv[0, 0, 0:1, :]),
            akk,
            akv[2 + i, :, 0:SL, :].reshape(QUARTER, HD),
            ava,
            slice(i * QUARTER, (i + 1) * QUARTER),
        )

    def anchor_step(rb, h):
        cols = pl.ds(pl.multiple_of(h * HD, HD), HD)
        rows = slice(rb * TILE, (rb + 1) * TILE)
        sa = lax.dot_general(cqv[rows, cols], akk[...], NT, preferred_element_type=F32)
        old = mo[rb * HEADS + h]
        top = jnp.maximum(jnp.max(sa, axis=1, keepdims=True) * SCALE, old)
        acc = jnp.dot(jnp.exp2(sa * SCALE - top[:, 0:1]).astype(BF), ava[...], preferred_element_type=F32)
        keep = jnp.exp2(old - top)
        acc = acc + acco[rb * HEADS + h] * jnp.concatenate([keep, keep], axis=1)
        obuf[rows, cols] = (acc[:, :HD] / acc[:, HD:]).astype(BF)

    stores = [
        pltpu.make_async_copy(
            obuf.at[pl.ds(rb * TILE, TILE)], out.at[pl.ds(rb * TILE, TILE)], ls.at[6 + rb]
        )
        for rb in range(NRB)
    ]

    def anchor_steps(rb):
        @pl.loop(0, HEADS // HG)
        def _(i):
            for u in range(HG):
                anchor_step(rb, i * HG + u)

        stores[rb].start()

    anchor_steps(0)
    anchor_steps(1)

    for d in range(1, NZ):
        recv(crecv.at[at_z(-d)], S_PZ + d - 1)
    parts = [cmsg[z].astype(F32)] + [crecv[at_z(-d)].astype(F32) for d in range(1, NZ)]
    lses = [p[64:72] + p[72:80] + p[80:88] for p in parts]
    top = functools.reduce(jnp.maximum, lses)
    weights = [jnp.exp2(x - top) for x in lses]
    weight_sum = functools.reduce(jnp.add, weights)
    weights = [x / weight_sum for x in weights]
    merged = []
    for h in range(HEADS):
        merged.append(functools.reduce(
            jnp.add, [x[:, h:h + 1] * p[h * 8:h * 8 + 8] for x, p in zip(weights, parts)]
        ))
    merged = jnp.concatenate(
        [jnp.concatenate(merged[0:4], axis=1), jnp.concatenate(merged[4:8], axis=1)], axis=0
    )
    abuf[y, z] = merged.astype(BF)

    for d in ZORDER:
        send(abuf.at[y, z], abuf.at[y, z], S_TZ + d - 1, dev(y, at_z(d), t))
    for k in (0,) + ZORDER:
        zz = at_z(-k)
        if k:
            recv(abuf.at[y, zz], S_TZ + k - 1)
        for d in YORDER:
            send(abuf.at[y, zz], abuf.at[y, zz], S_TY + 3 * k + d - 1, dev(at_y(d), z, t))

    anchor_steps(2)
    load_w.wait()
    for k in range(NZ):
        for d in range(1, NY):
            recv(abuf.at[at_y(-d), at_z(-k)], S_TY + 3 * k + d - 1)

    rows = abuf[...].reshape(NY * NZ * 16, 4 * HD)
    low = jnp.dot(rows, wv[0:4 * HD], preferred_element_type=F32).reshape(NY * NZ, 16, -1)
    high = jnp.dot(rows, wv[4 * HD:], preferred_element_type=F32).reshape(NY * NZ, 16, -1)
    partial = (low[:, 0:8] + high[:, 8:16]).reshape(pown.shape)
    pown[...] = partial
    psend[...] = partial.astype(BF)
    for d in range(1, TP):
        send(psend.at[at_t(d)], prec.at[t], S_RX + d - 1, dev(y, z, at_t(d)))
    for d in range(1, TP):
        recv(prec.at[at_t(-d)], S_RX + d - 1)
    answer = pown[t]
    for d in range(1, TP):
        answer = answer + prec[at_t(-d)].astype(F32)
    ansb[t] = answer.astype(BF)
    for d in range(1, TP):
        send(ansb.at[t], ansb.at[t], S_GX + d - 1, dev(y, z, at_t(d)))
    for d in range(1, TP):
        recv(ansb.at[at_t(-d)], S_GX + d - 1)
    ans[...] = ansb[...].reshape(ans.shape)

    for copy in sends:
        copy.wait_send()

    @pl.when(root)
    def _():
        for j in range(1, NZ):
            remote(rst.at[j], ast, S_AA + j - 1, S_AA, dev(0, j, t)).wait_send()

    @pl.when(y == 0)
    def _():
        for d in range(1, NY):
            remote(ast.at[d], akv.at[d, z], S_AB + d - 1, S_AB, dev(d, z, t)).wait_send()

    for copy in stores:
        copy.wait()


def body(cq, ck, cv, blen, qq, qk, qv, qpos, w):
    hbm = pl.BlockSpec(memory_space=pl.ANY)
    vmem = pl.BlockSpec(memory_space=pltpu.VMEM)
    smem = pl.BlockSpec(memory_space=pltpu.SMEM)
    columns = w.shape[1]
    v = pltpu.VMEM
    return pl.pallas_call(
        kernel,
        out_shape=(
            jax.ShapeDtypeStruct(cq.shape, BF),
            jax.ShapeDtypeStruct((NY * NZ * QROWS, columns), BF),
        ),
        in_specs=[hbm, hbm, hbm, smem, vmem, vmem, vmem, smem, hbm],
        out_specs=(hbm, vmem),
        scratch_shapes=[
            v(cq.shape, BF),
            v(w.shape, BF),
            v((NY, 4, QUARTER, HD), BF),
            v((ROWS, HD), BF),
            v((ROWS, 2 * HD), BF),
            v((ROWS, HD), BF),
            v((ROWS, 2 * HD), BF),
            v((TILE, TILE), F32),
            v((NRB * HEADS, TILE, HD), F32),
            v((NRB * HEADS, TILE, 2 * HD), F32),
            v(cq.shape, BF),
            v((NZ, 80, HD), BF),
            v((NY, 48, HD), BF),
            v((NZ, 4, SL + 16, HD), BF),
            v((4, SL + 16, HD), BF),
            v((4, NZ, SL + 16, HD), BF),
            v((ROWS, HD), BF),
            v((ROWS, 2 * HD), BF),
            v((NZ * 64, HD), F32),
            v((NZ * 64, 2 * HD), F32),
            v((NZ, 96, HD), BF),
            v((NZ, 96, HD), BF),
            v((NY, NZ, 16, 4 * HD), BF),
            v((TP, NY * NZ, columns), F32),
            v((TP, NY * NZ, columns), BF),
            v((TP, NY * NZ, columns), BF),
            v((TP, NY * NZ, columns), BF),
            pltpu.SemaphoreType.DMA((N_SEM,)),
            pltpu.SemaphoreType.DMA((N_SEM,)),
            pltpu.SemaphoreType.DMA((9,)),
        ],
        compiler_params=pltpu.CompilerParams(
            collective_id=1, has_side_effects=True, vmem_limit_bytes=48 * 2**20
        ),
        name="star_attention",
    )(cq, ck, cv, blen, qq, qk, qv, qpos, w)


def solution(mesh):
    in_specs = (
        P("ctx", "tp"),
        P("ctx", "tp"),
        P("ctx", "tp"),
        P("ctx"),
        P("ctx", "tp"),
        P("ctx", "tp"),
        P("ctx", "tp"),
        P("ctx"),
        P("tp", "ctx"),
    )
    out_specs = (P("ctx", "tp"), P(None, "ctx"))
    return jax.shard_map(body, mesh=mesh, in_specs=in_specs, out_specs=out_specs, check_vma=False)
```

```python
import functools
import math

import jax
import jax.numpy as jnp
from jax import lax
from jax.experimental import pallas as pl
from jax.experimental.pallas import tpu as pltpu
from jax.sharding import PartitionSpec as P

MESH = pl.DeviceIdType.MESH
NT = (((1,), (1,)), ((), ()))
BF = jnp.bfloat16
F32 = jnp.float32
NEG = -1e30
HD = 128
HEADS = 8
NY, NZ, TP = 4, 8, 8
ROWS = 768
QROWS = 8
TILE = 256
NRB = ROWS // TILE
SL = ROWS * 2 // (NY * NZ)
THIRD = ROWS // 3
SCALE = math.log2(math.e) / math.sqrt(HD)
LOG2E = math.log2(math.e)
ZORDER = (1, 7, 2, 6, 3, 5, 4)
YORDER = (1, 3, 2)
HG = 4

S_Q, S_SM, S_KV, S_AA, S_AB, S_AC, S_AD = 0, 7, 10, 16, 23, 26, 33
S_PZ, S_TZ, S_TY, S_RX, S_GX = 36, 43, 50, 74, 81
N_SEM = 88


def kernel(
    cq, ck, cv, blen, qq_hbm, qk_hbm, qv_hbm, qpos, w,
    out, ans,
    qq, qk, qv, cqv, wv, kvb, kk, va, akk, ava, bias,
    mo, acco, obuf,
    qbuf, sml, rst, ast, akv,
    p2kk, p2va, m2, acc2,
    cmsg, crecv, abuf, pown, psend, prec, ansb,
    ss, rs, ls,
):
    ctx = lax.axis_index("ctx")
    t = lax.axis_index("tp")
    z = lax.rem(ctx, NZ)
    c = lax.rem(ctx // NZ + 2 * z, NY)

    def at_z(d):
        return lax.rem(z + d + NZ, NZ)

    def at_c(d):
        return lax.rem(c + d + NY, NY)

    def at_t(d):
        return lax.rem(t + d + TP, TP)

    def dev(cc, zz, tt):
        return (lax.rem(cc + 2 * zz, NY) * NZ + zz, tt)

    def z_to(d):
        return at_z(-1) if d == 2 else z

    def z_from(d):
        return at_z(1) if d == 2 else z

    def next_to(d):
        return dev(at_c(d), z_to(d), t)

    def remote(src, dst, si, ri, device):
        return pltpu.make_async_remote_copy(
            src_ref=src, dst_ref=dst, send_sem=ss.at[si], recv_sem=rs.at[ri],
            device_id=device, device_id_type=MESH,
        )

    def recv(dst, ri):
        remote(dst, dst, ri, ri, next_to(1)).wait_recv()

    sends = []

    def send(src, dst, si, device):
        copy = remote(src, dst, si, si, device)
        copy.start()
        sends.append(copy)

    barrier = pltpu.get_barrier_semaphore()
    peers = (
        [dev(c, at_z(d), t) for d in range(1, NZ)]
        + [dev(at_c(1), z, t), dev(at_c(3), z, t), dev(at_c(2), at_z(1), t), dev(at_c(2), at_z(-1), t)]
        + [dev(c, z, at_t(d)) for d in range(1, TP)]
    )
    for peer in peers:
        pl.semaphore_signal(barrier, inc=1, device_id=peer, device_id_type=MESH)
    small_loads = [
        pltpu.make_async_copy(src, dst, ls.at[n])
        for n, (src, dst) in enumerate(((qq_hbm, qq), (qk_hbm, qk), (qv_hbm, qv)))
    ]
    loads = [
        pltpu.make_async_copy(src.at[pl.ds(a * THIRD, THIRD)], kvb.at[c, a, n], ls.at[3 + 2 * a + n])
        for a in range(3) for n, src in enumerate((ck, cv))
    ]
    load_q = pltpu.make_async_copy(cq, cqv, ls.at[9])
    load_w = pltpu.make_async_copy(w, wv, ls.at[10])
    for copy in small_loads + loads + [load_q, load_w]:
        copy.start()
    for copy in small_loads:
        copy.wait()

    row8 = lax.broadcasted_iota(jnp.int32, (8, HD), 0)
    lane8 = lax.broadcasted_iota(jnp.int32, (8, HD), 1)
    qf = qq[...].astype(F32)
    qbuf[z, 0:64, :] = jnp.concatenate([qf[:, h * HD:(h + 1) * HD] for h in range(HEADS)], axis=0).astype(BF)
    pos = jnp.zeros((8, HD), jnp.int32)
    key_pos = jnp.full((8, HD), 512, jnp.int32)
    for r in range(QROWS):
        pos = jnp.where(row8 == r, qpos[r], pos)
        key_pos = jnp.where(lane8 == c * QROWS + r, qpos[r], key_pos)
    pos = pos.astype(F32)
    key_pos = key_pos.astype(F32)
    qbuf[z, 64:80, :] = jnp.concatenate([pos, pos], axis=0).astype(BF)
    length = jnp.zeros((8, HD), jnp.int32) + blen[0]
    info = jnp.concatenate([length // 128, lax.rem(length, 128)], axis=0).astype(F32).astype(BF)
    sml[c, 0:16, :] = jnp.concatenate([qk[...].astype(F32), qv[...].astype(F32)], axis=0).astype(BF)
    sml[c, 16:32, :] = jnp.concatenate([key_pos, key_pos], axis=0).astype(BF)
    sml[c, 32:48, :] = info

    for copy in loads:
        copy.wait()
    pl.semaphore_wait(barrier, len(peers))

    for d in ZORDER:
        send(qbuf.at[z], qbuf.at[z], S_Q + d - 1, dev(c, at_z(d), t))
    first, second = pl.ds(0, 2), pl.ds(2, 1)
    for d in YORDER:
        send(kvb.at[c, first], kvb.at[c, first], S_KV + 2 * (d - 1), next_to(d))
    for d in YORDER:
        send(sml.at[c], sml.at[c], S_SM + d - 1, next_to(d))
    for d in YORDER:
        send(kvb.at[c, second], kvb.at[c, second], S_KV + 2 * (d - 1) + 1, next_to(d))

    root = ctx == 0

    @pl.when(root)
    def _():
        for j in range(NZ):
            for i in range(4):
                for q in range(SL // 16):
                    row = (i * NZ + (j - 1) % NZ if i == 2 else i * NZ + j) * SL + 16 * q
                    a, n, r = row // (2 * THIRD), row // THIRD % 2, row % THIRD
                    rst[j, i, 16 * q:16 * q + 16, :] = kvb[0, a, n, r:r + 16, :]
                rst[j, i, SL:SL + 16, :] = info
        ast[...] = rst[0]
        for j in range(1, NZ):
            remote(rst.at[j], ast, S_AA + j - 1, S_AA, dev(0, j, t)).start()

    row_of = lax.broadcasted_iota(jnp.int32, (THIRD, HD), 0)

    def live_keys(live, keys, other, values, to_kk, to_va, rows):
        to_kk[rows, :] = jnp.where(live, keys, other)
        to_va[rows, :HD] = jnp.where(live, values, jnp.zeros_like(values))
        to_va[rows, HD:] = jnp.where(live, 1.0, 0.0).astype(BF)

    for a in range(3):
        live_keys(
            row_of + a * THIRD < blen[0], kvb[c, a, 0], kvb[c, 0, 0, 0:1, :], kvb[c, a, 1],
            kk, va, slice(a * THIRD, (a + 1) * THIRD),
        )
    rr = lax.broadcasted_iota(jnp.int32, (TILE, TILE), 0)
    cc = lax.broadcasted_iota(jnp.int32, (TILE, TILE), 1)
    bias[...] = jnp.where(cc <= rr, 0.0, NEG)
    load_q.wait()

    def own_step(rb, h):
        qt = cqv[rb * TILE:(rb + 1) * TILE, pl.ds(pl.multiple_of(h * HD, HD), HD)]
        diagonal = slice(rb * TILE, (rb + 1) * TILE)
        sd = lax.dot_general(qt, kk[diagonal], NT, preferred_element_type=F32) + bias[...]
        top = jnp.max(sd, axis=1, keepdims=True)
        if rb:
            so = lax.dot_general(qt, kk[0:rb * TILE], NT, preferred_element_type=F32)
            top = jnp.maximum(top, jnp.max(so, axis=1, keepdims=True))
        top_s = top * SCALE
        pd = jnp.exp2(sd * SCALE - top_s).astype(BF)
        acc = jnp.dot(pd, va[diagonal], preferred_element_type=F32)
        if rb:
            po = jnp.exp2(so * SCALE - top_s).astype(BF)
            acc = acc + jnp.dot(po, va[0:rb * TILE], preferred_element_type=F32)
        acco[rb * HEADS + h] = acc
        mo[rb * HEADS + h] = jnp.broadcast_to(top_s, (TILE, HD))

    def own_steps(rb):
        @pl.loop(0, HEADS // HG)
        def _(i):
            for u in range(HG):
                own_step(rb, i * HG + u)

    own_steps(0)

    @pl.when(c == 0)
    def _():
        @pl.when(z != 0)
        def _():
            recv(ast, S_AA)
        akv[0, z] = ast[0]
        for d in range(1, NY):
            remote(ast.at[d], akv.at[d, z_to(d)], S_AB + d - 1, S_AB, next_to(d)).start()

    own_steps(1)

    @pl.when(c != 0)
    def _():
        recv(akv.at[c, z], S_AB)

    for d in ZORDER:
        send(akv.at[c, z], akv.at[c, z], S_AC + d - 1, dev(c, at_z(d), t))

    for d in range(1, NZ):
        recv(qbuf.at[at_z(-d)], S_Q + d - 1)
    for d in range(1, NY):
        recv(sml.at[at_c(-d)], S_SM + d - 1)
    half = NZ // 2 * 64

    def asked(i):
        return jnp.concatenate([qbuf[i * 4 + j, 0:64, :] for j in range(4)], axis=0)

    small = [sml[j].astype(F32) for j in range(NY)]
    zero96 = jnp.zeros((HD - NY * QROWS, HD), F32)
    ext_k = jnp.concatenate([s[0:8] for s in small] + [zero96], axis=0).astype(BF)
    ext_v = jnp.concatenate([s[8:16] for s in small] + [zero96], axis=0).astype(BF)
    ext_va = jnp.concatenate([ext_v, jnp.ones((HD, HD), BF)], axis=1)
    ext_pos = functools.reduce(jnp.minimum, [s[16:17] for s in small])

    for i in range(2):
        qt = asked(i)
        rows_pos = jnp.concatenate(
            [p for j in range(4) for p in [qbuf[i * 4 + j, 64:80, :].astype(F32)[0:8]] * HEADS], axis=0
        )
        se = lax.dot_general(qt, ext_k, NT, preferred_element_type=F32)
        se = jnp.where(ext_pos <= rows_pos, se, NEG)
        sa = lax.dot_general(qt, kk[...], NT, preferred_element_type=F32)
        top = jnp.maximum(jnp.max(se, axis=1, keepdims=True), jnp.max(sa, axis=1, keepdims=True)) * SCALE
        acc = jnp.dot(jnp.exp2(sa * SCALE - top).astype(BF), va[...], preferred_element_type=F32)
        acc = acc + jnp.dot(jnp.exp2(se * SCALE - top).astype(BF), ext_va, preferred_element_type=F32)
        m2[i * half:(i + 1) * half] = jnp.broadcast_to(top, (half, HD))
        acc2[i * half:(i + 1) * half] = acc

    def phase_two(thirds):
        at = 0
        for d in range(1, NY):
            slot = at_c(-d)
            length = sml[slot, 32:48, :].astype(F32)
            live_to = length[0:1] * 128.0 + length[8:9]
            for a in thirds:
                live_keys(
                    (row_of + a * THIRD).astype(F32) < live_to, kvb[slot, a, 0], kvb[slot, 0, 0, 0:1, :],
                    kvb[slot, a, 1], p2kk, p2va, slice(at, at + THIRD),
                )
                at += THIRD
        for i in range(2):
            part = slice(i * half, (i + 1) * half)
            sa = lax.dot_general(asked(i), p2kk[0:at], NT, preferred_element_type=F32)
            old = m2[part]
            top = jnp.maximum(jnp.max(sa, axis=1, keepdims=True) * SCALE, old)
            acc = jnp.dot(jnp.exp2(sa * SCALE - top[:, 0:1]).astype(BF), p2va[0:at], preferred_element_type=F32)
            keep = jnp.exp2(old - top)
            acc2[part] = acc + acc2[part] * jnp.concatenate([keep, keep], axis=1)
            m2[part] = top

    for d in range(1, NY):
        recv(kvb.at[at_c(-d), first], S_KV + 2 * (d - 1))
    phase_two((0, 1))
    for d in range(1, NY):
        recv(kvb.at[at_c(-d), second], S_KV + 2 * (d - 1) + 1)
    phase_two((2,))

    total = acc2[:, HD:]
    lse = m2[...] + jnp.log(total) * LOG2E
    part_out = acc2[:, :HD] / total
    for j in range(NZ):
        compact = jnp.zeros((8, HD), F32)
        for h in range(HEADS):
            compact = jnp.where(lane8 == h, lse[j * 64 + h * 8:j * 64 + h * 8 + 8], compact)
        high = compact.astype(BF).astype(F32)
        middle = (compact - high).astype(BF).astype(F32)
        low = compact - high - middle
        cmsg[j, 0:64, :] = part_out[j * 64:(j + 1) * 64].astype(BF)
        cmsg[j, 64:96, :] = jnp.concatenate([high, middle, low, jnp.zeros((8, HD), F32)], axis=0).astype(BF)
    for d in ZORDER:
        send(cmsg.at[at_z(d)], crecv.at[z], S_PZ + d - 1, dev(c, at_z(d), t))

    own_steps(2)

    for d in range(1, NZ):
        recv(akv.at[c, at_z(-d)], S_AC + d - 1)
    data = pl.ds(0, SL)
    for d in YORDER:
        send(akv.at[c, :, data], akv.at[c, :, data], S_AD + d - 1, next_to(d))

    for d in range(1, NZ):
        recv(crecv.at[at_z(-d)], S_PZ + d - 1)
    parts = [cmsg[z].astype(F32)] + [crecv[at_z(-d)].astype(F32) for d in range(1, NZ)]
    lses = [p[64:72] + p[72:80] + p[80:88] for p in parts]
    top = functools.reduce(jnp.maximum, lses)
    weights = [jnp.exp2(x - top) for x in lses]
    weight_sum = functools.reduce(jnp.add, weights)
    weights = [x / weight_sum for x in weights]
    merged = []
    for h in range(HEADS):
        merged.append(functools.reduce(
            jnp.add, [x[:, h:h + 1] * p[h * 8:h * 8 + 8] for x, p in zip(weights, parts)]
        ))
    merged = jnp.concatenate(
        [jnp.concatenate(merged[0:4], axis=1), jnp.concatenate(merged[4:8], axis=1)], axis=0
    )
    abuf[c, z] = merged.astype(BF)

    for d in ZORDER:
        send(abuf.at[c, z], abuf.at[c, z], S_TZ + d - 1, dev(c, at_z(d), t))

    def pass_on(k):
        zz = at_z(-k)
        if k:
            recv(abuf.at[c, zz], S_TZ + k - 1)
        for d in YORDER:
            send(abuf.at[c, zz], abuf.at[c, zz], S_TY + 3 * k + d - 1, next_to(d))

    pass_on(0)

    for d in range(1, NY):
        recv(akv.at[at_c(-d), :, data], S_AD + d - 1)
    alen = akv[c, z, SL:SL + 16, :].astype(F32)
    alive_to = jnp.where(ctx == 0, 0.0, alen[0:1] * 128.0 + alen[8:9])
    anchor = akv[:, :, 0:SL, :].reshape(2 * ROWS, HD)
    for a in range(3):
        keys_at = 2 * a * THIRD
        live_keys(
            (row_of + a * THIRD).astype(F32) < alive_to, anchor[keys_at:keys_at + THIRD], anchor[0:1],
            anchor[keys_at + THIRD:keys_at + 2 * THIRD], akk, ava, slice(a * THIRD, (a + 1) * THIRD),
        )

    def anchor_step(rb, h):
        cols = pl.ds(pl.multiple_of(h * HD, HD), HD)
        rows = slice(rb * TILE, (rb + 1) * TILE)
        sa = lax.dot_general(cqv[rows, cols], akk[...], NT, preferred_element_type=F32)
        old = mo[rb * HEADS + h]
        top = jnp.maximum(jnp.max(sa, axis=1, keepdims=True) * SCALE, old)
        acc = jnp.dot(jnp.exp2(sa * SCALE - top[:, 0:1]).astype(BF), ava[...], preferred_element_type=F32)
        keep = jnp.exp2(old - top)
        acc = acc + acco[rb * HEADS + h] * jnp.concatenate([keep, keep], axis=1)
        obuf[rows, cols] = (acc[:, :HD] / acc[:, HD:]).astype(BF)

    stores = [
        pltpu.make_async_copy(obuf.at[pl.ds(rb * TILE, TILE)], out.at[pl.ds(rb * TILE, TILE)], ls.at[rb])
        for rb in range(NRB)
    ]

    def anchor_steps(rb):
        @pl.loop(0, HEADS // HG)
        def _(i):
            for u in range(HG):
                anchor_step(rb, i * HG + u)

        stores[rb].start()

    anchor_steps(0)
    for k in ZORDER:
        pass_on(k)
    anchor_steps(1)
    load_w.wait()
    for k in range(NZ):
        for d in range(1, NY):
            recv(abuf.at[at_c(-d), lax.rem(z_from(d) - k + NZ, NZ)], S_TY + 3 * k + d - 1)

    rows = jnp.concatenate([abuf[(yy + 2 * zz) % NY, zz] for yy in range(NY) for zz in range(NZ)], axis=0)
    upper = jnp.dot(rows, wv[0:4 * HD], preferred_element_type=F32).reshape(NY * NZ, 16, -1)
    lower = jnp.dot(rows, wv[4 * HD:], preferred_element_type=F32).reshape(NY * NZ, 16, -1)
    partial = (upper[:, 0:8] + lower[:, 8:16]).reshape(pown.shape)
    pown[...] = partial
    psend[...] = partial.astype(BF)
    for d in range(1, TP):
        send(psend.at[at_t(d)], prec.at[t], S_RX + d - 1, dev(c, z, at_t(d)))
    anchor_steps(2)
    for d in range(1, TP):
        recv(prec.at[at_t(-d)], S_RX + d - 1)
    answer = pown[t]
    for d in range(1, TP):
        answer = answer + prec[at_t(-d)].astype(F32)
    ansb[t] = answer.astype(BF)
    for d in range(1, TP):
        send(ansb.at[t], ansb.at[t], S_GX + d - 1, dev(c, z, at_t(d)))
    for d in range(1, TP):
        recv(ansb.at[at_t(-d)], S_GX + d - 1)
    ans[...] = ansb[...].reshape(ans.shape)

    for copy in sends:
        copy.wait_send()

    @pl.when(root)
    def _():
        for j in range(1, NZ):
            remote(rst.at[j], ast, S_AA + j - 1, S_AA, dev(0, j, t)).wait_send()

    @pl.when(c == 0)
    def _():
        for d in range(1, NY):
            remote(ast.at[d], akv.at[d, z_to(d)], S_AB + d - 1, S_AB, next_to(d)).wait_send()

    for copy in stores:
        copy.wait()


def body(cq, ck, cv, blen, qq, qk, qv, qpos, w):
    hbm = pl.BlockSpec(memory_space=pl.ANY)
    vmem = pl.BlockSpec(memory_space=pltpu.VMEM)
    smem = pl.BlockSpec(memory_space=pltpu.SMEM)
    columns = w.shape[1]
    v = pltpu.VMEM
    return pl.pallas_call(
        kernel,
        out_shape=(
            jax.ShapeDtypeStruct(cq.shape, BF),
            jax.ShapeDtypeStruct((NY * NZ * QROWS, columns), BF),
        ),
        in_specs=[hbm, hbm, hbm, smem, hbm, hbm, hbm, smem, hbm],
        out_specs=(hbm, vmem),
        scratch_shapes=[
            v(qq.shape, BF),
            v(qk.shape, BF),
            v(qv.shape, BF),
            v(cq.shape, BF),
            v(w.shape, BF),
            v((NY, 3, 2, THIRD, HD), BF),
            v((ROWS, HD), BF),
            v((ROWS, 2 * HD), BF),
            v((ROWS, HD), BF),
            v((ROWS, 2 * HD), BF),
            v((TILE, TILE), F32),
            v((NRB * HEADS, TILE, HD), F32),
            v((NRB * HEADS, TILE, 2 * HD), F32),
            v(cq.shape, BF),
            v((NZ, 80, HD), BF),
            v((NY, 48, HD), BF),
            v((NZ, 4, SL + 16, HD), BF),
            v((4, SL + 16, HD), BF),
            v((4, NZ, SL + 16, HD), BF),
            v((2 * ROWS, HD), BF),
            v((2 * ROWS, 2 * HD), BF),
            v((NZ * 64, HD), F32),
            v((NZ * 64, 2 * HD), F32),
            v((NZ, 96, HD), BF),
            v((NZ, 96, HD), BF),
            v((NY, NZ, 16, 4 * HD), BF),
            v((TP, NY * NZ, columns), F32),
            v((TP, NY * NZ, columns), BF),
            v((TP, NY * NZ, columns), BF),
            v((TP, NY * NZ, columns), BF),
            pltpu.SemaphoreType.DMA((N_SEM,)),
            pltpu.SemaphoreType.DMA((N_SEM,)),
            pltpu.SemaphoreType.DMA((12,)),
        ],
        compiler_params=pltpu.CompilerParams(
            collective_id=1, has_side_effects=True, vmem_limit_bytes=63 * 2**20
        ),
        name="star_attention",
    )(cq, ck, cv, blen, qq, qk, qv, qpos, w)


def solution(mesh):
    in_specs = (
        P("ctx", "tp"),
        P("ctx", "tp"),
        P("ctx", "tp"),
        P("ctx"),
        P("ctx", "tp"),
        P("ctx", "tp"),
        P("ctx", "tp"),
        P("ctx"),
        P("tp", "ctx"),
    )
    out_specs = (P("ctx", "tp"), P(None, "ctx"))
    return jax.shard_map(body, mesh=mesh, in_specs=in_specs, out_specs=out_specs, check_vma=False)
```

```python
import functools
import math

import jax
import jax.numpy as jnp
from jax import lax
from jax.experimental import pallas as pl
from jax.experimental.pallas import tpu as pltpu
from jax.sharding import PartitionSpec as P

MESH = pl.DeviceIdType.MESH
NT = (((1,), (1,)), ((), ()))
BF = jnp.bfloat16
F32 = jnp.float32
NEG = -1e30
HD = 128
HEADS = 8
NY, NZ, TP = 4, 8, 8
ROWS = 768
QROWS = 8
TILE = 256
NRB = ROWS // TILE
SL = ROWS * 2 // (NY * NZ)
THIRD = ROWS // 3
SCALE = math.log2(math.e) / math.sqrt(HD)
LOG2E = math.log2(math.e)
ZORDER = (1, 7, 2, 6, 3, 5, 4)
YORDER = (1, 3, 2)
COPIES = 4
HG = 4

S_Q, S_SM, S_KV, S_AA, S_AB, S_AC, S_AD = 0, 7, 10, 16, 23, 26, 33
S_PZ, S_TZ, S_TY, S_RX, S_GX = 36, 43, 50, 74, 81
N_SEM = 88


def kernel(
    cq, ck, cv, blen, qq_hbm, qk_hbm, qv_hbm, qpos, w,
    out, ans,
    qq, qk, qv, cqv, wv, kvb, kk, va, akk, ava, bias,
    mo, acco, obuf,
    qbuf, sml, rst, ast, akv,
    p2kk, p2va, m2, acc2,
    cmsg, crecv, abuf, pown, psend, prec, ansb,
    ss, rs, ls,
):
    ctx = lax.axis_index("ctx")
    t = lax.axis_index("tp")
    z = lax.rem(ctx, NZ)
    c = lax.rem(ctx // NZ + 2 * z, NY)

    def at_z(d):
        return lax.rem(z + d + NZ, NZ)

    def at_c(d):
        return lax.rem(c + d + NY, NY)

    def at_t(d):
        return lax.rem(t + d + TP, TP)

    def dev(cc, zz, tt):
        return (lax.rem(cc + 2 * zz, NY) * NZ + zz, tt)

    def z_to(d):
        return at_z(-1) if d == 2 else z

    def z_from(d):
        return at_z(1) if d == 2 else z

    def next_to(d):
        return dev(at_c(d), z_to(d), t)

    def remote(src, dst, si, ri, device):
        return pltpu.make_async_remote_copy(
            src_ref=src, dst_ref=dst, send_sem=ss.at[si], recv_sem=rs.at[ri],
            device_id=device, device_id_type=MESH,
        )

    def recv(dst, ri):
        remote(dst, dst, ri, ri, next_to(1)).wait_recv()

    sends = []

    def send(src, dst, si, device):
        copy = remote(src, dst, si, si, device)
        copy.start()
        sends.append(copy)

    barrier = pltpu.get_barrier_semaphore()
    peers = (
        [dev(c, at_z(d), t) for d in range(1, NZ)]
        + [dev(at_c(1), z, t), dev(at_c(3), z, t), dev(at_c(2), at_z(1), t), dev(at_c(2), at_z(-1), t)]
        + [dev(c, z, at_t(d)) for d in range(1, TP)]
    )
    for peer in peers:
        pl.semaphore_signal(barrier, inc=1, device_id=peer, device_id_type=MESH)
    small_loads = [
        pltpu.make_async_copy(src, dst, ls.at[n])
        for n, (src, dst) in enumerate(((qq_hbm, qq), (qk_hbm, qk), (qv_hbm, qv)))
    ]
    loads = [
        pltpu.make_async_copy(src.at[pl.ds(a * THIRD, THIRD)], kvb.at[c, a, n], ls.at[3 + 2 * a + n])
        for a in range(3) for n, src in enumerate((ck, cv))
    ]
    load_q = pltpu.make_async_copy(cq, cqv, ls.at[9])
    load_w = pltpu.make_async_copy(w, wv, ls.at[10])
    for copy in small_loads + loads + [load_q, load_w]:
        copy.start()
    for copy in small_loads:
        copy.wait()

    row8 = lax.broadcasted_iota(jnp.int32, (8, HD), 0)
    lane8 = lax.broadcasted_iota(jnp.int32, (8, HD), 1)
    qf = qq[...].astype(F32)
    qbuf[z, 0:64, :] = jnp.concatenate([qf[:, h * HD:(h + 1) * HD] for h in range(HEADS)], axis=0).astype(BF)
    pos = jnp.zeros((8, HD), jnp.int32)
    key_pos = jnp.full((8, HD), 512, jnp.int32)
    for r in range(QROWS):
        pos = jnp.where(row8 == r, qpos[r], pos)
        key_pos = jnp.where(lane8 == c * QROWS + r, qpos[r], key_pos)
    pos = pos.astype(F32)
    key_pos = key_pos.astype(F32)
    qbuf[z, 64:80, :] = jnp.concatenate([pos, pos], axis=0).astype(BF)
    length = jnp.zeros((8, HD), jnp.int32) + blen[0]
    info = jnp.concatenate([length // 128, lax.rem(length, 128)], axis=0).astype(F32).astype(BF)
    sml[c, 0:16, :] = jnp.concatenate([qk[...].astype(F32), qv[...].astype(F32)], axis=0).astype(BF)
    sml[c, 16:32, :] = jnp.concatenate([key_pos, key_pos], axis=0).astype(BF)
    sml[c, 32:48, :] = info

    for copy in loads:
        copy.wait()
    pl.semaphore_wait(barrier, len(peers))

    for d in ZORDER:
        send(qbuf.at[z], qbuf.at[z], S_Q + d - 1, dev(c, at_z(d), t))
    first, second = pl.ds(0, 2), pl.ds(2, 1)
    for d in YORDER:
        send(kvb.at[c, first], kvb.at[c, first], S_KV + 2 * (d - 1), next_to(d))
    for d in YORDER:
        send(sml.at[c], sml.at[c], S_SM + d - 1, next_to(d))
    for d in YORDER:
        send(kvb.at[c, second], kvb.at[c, second], S_KV + 2 * (d - 1) + 1, next_to(d))

    root = ctx == 0

    @pl.when(root)
    def _():
        for j in range(NZ):
            for i in range(4):
                for q in range(SL // 16):
                    row = (i * NZ + (j - 1) % NZ if i == 2 else i * NZ + j) * SL + 16 * q
                    a, n, r = row // (2 * THIRD), row // THIRD % 2, row % THIRD
                    rst[j, i, 16 * q:16 * q + 16, :] = kvb[0, a, n, r:r + 16, :]
                rst[j, i, SL:SL + 16, :] = info
        ast[...] = rst[0]
        for j in range(1, NZ):
            remote(rst.at[j], ast, S_AA + j - 1, S_AA, dev(0, j, t)).start()

    row_of = lax.broadcasted_iota(jnp.int32, (THIRD, HD), 0)

    def live_keys(live, keys, other, values, to_kk, to_va, rows):
        to_kk[rows, :] = jnp.where(live, keys, other)
        to_va[rows, :HD] = jnp.where(live, values, jnp.zeros_like(values))
        to_va[rows, HD:] = jnp.where(live, 1.0, 0.0).astype(BF)

    for a in range(3):
        live_keys(
            row_of + a * THIRD < blen[0], kvb[c, a, 0], kvb[c, 0, 0, 0:1, :], kvb[c, a, 1],
            kk, va, slice(a * THIRD, (a + 1) * THIRD),
        )
    rr = lax.broadcasted_iota(jnp.int32, (TILE, TILE), 0)
    cc = lax.broadcasted_iota(jnp.int32, (TILE, TILE), 1)
    bias[...] = jnp.where(cc <= rr, 0.0, NEG)
    load_q.wait()

    def own_step(rb, h):
        qt = cqv[rb * TILE:(rb + 1) * TILE, pl.ds(pl.multiple_of(h * HD, HD), HD)]
        diagonal = slice(rb * TILE, (rb + 1) * TILE)
        sd = lax.dot_general(qt, kk[diagonal], NT, preferred_element_type=F32) + bias[...]
        top = jnp.max(sd, axis=1, keepdims=True)
        if rb:
            so = lax.dot_general(qt, kk[0:rb * TILE], NT, preferred_element_type=F32)
            top = jnp.maximum(top, jnp.max(so, axis=1, keepdims=True))
        top_s = top * SCALE
        pd = jnp.exp2(sd * SCALE - top_s).astype(BF)
        acc = jnp.dot(pd, va[diagonal], preferred_element_type=F32)
        if rb:
            po = jnp.exp2(so * SCALE - top_s).astype(BF)
            acc = acc + jnp.dot(po, va[0:rb * TILE], preferred_element_type=F32)
        acco[rb * HEADS + h] = acc
        mo[rb * HEADS + h] = jnp.broadcast_to(top_s, (TILE, HD))

    def own_steps(rb):
        @pl.loop(0, HEADS // HG)
        def _(i):
            for u in range(HG):
                own_step(rb, i * HG + u)

    own_steps(0)

    own_steps(1)

    for d in range(1, NZ):
        recv(qbuf.at[at_z(-d)], S_Q + d - 1)
    for d in range(1, NY):
        recv(sml.at[at_c(-d)], S_SM + d - 1)
    half = NZ // 2 * 64

    def asked(i):
        return jnp.concatenate([qbuf[i * 4 + j, 0:64, :] for j in range(4)], axis=0)

    small = [sml[j].astype(F32) for j in range(NY)]
    zero96 = jnp.zeros((HD - NY * QROWS, HD), F32)
    ext_k = jnp.concatenate([s[0:8] for s in small] + [zero96], axis=0).astype(BF)
    ext_v = jnp.concatenate([s[8:16] for s in small] + [zero96], axis=0).astype(BF)
    ext_va = jnp.concatenate([ext_v, jnp.ones((HD, HD), BF)], axis=1)
    ext_pos = functools.reduce(jnp.minimum, [s[16:17] for s in small])

    for i in range(2):
        qt = asked(i)
        rows_pos = jnp.concatenate(
            [p for j in range(4) for p in [qbuf[i * 4 + j, 64:80, :].astype(F32)[0:8]] * HEADS], axis=0
        )
        se = lax.dot_general(qt, ext_k, NT, preferred_element_type=F32)
        se = jnp.where(ext_pos <= rows_pos, se, NEG)
        sa = lax.dot_general(qt, kk[...], NT, preferred_element_type=F32)
        top = jnp.maximum(jnp.max(se, axis=1, keepdims=True), jnp.max(sa, axis=1, keepdims=True)) * SCALE
        acc = jnp.dot(jnp.exp2(sa * SCALE - top).astype(BF), va[...], preferred_element_type=F32)
        acc = acc + jnp.dot(jnp.exp2(se * SCALE - top).astype(BF), ext_va, preferred_element_type=F32)
        m2[i * half:(i + 1) * half] = jnp.broadcast_to(top, (half, HD))
        acc2[i * half:(i + 1) * half] = acc

    def phase_two(thirds):
        at = 0
        for d in range(1, NY):
            slot = at_c(-d)
            length = sml[slot, 32:48, :].astype(F32)
            live_to = length[0:1] * 128.0 + length[8:9]
            for a in thirds:
                live_keys(
                    (row_of + a * THIRD).astype(F32) < live_to, kvb[slot, a, 0], kvb[slot, 0, 0, 0:1, :],
                    kvb[slot, a, 1], p2kk, p2va, slice(at, at + THIRD),
                )
                at += THIRD
        for i in range(2):
            part = slice(i * half, (i + 1) * half)
            sa = lax.dot_general(asked(i), p2kk[0:at], NT, preferred_element_type=F32)
            old = m2[part]
            top = jnp.maximum(jnp.max(sa, axis=1, keepdims=True) * SCALE, old)
            acc = jnp.dot(jnp.exp2(sa * SCALE - top[:, 0:1]).astype(BF), p2va[0:at], preferred_element_type=F32)
            keep = jnp.exp2(old - top)
            acc2[part] = acc + acc2[part] * jnp.concatenate([keep, keep], axis=1)
            m2[part] = top

    for d in range(1, NY):
        recv(kvb.at[at_c(-d), first], S_KV + 2 * (d - 1))
    phase_two((0, 1))
    @pl.when(c == 0)
    def _():
        @pl.when(z != 0)
        def _():
            recv(ast, S_AA)
        akv[0, z] = ast[0]
        for d in range(1, NY):
            remote(ast.at[d], akv.at[d, z_to(d)], S_AB + d - 1, S_AB, next_to(d)).start()

    for d in range(1, NY):
        recv(kvb.at[at_c(-d), second], S_KV + 2 * (d - 1) + 1)
    phase_two((2,))

    total = acc2[:, HD:]
    lse = m2[...] + jnp.log(total) * LOG2E
    part_out = acc2[:, :HD] / total
    for j in range(NZ):
        compact = jnp.zeros((8, HD), F32)
        for h in range(HEADS):
            compact = jnp.where(lane8 == h, lse[j * 64 + h * 8:j * 64 + h * 8 + 8], compact)
        high = compact.astype(BF).astype(F32)
        middle = (compact - high).astype(BF).astype(F32)
        low = compact - high - middle
        cmsg[j, 0:64, :] = part_out[j * 64:(j + 1) * 64].astype(BF)
        cmsg[j, 64:96, :] = jnp.concatenate([high, middle, low, jnp.zeros((8, HD), F32)], axis=0).astype(BF)
    for d in ZORDER:
        send(cmsg.at[at_z(d)], crecv.at[z], S_PZ + d - 1, dev(c, at_z(d), t))

    @pl.when(c != 0)
    def _():
        recv(akv.at[c, z], S_AB)

    for d in ZORDER:
        send(akv.at[c, z], akv.at[c, z], S_AC + d - 1, dev(c, at_z(d), t))

    own_steps(2)

    for d in range(1, NZ):
        recv(crecv.at[at_z(-d)], S_PZ + d - 1)
    parts = [cmsg[z].astype(F32)] + [crecv[at_z(-d)].astype(F32) for d in range(1, NZ)]
    lses = [p[64:72] + p[72:80] + p[80:88] for p in parts]
    top = functools.reduce(jnp.maximum, lses)
    weights = [jnp.exp2(x - top) for x in lses]
    weight_sum = functools.reduce(jnp.add, weights)
    weights = [x / weight_sum for x in weights]
    merged = []
    for h in range(HEADS):
        merged.append(functools.reduce(
            jnp.add, [x[:, h:h + 1] * p[h * 8:h * 8 + 8] for x, p in zip(weights, parts)]
        ))
    merged = jnp.concatenate(
        [jnp.concatenate(merged[0:4], axis=1), jnp.concatenate(merged[4:8], axis=1)], axis=0
    )
    abuf[c, z] = merged.astype(BF)

    for d in ZORDER:
        send(abuf.at[c, z], abuf.at[c, z], S_TZ + d - 1, dev(c, at_z(d), t))

    def pass_on(k):
        zz = at_z(-k)
        if k:
            recv(abuf.at[c, zz], S_TZ + k - 1)
        for d in YORDER:
            send(abuf.at[c, zz], abuf.at[c, zz], S_TY + 3 * k + d - 1, next_to(d))

    pass_on(0)
    for d in range(1, NZ):
        recv(akv.at[c, at_z(-d)], S_AC + d - 1)
    data = pl.ds(0, SL)
    for d in YORDER:
        send(akv.at[c, :, data], akv.at[c, :, data], S_AD + d - 1, next_to(d))

    for k in ZORDER:
        pass_on(k)

    for d in range(1, NY):
        recv(akv.at[at_c(-d), :, data], S_AD + d - 1)
    alen = akv[c, z, SL:SL + 16, :].astype(F32)
    alive_to = jnp.where(ctx == 0, 0.0, alen[0:1] * 128.0 + alen[8:9])
    anchor = akv[:, :, 0:SL, :].reshape(2 * ROWS, HD)
    for a in range(3):
        keys_at = 2 * a * THIRD
        live_keys(
            (row_of + a * THIRD).astype(F32) < alive_to, anchor[keys_at:keys_at + THIRD], anchor[0:1],
            anchor[keys_at + THIRD:keys_at + 2 * THIRD], akk, ava, slice(a * THIRD, (a + 1) * THIRD),
        )

    def anchor_step(rb, h):
        cols = pl.ds(pl.multiple_of(h * HD, HD), HD)
        rows = slice(rb * TILE, (rb + 1) * TILE)
        sa = lax.dot_general(cqv[rows, cols], akk[...], NT, preferred_element_type=F32)
        old = mo[rb * HEADS + h]
        top = jnp.maximum(jnp.max(sa, axis=1, keepdims=True) * SCALE, old)
        acc = jnp.dot(jnp.exp2(sa * SCALE - top[:, 0:1]).astype(BF), ava[...], preferred_element_type=F32)
        keep = jnp.exp2(old - top)
        acc = acc + acco[rb * HEADS + h] * jnp.concatenate([keep, keep], axis=1)
        obuf[rows, cols] = (acc[:, :HD] / acc[:, HD:]).astype(BF)

    stores = [
        pltpu.make_async_copy(obuf.at[pl.ds(rb * TILE, TILE)], out.at[pl.ds(rb * TILE, TILE)], ls.at[rb])
        for rb in range(NRB)
    ]

    def anchor_steps(rb):
        @pl.loop(0, HEADS // HG)
        def _(i):
            for u in range(HG):
                anchor_step(rb, i * HG + u)

        stores[rb].start()

    anchor_steps(0)
    load_w.wait()
    for k in range(NZ):
        for d in range(1, NY):
            recv(abuf.at[at_c(-d), lax.rem(z_from(d) - k + NZ, NZ)], S_TY + 3 * k + d - 1)

    rows = jnp.concatenate([abuf[(yy + 2 * zz) % NY, zz] for yy in range(NY) for zz in range(NZ)], axis=0)
    upper = jnp.dot(rows, wv[0:4 * HD], preferred_element_type=F32).reshape(NY * NZ, 16, -1)
    lower = jnp.dot(rows, wv[4 * HD:], preferred_element_type=F32).reshape(NY * NZ, 16, -1)
    partial = (upper[:, 0:8] + lower[:, 8:16]).reshape(pown.shape)
    pown[...] = partial
    psend[...] = partial.astype(BF)
    for d in range(1, TP):
        send(psend.at[at_t(d)], prec.at[t], S_RX + d - 1, dev(c, z, at_t(d)))
    anchor_steps(1)
    for d in range(1, TP):
        recv(prec.at[at_t(-d)], S_RX + d - 1)
    answer = pown[t]
    for d in range(1, TP):
        answer = answer + prec[at_t(-d)].astype(F32)
    ansb[t] = answer.astype(BF)
    for d in range(1, TP):
        send(ansb.at[t], ansb.at[t], S_GX + d - 1, dev(c, z, at_t(d)))
    anchor_steps(2)
    for d in range(1, TP):
        recv(ansb.at[at_t(-d)], S_GX + d - 1)
    ans[...] = ansb[...].reshape(ans.shape)

    for copy in sends:
        copy.wait_send()

    @pl.when(root)
    def _():
        for j in range(1, NZ):
            remote(rst.at[j], ast, S_AA + j - 1, S_AA, dev(0, j, t)).wait_send()

    @pl.when(c == 0)
    def _():
        for d in range(1, NY):
            remote(ast.at[d], akv.at[d, z_to(d)], S_AB + d - 1, S_AB, next_to(d)).wait_send()

    for copy in stores:
        copy.wait()


def finish(block, answer, block_out, answer_out, held, held_answer, sem):
    rows = ROWS // COPIES
    pieces = [(block, held, block_out, pl.ds(i * rows, rows)) for i in range(COPIES)]
    pieces.append((answer, held_answer, answer_out, pl.ds(0, answer.shape[0])))
    loads = [
        pltpu.make_async_copy(src.at[at], here.at[at], sem.at[2 * i]) for i, (src, here, _, at) in enumerate(pieces)
    ]
    stores = [
        pltpu.make_async_copy(here.at[at], dst.at[at], sem.at[2 * i + 1])
        for i, (_, here, dst, at) in enumerate(pieces)
    ]
    for copy in loads:
        copy.start()
    for load, store in zip(loads, stores):
        load.wait()
        store.start()
    for copy in stores:
        copy.wait()


def body(cq, ck, cv, blen, qq, qk, qv, qpos, w):
    hbm = pl.BlockSpec(memory_space=pl.ANY)
    vmem = pl.BlockSpec(memory_space=pltpu.VMEM)
    smem = pl.BlockSpec(memory_space=pltpu.SMEM)
    columns = w.shape[1]
    v = pltpu.VMEM
    results = pl.pallas_call(
        kernel,
        out_shape=(
            jax.ShapeDtypeStruct(cq.shape, BF),
            jax.ShapeDtypeStruct((NY * NZ * QROWS, columns), BF),
        ),
        in_specs=[hbm, hbm, hbm, smem, hbm, hbm, hbm, smem, hbm],
        out_specs=(hbm, vmem),
        scratch_shapes=[
            v(qq.shape, BF),
            v(qk.shape, BF),
            v(qv.shape, BF),
            v(cq.shape, BF),
            v(w.shape, BF),
            v((NY, 3, 2, THIRD, HD), BF),
            v((ROWS, HD), BF),
            v((ROWS, 2 * HD), BF),
            v((ROWS, HD), BF),
            v((ROWS, 2 * HD), BF),
            v((TILE, TILE), F32),
            v((NRB * HEADS, TILE, HD), F32),
            v((NRB * HEADS, TILE, 2 * HD), F32),
            v(cq.shape, BF),
            v((NZ, 80, HD), BF),
            v((NY, 48, HD), BF),
            v((NZ, 4, SL + 16, HD), BF),
            v((4, SL + 16, HD), BF),
            v((4, NZ, SL + 16, HD), BF),
            v((2 * ROWS, HD), BF),
            v((2 * ROWS, 2 * HD), BF),
            v((NZ * 64, HD), F32),
            v((NZ * 64, 2 * HD), F32),
            v((NZ, 96, HD), BF),
            v((NZ, 96, HD), BF),
            v((NY, NZ, 16, 4 * HD), BF),
            v((TP, NY * NZ, columns), F32),
            v((TP, NY * NZ, columns), BF),
            v((TP, NY * NZ, columns), BF),
            v((TP, NY * NZ, columns), BF),
            pltpu.SemaphoreType.DMA((N_SEM,)),
            pltpu.SemaphoreType.DMA((N_SEM,)),
            pltpu.SemaphoreType.DMA((12,)),
        ],
        compiler_params=pltpu.CompilerParams(
            collective_id=1, has_side_effects=True, vmem_limit_bytes=63 * 2**20
        ),
        name="star_attention",
    )(cq, ck, cv, blen, qq, qk, qv, qpos, w)
    return pl.pallas_call(
        finish,
        out_shape=tuple(jax.ShapeDtypeStruct(x.shape, x.dtype) for x in results),
        in_specs=[hbm, hbm],
        out_specs=(hbm, hbm),
        scratch_shapes=[v(x.shape, x.dtype) for x in results] + [pltpu.SemaphoreType.DMA((2 * COPIES + 2,))],
        compiler_params=pltpu.CompilerParams(vmem_limit_bytes=62 * 2**20),
        name="results",
    )(*results)


def solution(mesh):
    in_specs = (
        P("ctx", "tp"),
        P("ctx", "tp"),
        P("ctx", "tp"),
        P("ctx"),
        P("ctx", "tp"),
        P("ctx", "tp"),
        P("ctx", "tp"),
        P("ctx"),
        P("tp", "ctx"),
    )
    out_specs = (P("ctx", "tp"), P(None, "ctx"))
    return jax.shard_map(body, mesh=mesh, in_specs=in_specs, out_specs=out_specs, check_vma=False)
```

```python
import functools
import math

import jax
import jax.numpy as jnp
from jax import lax
from jax.experimental import pallas as pl
from jax.experimental.pallas import tpu as pltpu
from jax.sharding import PartitionSpec as P

MESH = pl.DeviceIdType.MESH
NT = (((1,), (1,)), ((), ()))
BF = jnp.bfloat16
F32 = jnp.float32
NEG = -1e30
HD = 128
HEADS = 8
NY, NZ, TP = 4, 8, 8
ROWS = 768
QROWS = 8
TILE = 256
NRB = ROWS // TILE
SL = ROWS * 2 // (NY * NZ)
THIRD = ROWS // 3
SCALE = math.log2(math.e) / math.sqrt(HD)
LOG2E = math.log2(math.e)
ZORDER = (1, 7, 2, 6, 3, 5, 4)
YORDER = (1, 3, 2)
COPIES = 4
HG = 4

S_Q, S_SM, S_KV, S_AA, S_AB, S_AC, S_AD = 0, 7, 10, 22, 29, 32, 39
S_PZ, S_TZ, S_TY, S_RX, S_GX = 42, 49, 56, 80, 87
N_SEM = 94


def kernel(
    cq, ck, cv, blen, qq_hbm, qk_hbm, qv_hbm, qpos, w,
    out, ans,
    qq, qk, qv, cqv, wv, kvb, kk, va, akk, ava, bias,
    mo, acco, obuf,
    qbuf, sml, rst, ast, akv,
    p2kk, p2va, m2, acc2,
    cmsg, crecv, abuf, pown, psend, prec, ansb,
    ss, rs, ls,
):
    ctx = lax.axis_index("ctx")
    t = lax.axis_index("tp")
    z = lax.rem(ctx, NZ)
    c = lax.rem(ctx // NZ + 2 * z, NY)

    def at_z(d):
        return lax.rem(z + d + NZ, NZ)

    def at_c(d):
        return lax.rem(c + d + NY, NY)

    def at_t(d):
        return lax.rem(t + d + TP, TP)

    def dev(cc, zz, tt):
        return (lax.rem(cc + 2 * zz, NY) * NZ + zz, tt)

    def z_to(d):
        return at_z(-1) if d == 2 else z

    def z_from(d):
        return at_z(1) if d == 2 else z

    def next_to(d):
        return dev(at_c(d), z_to(d), t)

    def remote(src, dst, si, ri, device):
        return pltpu.make_async_remote_copy(
            src_ref=src, dst_ref=dst, send_sem=ss.at[si], recv_sem=rs.at[ri],
            device_id=device, device_id_type=MESH,
        )

    def recv(dst, ri):
        remote(dst, dst, ri, ri, next_to(1)).wait_recv()

    sends = []

    def send(src, dst, si, device):
        copy = remote(src, dst, si, si, device)
        copy.start()
        sends.append(copy)

    barrier = pltpu.get_barrier_semaphore()
    peers = (
        [dev(c, at_z(d), t) for d in range(1, NZ)]
        + [dev(at_c(1), z, t), dev(at_c(3), z, t), dev(at_c(2), at_z(1), t), dev(at_c(2), at_z(-1), t)]
        + [dev(c, z, at_t(d)) for d in range(1, TP)]
    )
    for peer in peers:
        pl.semaphore_signal(barrier, inc=1, device_id=peer, device_id_type=MESH)
    small_loads = [
        pltpu.make_async_copy(src, dst, ls.at[n])
        for n, (src, dst) in enumerate(((qq_hbm, qq), (qk_hbm, qk), (qv_hbm, qv)))
    ]
    loads = [
        pltpu.make_async_copy(src, kvb.at[c, n], ls.at[3 + n]) for n, src in enumerate((ck, cv))
    ]
    load_q = pltpu.make_async_copy(cq, cqv, ls.at[5])
    load_w = pltpu.make_async_copy(w, wv, ls.at[6])
    for copy in small_loads + loads + [load_q, load_w]:
        copy.start()
    pl.semaphore_wait(barrier, len(peers))

    first, second = pl.ds(0, 2 * THIRD), pl.ds(2 * THIRD, THIRD)

    def send_keys(part, at):
        for d in YORDER:
            for n, src in enumerate((ck, cv)):
                send(src.at[at], kvb.at[c, n, at], S_KV + 4 * (d - 1) + 2 * part + n, next_to(d))

    send_keys(0, first)
    for copy in small_loads:
        copy.wait()

    row8 = lax.broadcasted_iota(jnp.int32, (8, HD), 0)
    lane8 = lax.broadcasted_iota(jnp.int32, (8, HD), 1)
    qf = qq[...].astype(F32)
    qbuf[z, 0:64, :] = jnp.concatenate([qf[:, h * HD:(h + 1) * HD] for h in range(HEADS)], axis=0).astype(BF)
    pos = jnp.zeros((8, HD), jnp.int32)
    key_pos = jnp.full((8, HD), 512, jnp.int32)
    for r in range(QROWS):
        pos = jnp.where(row8 == r, qpos[r], pos)
        key_pos = jnp.where(lane8 == c * QROWS + r, qpos[r], key_pos)
    pos = pos.astype(F32)
    key_pos = key_pos.astype(F32)
    qbuf[z, 64:80, :] = jnp.concatenate([pos, pos], axis=0).astype(BF)
    length = jnp.zeros((8, HD), jnp.int32) + blen[0]
    info = jnp.concatenate([length // 128, lax.rem(length, 128)], axis=0).astype(F32).astype(BF)
    sml[c, 0:16, :] = jnp.concatenate([qk[...].astype(F32), qv[...].astype(F32)], axis=0).astype(BF)
    sml[c, 16:32, :] = jnp.concatenate([key_pos, key_pos], axis=0).astype(BF)
    sml[c, 32:48, :] = info

    for d in ZORDER:
        send(qbuf.at[z], qbuf.at[z], S_Q + d - 1, dev(c, at_z(d), t))
    for d in YORDER:
        send(sml.at[c], sml.at[c], S_SM + d - 1, next_to(d))
    send_keys(1, second)
    for copy in loads:
        copy.wait()

    root = ctx == 0

    @pl.when(root)
    def _():
        for j in range(NZ):
            for i in range(4):
                n, row = divmod((i * NZ + (j - 1) % NZ if i == 2 else i * NZ + j) * SL, ROWS)
                rst[j, i, 0:SL, :] = kvb[0, n, row:row + SL, :]
                rst[j, i, SL:SL + 16, :] = info
        ast[...] = rst[0]
        for j in range(1, NZ):
            remote(rst.at[j], ast, S_AA + j - 1, S_AA, dev(0, j, t)).start()

    row_of = lax.broadcasted_iota(jnp.int32, (THIRD, HD), 0)

    def live_keys(live, keys, other, values, to_kk, to_va, rows):
        to_kk[rows, :] = jnp.where(live, keys, other)
        to_va[rows, :HD] = jnp.where(live, values, jnp.zeros_like(values))
        to_va[rows, HD:] = jnp.where(live, 1.0, 0.0).astype(BF)

    for a in range(3):
        live_keys(
            row_of + a * THIRD < blen[0], kvb[c, 0, a * THIRD:(a + 1) * THIRD], kvb[c, 0, 0:1],
            kvb[c, 1, a * THIRD:(a + 1) * THIRD], kk, va, slice(a * THIRD, (a + 1) * THIRD),
        )
    rr = lax.broadcasted_iota(jnp.int32, (TILE, TILE), 0)
    cc = lax.broadcasted_iota(jnp.int32, (TILE, TILE), 1)
    bias[...] = jnp.where(cc <= rr, 0.0, NEG)
    load_q.wait()

    def own_step(rb, h):
        qt = cqv[rb * TILE:(rb + 1) * TILE, pl.ds(pl.multiple_of(h * HD, HD), HD)]
        diagonal = slice(rb * TILE, (rb + 1) * TILE)
        sd = lax.dot_general(qt, kk[diagonal], NT, preferred_element_type=F32) + bias[...]
        top = jnp.max(sd, axis=1, keepdims=True)
        if rb:
            so = lax.dot_general(qt, kk[0:rb * TILE], NT, preferred_element_type=F32)
            top = jnp.maximum(top, jnp.max(so, axis=1, keepdims=True))
        top_s = top * SCALE
        pd = jnp.exp2(sd * SCALE - top_s).astype(BF)
        acc = jnp.dot(pd, va[diagonal], preferred_element_type=F32)
        if rb:
            po = jnp.exp2(so * SCALE - top_s).astype(BF)
            acc = acc + jnp.dot(po, va[0:rb * TILE], preferred_element_type=F32)
        acco[rb * HEADS + h] = acc
        mo[rb * HEADS + h] = jnp.broadcast_to(top_s, (TILE, HD))

    def own_steps(rb):
        @pl.loop(0, HEADS // HG)
        def _(i):
            for u in range(HG):
                own_step(rb, i * HG + u)

    own_steps(0)

    own_steps(1)
    own_steps(2)

    for d in range(1, NZ):
        recv(qbuf.at[at_z(-d)], S_Q + d - 1)
    for d in range(1, NY):
        recv(sml.at[at_c(-d)], S_SM + d - 1)
    half = NZ // 2 * 64

    def asked(i):
        return jnp.concatenate([qbuf[i * 4 + j, 0:64, :] for j in range(4)], axis=0)

    small = [sml[j].astype(F32) for j in range(NY)]
    zero96 = jnp.zeros((HD - NY * QROWS, HD), F32)
    ext_k = jnp.concatenate([s[0:8] for s in small] + [zero96], axis=0).astype(BF)
    ext_v = jnp.concatenate([s[8:16] for s in small] + [zero96], axis=0).astype(BF)
    ext_va = jnp.concatenate([ext_v, jnp.ones((HD, HD), BF)], axis=1)
    ext_pos = functools.reduce(jnp.minimum, [s[16:17] for s in small])

    for i in range(2):
        qt = asked(i)
        rows_pos = jnp.concatenate(
            [p for j in range(4) for p in [qbuf[i * 4 + j, 64:80, :].astype(F32)[0:8]] * HEADS], axis=0
        )
        se = lax.dot_general(qt, ext_k, NT, preferred_element_type=F32)
        se = jnp.where(ext_pos <= rows_pos, se, NEG)
        sa = lax.dot_general(qt, kk[...], NT, preferred_element_type=F32)
        top = jnp.maximum(jnp.max(se, axis=1, keepdims=True), jnp.max(sa, axis=1, keepdims=True)) * SCALE
        acc = jnp.dot(jnp.exp2(sa * SCALE - top).astype(BF), va[...], preferred_element_type=F32)
        acc = acc + jnp.dot(jnp.exp2(se * SCALE - top).astype(BF), ext_va, preferred_element_type=F32)
        m2[i * half:(i + 1) * half] = jnp.broadcast_to(top, (half, HD))
        acc2[i * half:(i + 1) * half] = acc

    def phase_two(thirds):
        at = 0
        for d in range(1, NY):
            slot = at_c(-d)
            length = sml[slot, 32:48, :].astype(F32)
            live_to = length[0:1] * 128.0 + length[8:9]
            for a in thirds:
                live_keys(
                    (row_of + a * THIRD).astype(F32) < live_to, kvb[slot, 0, a * THIRD:(a + 1) * THIRD],
                    kvb[slot, 0, 0:1], kvb[slot, 1, a * THIRD:(a + 1) * THIRD], p2kk, p2va, slice(at, at + THIRD),
                )
                at += THIRD
        for i in range(2):
            part = slice(i * half, (i + 1) * half)
            sa = lax.dot_general(asked(i), p2kk[0:at], NT, preferred_element_type=F32)
            old = m2[part]
            top = jnp.maximum(jnp.max(sa, axis=1, keepdims=True) * SCALE, old)
            acc = jnp.dot(jnp.exp2(sa * SCALE - top[:, 0:1]).astype(BF), p2va[0:at], preferred_element_type=F32)
            keep = jnp.exp2(old - top)
            acc2[part] = acc + acc2[part] * jnp.concatenate([keep, keep], axis=1)
            m2[part] = top

    def recv_keys(part, at):
        for d in range(1, NY):
            for n in range(2):
                recv(kvb.at[at_c(-d), n, at], S_KV + 4 * (d - 1) + 2 * part + n)

    recv_keys(0, first)
    phase_two((0, 1))
    recv_keys(1, second)
    phase_two((2,))

    total = acc2[:, HD:]
    lse = m2[...] + jnp.log(total) * LOG2E
    part_out = acc2[:, :HD] / total
    for j in range(NZ):
        compact = jnp.zeros((8, HD), F32)
        for h in range(HEADS):
            compact = jnp.where(lane8 == h, lse[j * 64 + h * 8:j * 64 + h * 8 + 8], compact)
        high = compact.astype(BF).astype(F32)
        middle = (compact - high).astype(BF).astype(F32)
        low = compact - high - middle
        cmsg[j, 0:64, :] = part_out[j * 64:(j + 1) * 64].astype(BF)
        cmsg[j, 64:96, :] = jnp.concatenate([high, middle, low, jnp.zeros((8, HD), F32)], axis=0).astype(BF)
    for d in ZORDER:
        send(cmsg.at[at_z(d)], crecv.at[z], S_PZ + d - 1, dev(c, at_z(d), t))

    @pl.when(c == 0)
    def _():
        @pl.when(z != 0)
        def _():
            recv(ast, S_AA)
        akv[0, z] = ast[0]
        for d in range(1, NY):
            remote(ast.at[d], akv.at[d, z_to(d)], S_AB + d - 1, S_AB, next_to(d)).start()

    @pl.when(c != 0)
    def _():
        recv(akv.at[c, z], S_AB)

    for d in ZORDER:
        send(akv.at[c, z], akv.at[c, z], S_AC + d - 1, dev(c, at_z(d), t))


    for d in range(1, NZ):
        recv(crecv.at[at_z(-d)], S_PZ + d - 1)
    parts = [cmsg[z].astype(F32)] + [crecv[at_z(-d)].astype(F32) for d in range(1, NZ)]
    lses = [p[64:72] + p[72:80] + p[80:88] for p in parts]
    top = functools.reduce(jnp.maximum, lses)
    weights = [jnp.exp2(x - top) for x in lses]
    weight_sum = functools.reduce(jnp.add, weights)
    weights = [x / weight_sum for x in weights]
    merged = []
    for h in range(HEADS):
        merged.append(functools.reduce(
            jnp.add, [x[:, h:h + 1] * p[h * 8:h * 8 + 8] for x, p in zip(weights, parts)]
        ))
    merged = jnp.concatenate(
        [jnp.concatenate(merged[0:4], axis=1), jnp.concatenate(merged[4:8], axis=1)], axis=0
    )
    abuf[c, z] = merged.astype(BF)

    for d in ZORDER:
        send(abuf.at[c, z], abuf.at[c, z], S_TZ + d - 1, dev(c, at_z(d), t))

    def pass_on(k):
        zz = at_z(-k)
        if k:
            recv(abuf.at[c, zz], S_TZ + k - 1)
        for d in YORDER:
            send(abuf.at[c, zz], abuf.at[c, zz], S_TY + 3 * k + d - 1, next_to(d))

    pass_on(0)
    for d in range(1, NZ):
        recv(akv.at[c, at_z(-d)], S_AC + d - 1)
    data = pl.ds(0, SL)
    for d in YORDER:
        send(akv.at[c, :, data], akv.at[c, :, data], S_AD + d - 1, next_to(d))

    for k in ZORDER:
        pass_on(k)

    def anchor_step(rb, h):
        cols = pl.ds(pl.multiple_of(h * HD, HD), HD)
        rows = slice(rb * TILE, (rb + 1) * TILE)
        sa = lax.dot_general(cqv[rows, cols], akk[...], NT, preferred_element_type=F32)
        old = mo[rb * HEADS + h]
        top = jnp.maximum(jnp.max(sa, axis=1, keepdims=True) * SCALE, old)
        acc = jnp.dot(jnp.exp2(sa * SCALE - top[:, 0:1]).astype(BF), ava[...], preferred_element_type=F32)
        keep = jnp.exp2(old - top)
        acc = acc + acco[rb * HEADS + h] * jnp.concatenate([keep, keep], axis=1)
        obuf[rows, cols] = (acc[:, :HD] / acc[:, HD:]).astype(BF)

    stores = [
        pltpu.make_async_copy(obuf.at[pl.ds(rb * TILE, TILE)], out.at[pl.ds(rb * TILE, TILE)], ls.at[rb])
        for rb in range(NRB)
    ]

    def anchor_steps(rb):
        @pl.loop(0, HEADS // HG)
        def _(i):
            for u in range(HG):
                anchor_step(rb, i * HG + u)

        stores[rb].start()

    load_w.wait()
    for k in range(NZ):
        for d in range(1, NY):
            recv(abuf.at[at_c(-d), lax.rem(z_from(d) - k + NZ, NZ)], S_TY + 3 * k + d - 1)

    rows = jnp.concatenate([abuf[(yy + 2 * zz) % NY, zz] for yy in range(NY) for zz in range(NZ)], axis=0)
    upper = jnp.dot(rows, wv[0:4 * HD], preferred_element_type=F32).reshape(NY * NZ, 16, -1)
    lower = jnp.dot(rows, wv[4 * HD:], preferred_element_type=F32).reshape(NY * NZ, 16, -1)
    partial = (upper[:, 0:8] + lower[:, 8:16]).reshape(pown.shape)
    pown[...] = partial
    psend[...] = partial.astype(BF)
    for d in range(1, TP):
        send(psend.at[at_t(d)], prec.at[t], S_RX + d - 1, dev(c, z, at_t(d)))
    for d in range(1, NY):
        recv(akv.at[at_c(-d), :, data], S_AD + d - 1)
    alen = akv[c, z, SL:SL + 16, :].astype(F32)
    alive_to = jnp.where(ctx == 0, 0.0, alen[0:1] * 128.0 + alen[8:9])
    anchor = akv[:, :, 0:SL, :].reshape(2 * ROWS, HD)
    for a in range(3):
        keys_at = a * THIRD
        live_keys(
            (row_of + a * THIRD).astype(F32) < alive_to, anchor[keys_at:keys_at + THIRD], anchor[0:1],
            anchor[ROWS + keys_at:ROWS + keys_at + THIRD], akk, ava, slice(a * THIRD, (a + 1) * THIRD),
        )

    anchor_steps(0)
    anchor_steps(1)
    for d in range(1, TP):
        recv(prec.at[at_t(-d)], S_RX + d - 1)
    answer = pown[t]
    for d in range(1, TP):
        answer = answer + prec[at_t(-d)].astype(F32)
    ansb[t] = answer.astype(BF)
    for d in range(1, TP):
        send(ansb.at[t], ansb.at[t], S_GX + d - 1, dev(c, z, at_t(d)))
    anchor_steps(2)
    for d in range(1, TP):
        recv(ansb.at[at_t(-d)], S_GX + d - 1)
    ans[...] = ansb[...].reshape(ans.shape)

    for copy in sends:
        copy.wait_send()

    @pl.when(root)
    def _():
        for j in range(1, NZ):
            remote(rst.at[j], ast, S_AA + j - 1, S_AA, dev(0, j, t)).wait_send()

    @pl.when(c == 0)
    def _():
        for d in range(1, NY):
            remote(ast.at[d], akv.at[d, z_to(d)], S_AB + d - 1, S_AB, next_to(d)).wait_send()

    for copy in stores:
        copy.wait()


def finish(block, answer, block_out, answer_out, held, held_answer, sem):
    rows = ROWS // COPIES
    pieces = [(block, held, block_out, pl.ds(i * rows, rows)) for i in range(COPIES)]
    pieces.append((answer, held_answer, answer_out, pl.ds(0, answer.shape[0])))
    loads = [
        pltpu.make_async_copy(src.at[at], here.at[at], sem.at[2 * i]) for i, (src, here, _, at) in enumerate(pieces)
    ]
    stores = [
        pltpu.make_async_copy(here.at[at], dst.at[at], sem.at[2 * i + 1])
        for i, (_, here, dst, at) in enumerate(pieces)
    ]
    for copy in loads:
        copy.start()
    for load, store in zip(loads, stores):
        load.wait()
        store.start()
    for copy in stores:
        copy.wait()


def body(cq, ck, cv, blen, qq, qk, qv, qpos, w):
    hbm = pl.BlockSpec(memory_space=pl.ANY)
    vmem = pl.BlockSpec(memory_space=pltpu.VMEM)
    smem = pl.BlockSpec(memory_space=pltpu.SMEM)
    columns = w.shape[1]
    v = pltpu.VMEM
    results = pl.pallas_call(
        kernel,
        out_shape=(
            jax.ShapeDtypeStruct(cq.shape, BF),
            jax.ShapeDtypeStruct((NY * NZ * QROWS, columns), BF),
        ),
        in_specs=[hbm, hbm, hbm, smem, hbm, hbm, hbm, smem, hbm],
        out_specs=(hbm, vmem),
        scratch_shapes=[
            v(qq.shape, BF),
            v(qk.shape, BF),
            v(qv.shape, BF),
            v(cq.shape, BF),
            v(w.shape, BF),
            v((NY, 2, ROWS, HD), BF),
            v((ROWS, HD), BF),
            v((ROWS, 2 * HD), BF),
            v((ROWS, HD), BF),
            v((ROWS, 2 * HD), BF),
            v((TILE, TILE), F32),
            v((NRB * HEADS, TILE, HD), F32),
            v((NRB * HEADS, TILE, 2 * HD), F32),
            v(cq.shape, BF),
            v((NZ, 80, HD), BF),
            v((NY, 48, HD), BF),
            v((NZ, 4, SL + 16, HD), BF),
            v((4, SL + 16, HD), BF),
            v((4, NZ, SL + 16, HD), BF),
            v((2 * ROWS, HD), BF),
            v((2 * ROWS, 2 * HD), BF),
            v((NZ * 64, HD), F32),
            v((NZ * 64, 2 * HD), F32),
            v((NZ, 96, HD), BF),
            v((NZ, 96, HD), BF),
            v((NY, NZ, 16, 4 * HD), BF),
            v((TP, NY * NZ, columns), F32),
            v((TP, NY * NZ, columns), BF),
            v((TP, NY * NZ, columns), BF),
            v((TP, NY * NZ, columns), BF),
            pltpu.SemaphoreType.DMA((N_SEM,)),
            pltpu.SemaphoreType.DMA((N_SEM,)),
            pltpu.SemaphoreType.DMA((12,)),
        ],
        compiler_params=pltpu.CompilerParams(
            collective_id=1, has_side_effects=True, vmem_limit_bytes=63 * 2**20
        ),
        name="star_attention",
    )(cq, ck, cv, blen, qq, qk, qv, qpos, w)
    return pl.pallas_call(
        finish,
        out_shape=tuple(jax.ShapeDtypeStruct(x.shape, x.dtype) for x in results),
        in_specs=[hbm, hbm],
        out_specs=(hbm, hbm),
        scratch_shapes=[v(x.shape, x.dtype) for x in results] + [pltpu.SemaphoreType.DMA((2 * COPIES + 2,))],
        compiler_params=pltpu.CompilerParams(vmem_limit_bytes=62 * 2**20),
        name="results",
    )(*results)


def solution(mesh):
    in_specs = (
        P("ctx", "tp"),
        P("ctx", "tp"),
        P("ctx", "tp"),
        P("ctx"),
        P("ctx", "tp"),
        P("ctx", "tp"),
        P("ctx", "tp"),
        P("ctx"),
        P("tp", "ctx"),
    )
    out_specs = (P("ctx", "tp"), P(None, "ctx"))
    return jax.shard_map(body, mesh=mesh, in_specs=in_specs, out_specs=out_specs, check_vma=False)
```

```python
import functools
import math

import jax
import jax.numpy as jnp
from jax import lax
from jax.experimental import pallas as pl
from jax.experimental.pallas import tpu as pltpu
from jax.sharding import PartitionSpec as P

MESH = pl.DeviceIdType.MESH
NT = (((1,), (1,)), ((), ()))
BF = jnp.bfloat16
F32 = jnp.float32
NEG = -1e30
HD = 128
HEADS = 8
NY, NZ, TP = 4, 8, 8
ROWS = 768
QROWS = 8
TILE = 256
NRB = ROWS // TILE
SL = ROWS * 2 // (NY * NZ)
THIRD = ROWS // 3
SCALE = math.log2(math.e) / math.sqrt(HD)
LOG2E = math.log2(math.e)
ZORDER = (1, 7, 2, 6, 3, 5, 4)
YORDER = (1, 3, 2)
COPIES = 4
HG = 4

S_Q, S_SM, S_KV, S_AA, S_AC, S_AD = 0, 7, 10, 22, 29, 36
S_PZ, S_TZ, S_TY, S_RX, S_GX = 39, 46, 53, 77, 84
N_SEM = 91


def kernel(
    cq, ck, cv, blen, qq_hbm, qk_hbm, qv_hbm, qpos, w,
    out, ans,
    qq, qk, qv, cqv, wv, kvb, kk, va, akk, ava, bias,
    mo, acco, obuf,
    qbuf, sml, rst, akv,
    p2kk, p2va, m2, acc2,
    cmsg, crecv, abuf, pown, psend, prec, ansb,
    ss, rs, ls,
):
    ctx = lax.axis_index("ctx")
    t = lax.axis_index("tp")
    z = lax.rem(ctx, NZ)
    c = lax.rem(ctx // NZ + 2 * z, NY)

    def at_z(d):
        return lax.rem(z + d + NZ, NZ)

    def at_c(d):
        return lax.rem(c + d + NY, NY)

    def at_t(d):
        return lax.rem(t + d + TP, TP)

    def dev(cc, zz, tt):
        return (lax.rem(cc + 2 * zz, NY) * NZ + zz, tt)

    def z_to(d):
        return at_z(-1) if d == 2 else z

    def z_from(d):
        return at_z(1) if d == 2 else z

    def next_to(d):
        return dev(at_c(d), z_to(d), t)

    def remote(src, dst, si, ri, device):
        return pltpu.make_async_remote_copy(
            src_ref=src, dst_ref=dst, send_sem=ss.at[si], recv_sem=rs.at[ri],
            device_id=device, device_id_type=MESH,
        )

    def recv(dst, ri):
        remote(dst, dst, ri, ri, next_to(1)).wait_recv()

    sends = []

    def send(src, dst, si, device):
        copy = remote(src, dst, si, si, device)
        copy.start()
        sends.append(copy)

    barrier = pltpu.get_barrier_semaphore()
    peers = (
        [dev(c, at_z(d), t) for d in range(1, NZ)]
        + [dev(at_c(1), z, t), dev(at_c(3), z, t), dev(at_c(2), at_z(1), t), dev(at_c(2), at_z(-1), t)]
        + [dev(c, z, at_t(d)) for d in range(1, TP)]
    )
    for peer in peers:
        pl.semaphore_signal(barrier, inc=1, device_id=peer, device_id_type=MESH)
    small_loads = [
        pltpu.make_async_copy(src, dst, ls.at[n])
        for n, (src, dst) in enumerate(((qq_hbm, qq), (qk_hbm, qk), (qv_hbm, qv)))
    ]
    loads = [
        pltpu.make_async_copy(src, kvb.at[c, n], ls.at[3 + n]) for n, src in enumerate((ck, cv))
    ]
    load_q = pltpu.make_async_copy(cq, cqv, ls.at[5])
    load_w = pltpu.make_async_copy(w, wv, ls.at[6])
    for copy in small_loads + loads + [load_q, load_w]:
        copy.start()
    pl.semaphore_wait(barrier, len(peers))

    first, second = pl.ds(0, 2 * THIRD), pl.ds(2 * THIRD, THIRD)

    def send_keys(part, at):
        for d in YORDER:
            for n, src in enumerate((ck, cv)):
                send(src.at[at], kvb.at[c, n, at], S_KV + 4 * (d - 1) + 2 * part + n, next_to(d))

    send_keys(0, first)
    for copy in small_loads:
        copy.wait()

    row8 = lax.broadcasted_iota(jnp.int32, (8, HD), 0)
    lane8 = lax.broadcasted_iota(jnp.int32, (8, HD), 1)
    qf = qq[...].astype(F32)
    qbuf[z, 0:64, :] = jnp.concatenate([qf[:, h * HD:(h + 1) * HD] for h in range(HEADS)], axis=0).astype(BF)
    pos = jnp.zeros((8, HD), jnp.int32)
    key_pos = jnp.full((8, HD), 512, jnp.int32)
    for r in range(QROWS):
        pos = jnp.where(row8 == r, qpos[r], pos)
        key_pos = jnp.where(lane8 == c * QROWS + r, qpos[r], key_pos)
    pos = pos.astype(F32)
    key_pos = key_pos.astype(F32)
    qbuf[z, 64:80, :] = jnp.concatenate([pos, pos], axis=0).astype(BF)
    length = jnp.zeros((8, HD), jnp.int32) + blen[0]
    info = jnp.concatenate([length // 128, lax.rem(length, 128)], axis=0).astype(F32).astype(BF)
    sml[c, 0:16, :] = jnp.concatenate([qk[...].astype(F32), qv[...].astype(F32)], axis=0).astype(BF)
    sml[c, 16:32, :] = jnp.concatenate([key_pos, key_pos], axis=0).astype(BF)
    sml[c, 32:48, :] = info

    for d in ZORDER:
        send(qbuf.at[z], qbuf.at[z], S_Q + d - 1, dev(c, at_z(d), t))
    for d in YORDER:
        send(sml.at[c], sml.at[c], S_SM + d - 1, next_to(d))
    send_keys(1, second)
    for copy in loads:
        copy.wait()

    row_of = lax.broadcasted_iota(jnp.int32, (THIRD, HD), 0)

    def live_keys(live, keys, other, values, to_kk, to_va, rows):
        to_kk[rows, :] = jnp.where(live, keys, other)
        to_va[rows, :HD] = jnp.where(live, values, jnp.zeros_like(values))
        to_va[rows, HD:] = jnp.where(live, 1.0, 0.0).astype(BF)

    for a in range(3):
        live_keys(
            row_of + a * THIRD < blen[0], kvb[c, 0, a * THIRD:(a + 1) * THIRD], kvb[c, 0, 0:1],
            kvb[c, 1, a * THIRD:(a + 1) * THIRD], kk, va, slice(a * THIRD, (a + 1) * THIRD),
        )
    rr = lax.broadcasted_iota(jnp.int32, (TILE, TILE), 0)
    cc = lax.broadcasted_iota(jnp.int32, (TILE, TILE), 1)
    bias[...] = jnp.where(cc <= rr, 0.0, NEG)
    load_q.wait()

    def own_step(rb, h):
        qt = cqv[rb * TILE:(rb + 1) * TILE, pl.ds(pl.multiple_of(h * HD, HD), HD)]
        diagonal = slice(rb * TILE, (rb + 1) * TILE)
        sd = lax.dot_general(qt, kk[diagonal], NT, preferred_element_type=F32) + bias[...]
        top = jnp.max(sd, axis=1, keepdims=True)
        if rb:
            so = lax.dot_general(qt, kk[0:rb * TILE], NT, preferred_element_type=F32)
            top = jnp.maximum(top, jnp.max(so, axis=1, keepdims=True))
        top_s = top * SCALE
        pd = jnp.exp2(sd * SCALE - top_s).astype(BF)
        acc = jnp.dot(pd, va[diagonal], preferred_element_type=F32)
        if rb:
            po = jnp.exp2(so * SCALE - top_s).astype(BF)
            acc = acc + jnp.dot(po, va[0:rb * TILE], preferred_element_type=F32)
        acco[rb * HEADS + h] = acc
        mo[rb * HEADS + h] = jnp.broadcast_to(top_s, (TILE, HD))

    def own_steps(rb):
        @pl.loop(0, HEADS // HG)
        def _(i):
            for u in range(HG):
                own_step(rb, i * HG + u)

    own_steps(0)

    own_steps(1)
    own_steps(2)

    for d in range(1, NZ):
        recv(qbuf.at[at_z(-d)], S_Q + d - 1)
    for d in range(1, NY):
        recv(sml.at[at_c(-d)], S_SM + d - 1)
    half = NZ // 2 * 64

    def asked(i):
        return jnp.concatenate([qbuf[i * 4 + j, 0:64, :] for j in range(4)], axis=0)

    small = [sml[j].astype(F32) for j in range(NY)]
    zero96 = jnp.zeros((HD - NY * QROWS, HD), F32)
    ext_k = jnp.concatenate([s[0:8] for s in small] + [zero96], axis=0).astype(BF)
    ext_v = jnp.concatenate([s[8:16] for s in small] + [zero96], axis=0).astype(BF)
    ext_va = jnp.concatenate([ext_v, jnp.ones((HD, HD), BF)], axis=1)
    ext_pos = functools.reduce(jnp.minimum, [s[16:17] for s in small])

    for i in range(2):
        qt = asked(i)
        rows_pos = jnp.concatenate(
            [p for j in range(4) for p in [qbuf[i * 4 + j, 64:80, :].astype(F32)[0:8]] * HEADS], axis=0
        )
        se = lax.dot_general(qt, ext_k, NT, preferred_element_type=F32)
        se = jnp.where(ext_pos <= rows_pos, se, NEG)
        sa = lax.dot_general(qt, kk[...], NT, preferred_element_type=F32)
        top = jnp.maximum(jnp.max(se, axis=1, keepdims=True), jnp.max(sa, axis=1, keepdims=True)) * SCALE
        acc = jnp.dot(jnp.exp2(sa * SCALE - top).astype(BF), va[...], preferred_element_type=F32)
        acc = acc + jnp.dot(jnp.exp2(se * SCALE - top).astype(BF), ext_va, preferred_element_type=F32)
        m2[i * half:(i + 1) * half] = jnp.broadcast_to(top, (half, HD))
        acc2[i * half:(i + 1) * half] = acc

    def phase_two(thirds):
        at = 0
        for d in range(1, NY):
            slot = at_c(-d)
            length = sml[slot, 32:48, :].astype(F32)
            live_to = length[0:1] * 128.0 + length[8:9]
            for a in thirds:
                live_keys(
                    (row_of + a * THIRD).astype(F32) < live_to, kvb[slot, 0, a * THIRD:(a + 1) * THIRD],
                    kvb[slot, 0, 0:1], kvb[slot, 1, a * THIRD:(a + 1) * THIRD], p2kk, p2va, slice(at, at + THIRD),
                )
                at += THIRD
        for i in range(2):
            part = slice(i * half, (i + 1) * half)
            sa = lax.dot_general(asked(i), p2kk[0:at], NT, preferred_element_type=F32)
            old = m2[part]
            top = jnp.maximum(jnp.max(sa, axis=1, keepdims=True) * SCALE, old)
            acc = jnp.dot(jnp.exp2(sa * SCALE - top[:, 0:1]).astype(BF), p2va[0:at], preferred_element_type=F32)
            keep = jnp.exp2(old - top)
            acc2[part] = acc + acc2[part] * jnp.concatenate([keep, keep], axis=1)
            m2[part] = top

    def recv_keys(part, at):
        for d in range(1, NY):
            for n in range(2):
                recv(kvb.at[at_c(-d), n, at], S_KV + 4 * (d - 1) + 2 * part + n)

    recv_keys(0, first)
    phase_two((0, 1))
    recv_keys(1, second)

    source_z = jnp.where(c == 2, NZ - 1, 0)

    @pl.when(z == source_z)
    def _():
        for j in range(NZ):
            row = pl.multiple_of(lax.rem(c, 2) * (ROWS // 2) + j * SL, 16)
            rst[j, 0:SL, :] = kvb[0, c // 2, pl.ds(row, SL), :]
            rst[j, SL:SL + 16, :] = sml[0, 32:48, :]
        akv[c, z] = rst[z]
        for d in range(1, NZ):
            to_z = at_z(d)
            remote(rst.at[to_z], akv.at[c, to_z], S_AA + d - 1, S_AA, dev(c, to_z, t)).start()

    phase_two((2,))

    total = acc2[:, HD:]
    lse = m2[...] + jnp.log(total) * LOG2E
    part_out = acc2[:, :HD] / total
    for j in range(NZ):
        compact = jnp.zeros((8, HD), F32)
        for h in range(HEADS):
            compact = jnp.where(lane8 == h, lse[j * 64 + h * 8:j * 64 + h * 8 + 8], compact)
        high = compact.astype(BF).astype(F32)
        middle = (compact - high).astype(BF).astype(F32)
        low = compact - high - middle
        cmsg[j, 0:64, :] = part_out[j * 64:(j + 1) * 64].astype(BF)
        cmsg[j, 64:96, :] = jnp.concatenate([high, middle, low, jnp.zeros((8, HD), F32)], axis=0).astype(BF)
    for d in ZORDER:
        send(cmsg.at[at_z(d)], crecv.at[z], S_PZ + d - 1, dev(c, at_z(d), t))

    @pl.when(z != source_z)
    def _():
        recv(akv.at[c, z], S_AA)

    for d in ZORDER:
        send(akv.at[c, z], akv.at[c, z], S_AC + d - 1, dev(c, at_z(d), t))


    for d in range(1, NZ):
        recv(crecv.at[at_z(-d)], S_PZ + d - 1)
    parts = [cmsg[z].astype(F32)] + [crecv[at_z(-d)].astype(F32) for d in range(1, NZ)]
    lses = [p[64:72] + p[72:80] + p[80:88] for p in parts]
    top = functools.reduce(jnp.maximum, lses)
    weights = [jnp.exp2(x - top) for x in lses]
    weight_sum = functools.reduce(jnp.add, weights)
    weights = [x / weight_sum for x in weights]
    merged = []
    for h in range(HEADS):
        merged.append(functools.reduce(
            jnp.add, [x[:, h:h + 1] * p[h * 8:h * 8 + 8] for x, p in zip(weights, parts)]
        ))
    merged = jnp.concatenate(
        [jnp.concatenate(merged[0:4], axis=1), jnp.concatenate(merged[4:8], axis=1)], axis=0
    )
    abuf[c, z] = merged.astype(BF)

    for d in ZORDER:
        send(abuf.at[c, z], abuf.at[c, z], S_TZ + d - 1, dev(c, at_z(d), t))

    def pass_on(k):
        zz = at_z(-k)
        if k:
            recv(abuf.at[c, zz], S_TZ + k - 1)
        for d in YORDER:
            send(abuf.at[c, zz], abuf.at[c, zz], S_TY + 3 * k + d - 1, next_to(d))

    pass_on(0)
    for d in range(1, NZ):
        recv(akv.at[c, at_z(-d)], S_AC + d - 1)
    data = pl.ds(0, SL)
    for d in YORDER:
        send(akv.at[c, :, data], akv.at[c, :, data], S_AD + d - 1, next_to(d))

    for k in ZORDER:
        pass_on(k)

    def anchor_step(rb, h):
        cols = pl.ds(pl.multiple_of(h * HD, HD), HD)
        rows = slice(rb * TILE, (rb + 1) * TILE)
        sa = lax.dot_general(cqv[rows, cols], akk[...], NT, preferred_element_type=F32)
        old = mo[rb * HEADS + h]
        top = jnp.maximum(jnp.max(sa, axis=1, keepdims=True) * SCALE, old)
        acc = jnp.dot(jnp.exp2(sa * SCALE - top[:, 0:1]).astype(BF), ava[...], preferred_element_type=F32)
        keep = jnp.exp2(old - top)
        acc = acc + acco[rb * HEADS + h] * jnp.concatenate([keep, keep], axis=1)
        obuf[rows, cols] = (acc[:, :HD] / acc[:, HD:]).astype(BF)

    stores = [
        pltpu.make_async_copy(obuf.at[pl.ds(rb * TILE, TILE)], out.at[pl.ds(rb * TILE, TILE)], ls.at[rb])
        for rb in range(NRB)
    ]

    def anchor_steps(rb):
        @pl.loop(0, HEADS // HG)
        def _(i):
            for u in range(HG):
                anchor_step(rb, i * HG + u)

        stores[rb].start()

    for d in range(1, NY):
        recv(akv.at[at_c(-d), :, data], S_AD + d - 1)
    alen = akv[c, z, SL:SL + 16, :].astype(F32)
    alive_to = jnp.where(ctx == 0, 0.0, alen[0:1] * 128.0 + alen[8:9])
    anchor = akv[:, :, 0:SL, :].reshape(2 * ROWS, HD)
    for a in range(3):
        keys_at = a * THIRD
        live_keys(
            (row_of + a * THIRD).astype(F32) < alive_to, anchor[keys_at:keys_at + THIRD], anchor[0:1],
            anchor[ROWS + keys_at:ROWS + keys_at + THIRD], akk, ava, slice(a * THIRD, (a + 1) * THIRD),
        )

    anchor_steps(0)
    load_w.wait()
    for k in range(NZ):
        for d in range(1, NY):
            recv(abuf.at[at_c(-d), lax.rem(z_from(d) - k + NZ, NZ)], S_TY + 3 * k + d - 1)

    rows = jnp.concatenate([abuf[(yy + 2 * zz) % NY, zz] for yy in range(NY) for zz in range(NZ)], axis=0)
    upper = jnp.dot(rows, wv[0:4 * HD], preferred_element_type=F32).reshape(NY * NZ, 16, -1)
    lower = jnp.dot(rows, wv[4 * HD:], preferred_element_type=F32).reshape(NY * NZ, 16, -1)
    partial = (upper[:, 0:8] + lower[:, 8:16]).reshape(pown.shape)
    pown[...] = partial
    psend[...] = partial.astype(BF)
    for d in range(1, TP):
        send(psend.at[at_t(d)], prec.at[t], S_RX + d - 1, dev(c, z, at_t(d)))
    anchor_steps(1)
    for d in range(1, TP):
        recv(prec.at[at_t(-d)], S_RX + d - 1)
    answer = pown[t]
    for d in range(1, TP):
        answer = answer + prec[at_t(-d)].astype(F32)
    ansb[t] = answer.astype(BF)
    for d in range(1, TP):
        send(ansb.at[t], ansb.at[t], S_GX + d - 1, dev(c, z, at_t(d)))
    anchor_steps(2)
    for d in range(1, TP):
        recv(ansb.at[at_t(-d)], S_GX + d - 1)
    ans[...] = ansb[...].reshape(ans.shape)

    for copy in sends:
        copy.wait_send()

    @pl.when(z == source_z)
    def _():
        for d in range(1, NZ):
            to_z = at_z(d)
            remote(rst.at[to_z], akv.at[c, to_z], S_AA + d - 1, S_AA, dev(c, to_z, t)).wait_send()

    for copy in stores:
        copy.wait()


def finish(block, answer, block_out, answer_out, held, held_answer, sem):
    rows = ROWS // COPIES
    pieces = [(block, held, block_out, pl.ds(i * rows, rows)) for i in range(COPIES)]
    pieces.append((answer, held_answer, answer_out, pl.ds(0, answer.shape[0])))
    loads = [
        pltpu.make_async_copy(src.at[at], here.at[at], sem.at[2 * i]) for i, (src, here, _, at) in enumerate(pieces)
    ]
    stores = [
        pltpu.make_async_copy(here.at[at], dst.at[at], sem.at[2 * i + 1])
        for i, (_, here, dst, at) in enumerate(pieces)
    ]
    for copy in loads:
        copy.start()
    for load, store in zip(loads, stores):
        load.wait()
        store.start()
    for copy in stores:
        copy.wait()


def body(cq, ck, cv, blen, qq, qk, qv, qpos, w):
    hbm = pl.BlockSpec(memory_space=pl.ANY)
    vmem = pl.BlockSpec(memory_space=pltpu.VMEM)
    smem = pl.BlockSpec(memory_space=pltpu.SMEM)
    columns = w.shape[1]
    v = pltpu.VMEM
    results = pl.pallas_call(
        kernel,
        out_shape=(
            jax.ShapeDtypeStruct(cq.shape, BF),
            jax.ShapeDtypeStruct((NY * NZ * QROWS, columns), BF),
        ),
        in_specs=[hbm, hbm, hbm, smem, hbm, hbm, hbm, smem, hbm],
        out_specs=(hbm, vmem),
        scratch_shapes=[
            v(qq.shape, BF),
            v(qk.shape, BF),
            v(qv.shape, BF),
            v(cq.shape, BF),
            v(w.shape, BF),
            v((NY, 2, ROWS, HD), BF),
            v((ROWS, HD), BF),
            v((ROWS, 2 * HD), BF),
            v((ROWS, HD), BF),
            v((ROWS, 2 * HD), BF),
            v((TILE, TILE), F32),
            v((NRB * HEADS, TILE, HD), F32),
            v((NRB * HEADS, TILE, 2 * HD), F32),
            v(cq.shape, BF),
            v((NZ, 80, HD), BF),
            v((NY, 48, HD), BF),
            v((NZ, SL + 16, HD), BF),
            v((4, NZ, SL + 16, HD), BF),
            v((2 * ROWS, HD), BF),
            v((2 * ROWS, 2 * HD), BF),
            v((NZ * 64, HD), F32),
            v((NZ * 64, 2 * HD), F32),
            v((NZ, 96, HD), BF),
            v((NZ, 96, HD), BF),
            v((NY, NZ, 16, 4 * HD), BF),
            v((TP, NY * NZ, columns), F32),
            v((TP, NY * NZ, columns), BF),
            v((TP, NY * NZ, columns), BF),
            v((TP, NY * NZ, columns), BF),
            pltpu.SemaphoreType.DMA((N_SEM,)),
            pltpu.SemaphoreType.DMA((N_SEM,)),
            pltpu.SemaphoreType.DMA((12,)),
        ],
        compiler_params=pltpu.CompilerParams(
            collective_id=1, has_side_effects=True, vmem_limit_bytes=63 * 2**20
        ),
        name="star_attention",
    )(cq, ck, cv, blen, qq, qk, qv, qpos, w)
    return pl.pallas_call(
        finish,
        out_shape=tuple(jax.ShapeDtypeStruct(x.shape, x.dtype) for x in results),
        in_specs=[hbm, hbm],
        out_specs=(hbm, hbm),
        scratch_shapes=[v(x.shape, x.dtype) for x in results] + [pltpu.SemaphoreType.DMA((2 * COPIES + 2,))],
        compiler_params=pltpu.CompilerParams(vmem_limit_bytes=62 * 2**20),
        name="results",
    )(*results)


def solution(mesh):
    in_specs = (
        P("ctx", "tp"),
        P("ctx", "tp"),
        P("ctx", "tp"),
        P("ctx"),
        P("ctx", "tp"),
        P("ctx", "tp"),
        P("ctx", "tp"),
        P("ctx"),
        P("tp", "ctx"),
    )
    out_specs = (P("ctx", "tp"), P(None, "ctx"))
    return jax.shard_map(body, mesh=mesh, in_specs=in_specs, out_specs=out_specs, check_vma=False)
```

```python
import functools
import math

import jax
import jax.numpy as jnp
from jax import lax
from jax.experimental import pallas as pl
from jax.experimental.pallas import tpu as pltpu
from jax.sharding import PartitionSpec as P

MESH = pl.DeviceIdType.MESH
NT = (((1,), (1,)), ((), ()))
BF = jnp.bfloat16
F32 = jnp.float32
NEG = -1e30
HD = 128
HEADS = 8
NY, NZ, TP = 4, 8, 8
ROWS = 768
QROWS = 8
TILE = 256
NRB = ROWS // TILE
SL = ROWS * 2 // (NY * NZ)
THIRD = ROWS // 3
SCALE = math.log2(math.e) / math.sqrt(HD)
LOG2E = math.log2(math.e)
ZORDER = (1, 7, 2, 6, 3, 5, 4)
YORDER = (1, 3, 2)
COPIES = 4
HG = 4

S_Q, S_SM, S_KV, S_AA, S_AC, S_AD = 0, 7, 11, 27, 34, 41
S_PZ, S_TZ, S_TY, S_RX, S_GX = 44, 51, 58, 82, 89
N_SEM = 96


def kernel(
    cq, ck, cv, blen, qq_hbm, qk_hbm, qv_hbm, qpos, w,
    out, ans,
    qq, qk, qv, cqv, wv, kvb, kk, va, akk, ava, bias,
    mo, acco, obuf,
    qbuf, sml, rst, akv,
    p2kk, p2va, m2, acc2,
    cmsg, crecv, abuf, pown, psend, prec, ansb,
    ss, rs, ls,
):
    ctx = lax.axis_index("ctx")
    t = lax.axis_index("tp")
    z = lax.rem(ctx, NZ)
    c = lax.rem(ctx // NZ + 2 * z, NY)

    def at_z(d):
        return lax.rem(z + d + NZ, NZ)

    def at_c(d):
        return lax.rem(c + d + NY, NY)

    def at_t(d):
        return lax.rem(t + d + TP, TP)

    def dev(cc, zz, tt):
        return (lax.rem(cc + 2 * zz, NY) * NZ + zz, tt)

    def z_to(d):
        return at_z(-1) if d == 2 else z

    def z_from(d):
        return at_z(1) if d == 2 else z

    def next_to(d):
        return dev(at_c(d), z_to(d), t)

    def remote(src, dst, si, ri, device):
        return pltpu.make_async_remote_copy(
            src_ref=src, dst_ref=dst, send_sem=ss.at[si], recv_sem=rs.at[ri],
            device_id=device, device_id_type=MESH,
        )

    def recv(dst, ri):
        remote(dst, dst, ri, ri, next_to(1)).wait_recv()

    sends = []

    def send(src, dst, si, device):
        copy = remote(src, dst, si, si, device)
        copy.start()
        sends.append(copy)

    barrier = pltpu.get_barrier_semaphore()
    peers = (
        [dev(c, at_z(d), t) for d in range(1, NZ)]
        + [dev(at_c(1), z, t), dev(at_c(3), z, t), dev(at_c(2), at_z(1), t), dev(at_c(2), at_z(-1), t)]
        + [dev(c, z, at_t(d)) for d in range(1, TP)]
    )
    for peer in peers:
        pl.semaphore_signal(barrier, inc=1, device_id=peer, device_id_type=MESH)
    small_loads = [
        pltpu.make_async_copy(src, dst, ls.at[n])
        for n, (src, dst) in enumerate(((qq_hbm, qq), (qk_hbm, qk), (qv_hbm, qv)))
    ]
    loads = [
        pltpu.make_async_copy(src, kvb.at[c, n], ls.at[3 + n]) for n, src in enumerate((ck, cv))
    ]
    load_q = pltpu.make_async_copy(cq, cqv, ls.at[5])
    load_w = pltpu.make_async_copy(w, wv, ls.at[6])
    for copy in small_loads + loads + [load_q, load_w]:
        copy.start()
    pl.semaphore_wait(barrier, len(peers))

    def key_parts(part):
        at, length = (0, 2 * THIRD) if part == 0 else (2 * THIRD, THIRD)
        whole, half = pl.ds(at, length), length // 2
        return (
            (whole, dev(at_c(1), z, t), at_c(-1)),
            (whole, dev(at_c(3), z, t), at_c(-3)),
            (pl.ds(at, half), dev(at_c(2), at_z(-1), t), at_c(2)),
            (pl.ds(at + half, half), dev(at_c(2), at_z(1), t), at_c(2)),
        )

    def send_keys(part):
        for n, src in enumerate((ck, cv)):
            for k, (rows, peer, _) in enumerate(key_parts(part)):
                send(src.at[rows], kvb.at[c, n, rows], S_KV + 8 * part + 4 * n + k, peer)

    send_keys(0)
    for copy in small_loads:
        copy.wait()

    row8 = lax.broadcasted_iota(jnp.int32, (8, HD), 0)
    lane8 = lax.broadcasted_iota(jnp.int32, (8, HD), 1)
    qf = qq[...].astype(F32)
    qbuf[z, 0:64, :] = jnp.concatenate([qf[:, h * HD:(h + 1) * HD] for h in range(HEADS)], axis=0).astype(BF)
    pos = jnp.zeros((8, HD), jnp.int32)
    key_pos = jnp.full((8, HD), 512, jnp.int32)
    for r in range(QROWS):
        pos = jnp.where(row8 == r, qpos[r], pos)
        key_pos = jnp.where(lane8 == c * QROWS + r, qpos[r], key_pos)
    pos = pos.astype(F32)
    key_pos = key_pos.astype(F32)
    qbuf[z, 64:80, :] = jnp.concatenate([pos, pos], axis=0).astype(BF)
    length = jnp.zeros((8, HD), jnp.int32) + blen[0]
    info = jnp.concatenate([length // 128, lax.rem(length, 128)], axis=0).astype(F32).astype(BF)
    sml[c, 0:16, :] = jnp.concatenate([qk[...].astype(F32), qv[...].astype(F32)], axis=0).astype(BF)
    sml[c, 16:32, :] = jnp.concatenate([key_pos, key_pos], axis=0).astype(BF)
    sml[c, 32:48, :] = info

    for d in ZORDER:
        send(qbuf.at[z], qbuf.at[z], S_Q + d - 1, dev(c, at_z(d), t))
    for d in YORDER:
        send(sml.at[c], sml.at[c], S_SM + d - 1, next_to(d))
    send(sml.at[c], sml.at[NY], S_SM + 3, dev(at_c(2), at_z(1), t))
    send_keys(1)
    for copy in loads:
        copy.wait()

    row_of = lax.broadcasted_iota(jnp.int32, (THIRD, HD), 0)

    def live_keys(live, keys, other, values, to_kk, to_va, rows):
        to_kk[rows, :] = jnp.where(live, keys, other)
        to_va[rows, :HD] = jnp.where(live, values, jnp.zeros_like(values))
        to_va[rows, HD:] = jnp.where(live, 1.0, 0.0).astype(BF)

    for a in range(3):
        live_keys(
            row_of + a * THIRD < blen[0], kvb[c, 0, a * THIRD:(a + 1) * THIRD], kvb[c, 0, 0:1],
            kvb[c, 1, a * THIRD:(a + 1) * THIRD], kk, va, slice(a * THIRD, (a + 1) * THIRD),
        )
    rr = lax.broadcasted_iota(jnp.int32, (TILE, TILE), 0)
    cc = lax.broadcasted_iota(jnp.int32, (TILE, TILE), 1)
    bias[...] = jnp.where(cc <= rr, 0.0, NEG)
    load_q.wait()

    def own_step(rb, h):
        qt = cqv[rb * TILE:(rb + 1) * TILE, pl.ds(pl.multiple_of(h * HD, HD), HD)]
        diagonal = slice(rb * TILE, (rb + 1) * TILE)
        sd = lax.dot_general(qt, kk[diagonal], NT, preferred_element_type=F32) + bias[...]
        top = jnp.max(sd, axis=1, keepdims=True)
        if rb:
            so = lax.dot_general(qt, kk[0:rb * TILE], NT, preferred_element_type=F32)
            top = jnp.maximum(top, jnp.max(so, axis=1, keepdims=True))
        top_s = top * SCALE
        pd = jnp.exp2(sd * SCALE - top_s).astype(BF)
        acc = jnp.dot(pd, va[diagonal], preferred_element_type=F32)
        if rb:
            po = jnp.exp2(so * SCALE - top_s).astype(BF)
            acc = acc + jnp.dot(po, va[0:rb * TILE], preferred_element_type=F32)
        acco[rb * HEADS + h] = acc
        mo[rb * HEADS + h] = jnp.broadcast_to(top_s, (TILE, HD))

    def own_steps(rb):
        @pl.loop(0, HEADS // HG)
        def _(i):
            for u in range(HG):
                own_step(rb, i * HG + u)

    own_steps(0)

    own_steps(1)
    own_steps(2)

    for d in range(1, NZ):
        recv(qbuf.at[at_z(-d)], S_Q + d - 1)
    for d in range(1, NY):
        recv(sml.at[at_c(-d)], S_SM + d - 1)
    recv(sml.at[NY], S_SM + 3)
    half = NZ // 2 * 64

    def asked(i):
        return jnp.concatenate([qbuf[i * 4 + j, 0:64, :] for j in range(4)], axis=0)

    small = [sml[j].astype(F32) for j in range(NY)]
    zero96 = jnp.zeros((HD - NY * QROWS, HD), F32)
    ext_k = jnp.concatenate([s[0:8] for s in small] + [zero96], axis=0).astype(BF)
    ext_v = jnp.concatenate([s[8:16] for s in small] + [zero96], axis=0).astype(BF)
    ext_va = jnp.concatenate([ext_v, jnp.ones((HD, HD), BF)], axis=1)
    ext_pos = functools.reduce(jnp.minimum, [s[16:17] for s in small])

    for i in range(2):
        qt = asked(i)
        rows_pos = jnp.concatenate(
            [p for j in range(4) for p in [qbuf[i * 4 + j, 64:80, :].astype(F32)[0:8]] * HEADS], axis=0
        )
        se = lax.dot_general(qt, ext_k, NT, preferred_element_type=F32)
        se = jnp.where(ext_pos <= rows_pos, se, NEG)
        sa = lax.dot_general(qt, kk[...], NT, preferred_element_type=F32)
        top = jnp.maximum(jnp.max(se, axis=1, keepdims=True), jnp.max(sa, axis=1, keepdims=True)) * SCALE
        acc = jnp.dot(jnp.exp2(sa * SCALE - top).astype(BF), va[...], preferred_element_type=F32)
        acc = acc + jnp.dot(jnp.exp2(se * SCALE - top).astype(BF), ext_va, preferred_element_type=F32)
        m2[i * half:(i + 1) * half] = jnp.broadcast_to(top, (half, HD))
        acc2[i * half:(i + 1) * half] = acc

    def length_of(slot):
        length = sml[slot, 32:48, :].astype(F32)
        return length[0:1] * 128.0 + length[8:9]

    def phase_two(thirds):
        at = 0
        below = length_of(NY)
        for d in range(1, NY):
            slot = at_c(-d)
            above = length_of(slot)
            for a in thirds:
                live_to = above
                if d == 2 and a:
                    live_to = jnp.where(row_of < THIRD // 2, above, below) if a == 2 else below
                live_keys(
                    (row_of + a * THIRD).astype(F32) < live_to, kvb[slot, 0, a * THIRD:(a + 1) * THIRD],
                    kvb[slot, 0, 0:1], kvb[slot, 1, a * THIRD:(a + 1) * THIRD], p2kk, p2va, slice(at, at + THIRD),
                )
                at += THIRD
        for i in range(2):
            part = slice(i * half, (i + 1) * half)
            sa = lax.dot_general(asked(i), p2kk[0:at], NT, preferred_element_type=F32)
            old = m2[part]
            top = jnp.maximum(jnp.max(sa, axis=1, keepdims=True) * SCALE, old)
            acc = jnp.dot(jnp.exp2(sa * SCALE - top[:, 0:1]).astype(BF), p2va[0:at], preferred_element_type=F32)
            keep = jnp.exp2(old - top)
            acc2[part] = acc + acc2[part] * jnp.concatenate([keep, keep], axis=1)
            m2[part] = top

    def recv_keys(part):
        for n in range(2):
            for k, (rows, _, slot) in enumerate(key_parts(part)):
                recv(kvb.at[slot, n, rows], S_KV + 8 * part + 4 * n + k)

    recv_keys(0)
    phase_two((0, 1))
    recv_keys(1)

    source_z = jnp.where(c == 2, NZ - 1, 0)

    @pl.when(z == source_z)
    def _():
        for j in range(NZ):
            row = pl.multiple_of(at_c(2) * (ROWS // 4) + j % 4 * SL, 16)
            rst[j, 0:SL, :] = kvb[0, j // 4, pl.ds(row, SL), :]
            rst[j, SL:SL + 16, :] = sml[0, 32:48, :]
        akv[c, z] = rst[z]
        for d in range(1, NZ):
            to_z = at_z(d)
            remote(rst.at[to_z], akv.at[c, to_z], S_AA + d - 1, S_AA, dev(c, to_z, t)).start()

    phase_two((2,))

    total = acc2[:, HD:]
    lse = m2[...] + jnp.log(total) * LOG2E
    part_out = acc2[:, :HD] / total
    for j in range(NZ):
        compact = jnp.zeros((8, HD), F32)
        for h in range(HEADS):
            compact = jnp.where(lane8 == h, lse[j * 64 + h * 8:j * 64 + h * 8 + 8], compact)
        high = compact.astype(BF).astype(F32)
        middle = (compact - high).astype(BF).astype(F32)
        low = compact - high - middle
        cmsg[j, 0:64, :] = part_out[j * 64:(j + 1) * 64].astype(BF)
        pieces = high + pltpu.roll(middle, 8, 1) + pltpu.roll(low, 16, 1)
        cmsg[j, 64:80, :] = jnp.concatenate([pieces, pieces], axis=0).astype(BF)
    for d in ZORDER:
        send(cmsg.at[at_z(d)], crecv.at[z], S_PZ + d - 1, dev(c, at_z(d), t))

    @pl.when(z != source_z)
    def _():
        recv(akv.at[c, z], S_AA)

    for d in ZORDER:
        send(akv.at[c, z], akv.at[c, z], S_AC + d - 1, dev(c, at_z(d), t))


    for d in range(1, NZ):
        recv(crecv.at[at_z(-d)], S_PZ + d - 1)
    parts = [cmsg[z].astype(F32)] + [crecv[at_z(-d)].astype(F32) for d in range(1, NZ)]
    lses = [p[64:72] + pltpu.roll(p[64:72], HD - 8, 1) + pltpu.roll(p[64:72], HD - 16, 1) for p in parts]
    top = functools.reduce(jnp.maximum, lses)
    weights = [jnp.exp2(x - top) for x in lses]
    weight_sum = functools.reduce(jnp.add, weights)
    weights = [x / weight_sum for x in weights]
    merged = []
    for h in range(HEADS):
        merged.append(functools.reduce(
            jnp.add, [x[:, h:h + 1] * p[h * 8:h * 8 + 8] for x, p in zip(weights, parts)]
        ))
    merged = jnp.concatenate(
        [jnp.concatenate(merged[0:4], axis=1), jnp.concatenate(merged[4:8], axis=1)], axis=0
    )
    abuf[c, z] = merged.astype(BF)

    for d in ZORDER:
        send(abuf.at[c, z], abuf.at[c, z], S_TZ + d - 1, dev(c, at_z(d), t))

    def pass_on(k):
        zz = at_z(-k)
        if k:
            recv(abuf.at[c, zz], S_TZ + k - 1)
        for d in YORDER:
            send(abuf.at[c, zz], abuf.at[c, zz], S_TY + 3 * k + d - 1, next_to(d))

    pass_on(0)
    for d in range(1, NZ):
        recv(akv.at[c, at_z(-d)], S_AC + d - 1)
    data = pl.ds(0, SL)
    for d in YORDER:
        send(akv.at[c, :, data], akv.at[c, :, data], S_AD + d - 1, next_to(d))

    for k in ZORDER:
        pass_on(k)

    def anchor_step(i):
        cols = pl.ds(pl.multiple_of(lax.rem(i, HEADS) * HD, HD), HD)
        rows = pl.ds(pl.multiple_of(i // HEADS * TILE, TILE), TILE)
        sa = lax.dot_general(cqv[rows, cols], akk[...], NT, preferred_element_type=F32)
        old = mo[i]
        top = jnp.maximum(jnp.max(sa, axis=1, keepdims=True) * SCALE, old)
        acc = jnp.dot(jnp.exp2(sa * SCALE - top[:, 0:1]).astype(BF), ava[...], preferred_element_type=F32)
        keep = jnp.exp2(old - top)
        acc = acc + acco[i] * jnp.concatenate([keep, keep], axis=1)
        obuf[rows, cols] = (acc[:, :HD] / acc[:, HD:]).astype(BF)

    stores = [
        pltpu.make_async_copy(obuf.at[pl.ds(rb * TILE, TILE)], out.at[pl.ds(rb * TILE, TILE)], ls.at[rb])
        for rb in range(NRB)
    ]

    def anchor_steps(start, steps):
        @pl.loop(0, 2)
        def _(i):
            for u in range(steps // 2):
                anchor_step(start + i * (steps // 2) + u)

    load_w.wait()
    for k in range(NZ):
        for d in range(1, NY):
            recv(abuf.at[at_c(-d), lax.rem(z_from(d) - k + NZ, NZ)], S_TY + 3 * k + d - 1)

    rows = jnp.concatenate([abuf[(yy + 2 * zz) % NY, zz] for yy in range(NY) for zz in range(NZ)], axis=0)
    upper = jnp.dot(rows, wv[0:4 * HD], preferred_element_type=F32).reshape(NY * NZ, 16, -1)
    lower = jnp.dot(rows, wv[4 * HD:], preferred_element_type=F32).reshape(NY * NZ, 16, -1)
    partial = (upper[:, 0:8] + lower[:, 8:16]).reshape(pown.shape)
    pown[...] = partial
    psend[...] = partial.astype(BF)
    for d in range(1, TP):
        send(psend.at[at_t(d)], prec.at[t], S_RX + d - 1, dev(c, z, at_t(d)))
    for d in range(1, NY):
        recv(akv.at[at_c(-d), :, data], S_AD + d - 1)
    alen = akv[c, z, SL:SL + 16, :].astype(F32)
    alive_to = jnp.where(ctx == 0, 0.0, alen[0:1] * 128.0 + alen[8:9])
    anchor_k, anchor_v = (
        jnp.concatenate([akv[(p + 2) % 4, n:n + 4, 0:SL, :].reshape(4 * SL, HD) for p in range(4)], axis=0)
        for n in (0, 4)
    )
    for a in range(3):
        part = slice(a * THIRD, (a + 1) * THIRD)
        live_keys(
            (row_of + a * THIRD).astype(F32) < alive_to, anchor_k[part], anchor_k[0:1], anchor_v[part],
            akk, ava, part,
        )

    anchor_steps(0, 14)
    stores[0].start()
    for d in range(1, TP):
        recv(prec.at[at_t(-d)], S_RX + d - 1)
    answer = pown[t]
    for d in range(1, TP):
        answer = answer + prec[at_t(-d)].astype(F32)
    ansb[t] = answer.astype(BF)
    for d in range(1, TP):
        send(ansb.at[t], ansb.at[t], S_GX + d - 1, dev(c, z, at_t(d)))
    anchor_steps(14, 10)
    stores[1].start()
    stores[2].start()
    for d in range(1, TP):
        recv(ansb.at[at_t(-d)], S_GX + d - 1)
    ans[...] = ansb[...].reshape(ans.shape)

    for copy in sends:
        copy.wait_send()

    @pl.when(z == source_z)
    def _():
        for d in range(1, NZ):
            to_z = at_z(d)
            remote(rst.at[to_z], akv.at[c, to_z], S_AA + d - 1, S_AA, dev(c, to_z, t)).wait_send()

    for copy in stores:
        copy.wait()


def finish(block, answer, block_out, answer_out, held, held_answer, sem):
    rows = ROWS // COPIES
    pieces = [(block, held, block_out, pl.ds(i * rows, rows)) for i in range(COPIES)]
    pieces.append((answer, held_answer, answer_out, pl.ds(0, answer.shape[0])))
    loads = [
        pltpu.make_async_copy(src.at[at], here.at[at], sem.at[2 * i]) for i, (src, here, _, at) in enumerate(pieces)
    ]
    stores = [
        pltpu.make_async_copy(here.at[at], dst.at[at], sem.at[2 * i + 1])
        for i, (_, here, dst, at) in enumerate(pieces)
    ]
    for copy in loads:
        copy.start()
    for load, store in zip(loads, stores):
        load.wait()
        store.start()
    for copy in stores:
        copy.wait()


def body(cq, ck, cv, blen, qq, qk, qv, qpos, w):
    hbm = pl.BlockSpec(memory_space=pl.ANY)
    vmem = pl.BlockSpec(memory_space=pltpu.VMEM)
    smem = pl.BlockSpec(memory_space=pltpu.SMEM)
    columns = w.shape[1]
    v = pltpu.VMEM
    results = pl.pallas_call(
        kernel,
        out_shape=(
            jax.ShapeDtypeStruct(cq.shape, BF),
            jax.ShapeDtypeStruct((NY * NZ * QROWS, columns), BF),
        ),
        in_specs=[hbm, hbm, hbm, smem, hbm, hbm, hbm, smem, hbm],
        out_specs=(hbm, vmem),
        scratch_shapes=[
            v(qq.shape, BF),
            v(qk.shape, BF),
            v(qv.shape, BF),
            v(cq.shape, BF),
            v(w.shape, BF),
            v((NY, 2, ROWS, HD), BF),
            v((ROWS, HD), BF),
            v((ROWS, 2 * HD), BF),
            v((ROWS, HD), BF),
            v((ROWS, 2 * HD), BF),
            v((TILE, TILE), F32),
            v((NRB * HEADS, TILE, HD), F32),
            v((NRB * HEADS, TILE, 2 * HD), F32),
            v(cq.shape, BF),
            v((NZ, 80, HD), BF),
            v((NY + 1, 48, HD), BF),
            v((NZ, SL + 16, HD), BF),
            v((4, NZ, SL + 16, HD), BF),
            v((2 * ROWS, HD), BF),
            v((2 * ROWS, 2 * HD), BF),
            v((NZ * 64, HD), F32),
            v((NZ * 64, 2 * HD), F32),
            v((NZ, 80, HD), BF),
            v((NZ, 80, HD), BF),
            v((NY, NZ, 16, 4 * HD), BF),
            v((TP, NY * NZ, columns), F32),
            v((TP, NY * NZ, columns), BF),
            v((TP, NY * NZ, columns), BF),
            v((TP, NY * NZ, columns), BF),
            pltpu.SemaphoreType.DMA((N_SEM,)),
            pltpu.SemaphoreType.DMA((N_SEM,)),
            pltpu.SemaphoreType.DMA((12,)),
        ],
        compiler_params=pltpu.CompilerParams(
            collective_id=1, has_side_effects=True, vmem_limit_bytes=63 * 2**20
        ),
        name="star_attention",
    )(cq, ck, cv, blen, qq, qk, qv, qpos, w)
    return pl.pallas_call(
        finish,
        out_shape=tuple(jax.ShapeDtypeStruct(x.shape, x.dtype) for x in results),
        in_specs=[hbm, hbm],
        out_specs=(hbm, hbm),
        scratch_shapes=[v(x.shape, x.dtype) for x in results] + [pltpu.SemaphoreType.DMA((2 * COPIES + 2,))],
        compiler_params=pltpu.CompilerParams(vmem_limit_bytes=62 * 2**20),
        name="results",
    )(*results)


def solution(mesh):
    in_specs = (
        P("ctx", "tp"),
        P("ctx", "tp"),
        P("ctx", "tp"),
        P("ctx"),
        P("ctx", "tp"),
        P("ctx", "tp"),
        P("ctx", "tp"),
        P("ctx"),
        P("tp", "ctx"),
    )
    out_specs = (P("ctx", "tp"), P(None, "ctx"))
    return jax.shard_map(body, mesh=mesh, in_specs=in_specs, out_specs=out_specs, check_vma=False)
```

```python
import functools
import math

import jax
import jax.numpy as jnp
from jax import lax
from jax.experimental import pallas as pl
from jax.experimental.pallas import tpu as pltpu
from jax.sharding import PartitionSpec as P

MESH = pl.DeviceIdType.MESH
NT = (((1,), (1,)), ((), ()))
BF = jnp.bfloat16
F32 = jnp.float32
NEG = -1e30
HD = 128
HEADS = 8
NY, NZ, TP = 4, 8, 8
ROWS = 768
QROWS = 8
TILE = 256
NRB = ROWS // TILE
SL = ROWS * 2 // (NY * NZ)
THIRD = ROWS // 3
SCALE = math.log2(math.e) / math.sqrt(HD)
LOG2E = math.log2(math.e)
ZORDER = (1, 7, 2, 6, 3, 5, 4)
YORDER = (1, 3, 2)
COPIES = 4
HG = 4

S_Q, S_SM, S_KV, S_AA, S_AC, S_AD = 0, 7, 11, 27, 34, 41
S_PZ, S_TZ, S_TY, S_RX, S_GX = 44, 51, 58, 82, 89
N_SEM = 96


def kernel(
    cq, ck, cv, blen, qq_hbm, qk_hbm, qv_hbm, qpos, w,
    out, ans,
    qq, qk, qv, cqv, wv, kvb, kk, va, akk, ava, bias,
    mo, acco, obuf,
    qbuf, sml, rst, akv,
    p2kk, p2va, m2, acc2,
    cmsg, crecv, abuf, pown, psend, prec, ansb,
    ss, rs, ls,
):
    ctx = lax.axis_index("ctx")
    t = lax.axis_index("tp")
    z = lax.rem(ctx, NZ)
    c = lax.rem(ctx // NZ + 2 * z, NY)

    def at_z(d):
        return lax.rem(z + d + NZ, NZ)

    def at_c(d):
        return lax.rem(c + d + NY, NY)

    def at_t(d):
        return lax.rem(t + d + TP, TP)

    def dev(cc, zz, tt):
        return (lax.rem(cc + 2 * zz, NY) * NZ + zz, tt)

    def z_to(d):
        return at_z(-1) if d == 2 else z

    def z_from(d):
        return at_z(1) if d == 2 else z

    def next_to(d):
        return dev(at_c(d), z_to(d), t)

    def remote(src, dst, si, ri, device):
        return pltpu.make_async_remote_copy(
            src_ref=src, dst_ref=dst, send_sem=ss.at[si], recv_sem=rs.at[ri],
            device_id=device, device_id_type=MESH,
        )

    def recv(dst, ri):
        remote(dst, dst, ri, ri, next_to(1)).wait_recv()

    sends = []

    def send(src, dst, si, device):
        copy = remote(src, dst, si, si, device)
        copy.start()
        sends.append(copy)

    barrier = pltpu.get_barrier_semaphore()
    peers = (
        [dev(c, at_z(d), t) for d in range(1, NZ)]
        + [dev(at_c(1), z, t), dev(at_c(3), z, t), dev(at_c(2), at_z(1), t), dev(at_c(2), at_z(-1), t)]
        + [dev(c, z, at_t(d)) for d in range(1, TP)]
    )
    for peer in peers:
        pl.semaphore_signal(barrier, inc=1, device_id=peer, device_id_type=MESH)
    small_loads = [
        pltpu.make_async_copy(src, dst, ls.at[n])
        for n, (src, dst) in enumerate(((qq_hbm, qq), (qk_hbm, qk), (qv_hbm, qv)))
    ]
    loads = [
        pltpu.make_async_copy(src, kvb.at[c, n], ls.at[3 + n]) for n, src in enumerate((ck, cv))
    ]
    load_q = pltpu.make_async_copy(cq, cqv, ls.at[5])
    load_w = pltpu.make_async_copy(w, wv, ls.at[6])
    for copy in small_loads + loads + [load_q, load_w]:
        copy.start()
    pl.semaphore_wait(barrier, len(peers))

    def key_parts(part):
        at, length = (0, 2 * THIRD) if part == 0 else (2 * THIRD, THIRD)
        whole, half = pl.ds(at, length), length // 2
        return (
            (whole, dev(at_c(1), z, t), at_c(-1)),
            (whole, dev(at_c(3), z, t), at_c(-3)),
            (pl.ds(at, half), dev(at_c(2), at_z(-1), t), at_c(2)),
            (pl.ds(at + half, half), dev(at_c(2), at_z(1), t), at_c(2)),
        )

    def send_keys(part):
        for n, src in enumerate((ck, cv)):
            for k, (rows, peer, _) in enumerate(key_parts(part)):
                send(src.at[rows], kvb.at[c, n, rows], S_KV + 8 * part + 4 * n + k, peer)

    send_keys(0)
    for copy in small_loads:
        copy.wait()

    row8 = lax.broadcasted_iota(jnp.int32, (8, HD), 0)
    lane8 = lax.broadcasted_iota(jnp.int32, (8, HD), 1)
    qf = qq[...].astype(F32)
    qbuf[z, 0:64, :] = jnp.concatenate([qf[:, h * HD:(h + 1) * HD] for h in range(HEADS)], axis=0).astype(BF)
    pos = jnp.zeros((8, HD), jnp.int32)
    key_pos = jnp.full((8, HD), 512, jnp.int32)
    for r in range(QROWS):
        pos = jnp.where(row8 == r, qpos[r], pos)
        key_pos = jnp.where(lane8 == c * QROWS + r, qpos[r], key_pos)
    pos = pos.astype(F32)
    key_pos = key_pos.astype(F32)
    qbuf[z, 64:80, :] = jnp.concatenate([pos, pos], axis=0).astype(BF)
    length = jnp.zeros((8, HD), jnp.int32) + blen[0]
    info = jnp.concatenate([length // 128, lax.rem(length, 128)], axis=0).astype(F32).astype(BF)
    sml[c, 0:16, :] = jnp.concatenate([qk[...].astype(F32), qv[...].astype(F32)], axis=0).astype(BF)
    sml[c, 16:32, :] = jnp.concatenate([key_pos, key_pos], axis=0).astype(BF)
    sml[c, 32:48, :] = info

    for d in ZORDER:
        send(qbuf.at[z], qbuf.at[z], S_Q + d - 1, dev(c, at_z(d), t))
    for d in YORDER:
        send(sml.at[c], sml.at[c], S_SM + d - 1, next_to(d))
    send(sml.at[c], sml.at[NY], S_SM + 3, dev(at_c(2), at_z(1), t))
    for copy in loads:
        copy.wait()

    row_of = lax.broadcasted_iota(jnp.int32, (THIRD, HD), 0)

    def live_keys(live, keys, other, values, to_kk, to_va, rows):
        to_kk[rows, :] = jnp.where(live, keys, other)
        to_va[rows, :HD] = jnp.where(live, values, jnp.zeros_like(values))
        to_va[rows, HD:] = jnp.where(live, 1.0, 0.0).astype(BF)

    for a in range(3):
        live_keys(
            row_of + a * THIRD < blen[0], kvb[c, 0, a * THIRD:(a + 1) * THIRD], kvb[c, 0, 0:1],
            kvb[c, 1, a * THIRD:(a + 1) * THIRD], kk, va, slice(a * THIRD, (a + 1) * THIRD),
        )
    rr = lax.broadcasted_iota(jnp.int32, (TILE, TILE), 0)
    cc = lax.broadcasted_iota(jnp.int32, (TILE, TILE), 1)
    bias[...] = jnp.where(cc <= rr, 0.0, NEG)
    load_q.wait()

    def own_step(rb, h):
        qt = cqv[rb * TILE:(rb + 1) * TILE, pl.ds(pl.multiple_of(h * HD, HD), HD)]
        diagonal = slice(rb * TILE, (rb + 1) * TILE)
        sd = lax.dot_general(qt, kk[diagonal], NT, preferred_element_type=F32) + bias[...]
        top = jnp.max(sd, axis=1, keepdims=True)
        if rb:
            so = lax.dot_general(qt, kk[0:rb * TILE], NT, preferred_element_type=F32)
            top = jnp.maximum(top, jnp.max(so, axis=1, keepdims=True))
        top_s = top * SCALE
        pd = jnp.exp2(sd * SCALE - top_s).astype(BF)
        acc = jnp.dot(pd, va[diagonal], preferred_element_type=F32)
        if rb:
            po = jnp.exp2(so * SCALE - top_s).astype(BF)
            acc = acc + jnp.dot(po, va[0:rb * TILE], preferred_element_type=F32)
        acco[rb * HEADS + h] = acc
        mo[rb * HEADS + h] = jnp.broadcast_to(top_s, (TILE, HD))

    def own_steps(rb):
        @pl.loop(0, HEADS // HG)
        def _(i):
            for u in range(HG):
                own_step(rb, i * HG + u)

    own_steps(0)

    own_steps(1)
    send_keys(1)
    own_steps(2)

    for d in range(1, NZ):
        recv(qbuf.at[at_z(-d)], S_Q + d - 1)
    for d in range(1, NY):
        recv(sml.at[at_c(-d)], S_SM + d - 1)
    recv(sml.at[NY], S_SM + 3)
    half = NZ // 2 * 64

    def asked(i):
        return jnp.concatenate([qbuf[i * 4 + j, 0:64, :] for j in range(4)], axis=0)

    small = [sml[j].astype(F32) for j in range(NY)]
    zero96 = jnp.zeros((HD - NY * QROWS, HD), F32)
    ext_k = jnp.concatenate([s[0:8] for s in small] + [zero96], axis=0).astype(BF)
    ext_v = jnp.concatenate([s[8:16] for s in small] + [zero96], axis=0).astype(BF)
    ext_va = jnp.concatenate([ext_v, jnp.ones((HD, HD), BF)], axis=1)
    ext_pos = functools.reduce(jnp.minimum, [s[16:17] for s in small])

    for i in range(2):
        qt = asked(i)
        rows_pos = jnp.concatenate(
            [p for j in range(4) for p in [qbuf[i * 4 + j, 64:80, :].astype(F32)[0:8]] * HEADS], axis=0
        )
        se = lax.dot_general(qt, ext_k, NT, preferred_element_type=F32)
        se = jnp.where(ext_pos <= rows_pos, se, NEG)
        sa = lax.dot_general(qt, kk[...], NT, preferred_element_type=F32)
        top = jnp.maximum(jnp.max(se, axis=1, keepdims=True), jnp.max(sa, axis=1, keepdims=True)) * SCALE
        acc = jnp.dot(jnp.exp2(sa * SCALE - top).astype(BF), va[...], preferred_element_type=F32)
        acc = acc + jnp.dot(jnp.exp2(se * SCALE - top).astype(BF), ext_va, preferred_element_type=F32)
        m2[i * half:(i + 1) * half] = jnp.broadcast_to(top, (half, HD))
        acc2[i * half:(i + 1) * half] = acc

    def length_of(slot):
        length = sml[slot, 32:48, :].astype(F32)
        return length[0:1] * 128.0 + length[8:9]

    def phase_two(thirds):
        at = 0
        below = length_of(NY)
        for d in range(1, NY):
            slot = at_c(-d)
            above = length_of(slot)
            for a in thirds:
                live_to = above
                if d == 2 and a:
                    live_to = jnp.where(row_of < THIRD // 2, above, below) if a == 2 else below
                live_keys(
                    (row_of + a * THIRD).astype(F32) < live_to, kvb[slot, 0, a * THIRD:(a + 1) * THIRD],
                    kvb[slot, 0, 0:1], kvb[slot, 1, a * THIRD:(a + 1) * THIRD], p2kk, p2va, slice(at, at + THIRD),
                )
                at += THIRD
        for i in range(2):
            part = slice(i * half, (i + 1) * half)
            sa = lax.dot_general(asked(i), p2kk[0:at], NT, preferred_element_type=F32)
            old = m2[part]
            top = jnp.maximum(jnp.max(sa, axis=1, keepdims=True) * SCALE, old)
            acc = jnp.dot(jnp.exp2(sa * SCALE - top[:, 0:1]).astype(BF), p2va[0:at], preferred_element_type=F32)
            keep = jnp.exp2(old - top)
            acc2[part] = acc + acc2[part] * jnp.concatenate([keep, keep], axis=1)
            m2[part] = top

    def recv_keys(part):
        for n in range(2):
            for k, (rows, _, slot) in enumerate(key_parts(part)):
                recv(kvb.at[slot, n, rows], S_KV + 8 * part + 4 * n + k)

    recv_keys(0)
    phase_two((0, 1))
    recv_keys(1)

    source_z = jnp.where(c == 2, NZ - 1, 0)

    @pl.when(z == source_z)
    def _():
        for j in range(NZ):
            row = pl.multiple_of(at_c(2) * (ROWS // 4) + j % 4 * SL, 16)
            rst[j, 0:SL, :] = kvb[0, j // 4, pl.ds(row, SL), :]
            rst[j, SL:SL + 16, :] = sml[0, 32:48, :]
        akv[c, z] = rst[z]
        for d in range(1, NZ):
            to_z = at_z(d)
            remote(rst.at[to_z], akv.at[c, to_z], S_AA + d - 1, S_AA, dev(c, to_z, t)).start()

    phase_two((2,))

    total = acc2[:, HD:]
    lse = m2[...] + jnp.log(total) * LOG2E
    part_out = acc2[:, :HD] / total
    for j in range(NZ):
        compact = jnp.zeros((8, HD), F32)
        for h in range(HEADS):
            compact = jnp.where(lane8 == h, lse[j * 64 + h * 8:j * 64 + h * 8 + 8], compact)
        high = compact.astype(BF).astype(F32)
        middle = (compact - high).astype(BF).astype(F32)
        low = compact - high - middle
        cmsg[j, 0:64, :] = part_out[j * 64:(j + 1) * 64].astype(BF)
        pieces = high + pltpu.roll(middle, 8, 1) + pltpu.roll(low, 16, 1)
        cmsg[j, 64:80, :] = jnp.concatenate([pieces, pieces], axis=0).astype(BF)
    for d in ZORDER:
        send(cmsg.at[at_z(d)], crecv.at[z], S_PZ + d - 1, dev(c, at_z(d), t))

    @pl.when(z != source_z)
    def _():
        recv(akv.at[c, z], S_AA)

    for d in ZORDER:
        send(akv.at[c, z], akv.at[c, z], S_AC + d - 1, dev(c, at_z(d), t))


    for d in range(1, NZ):
        recv(crecv.at[at_z(-d)], S_PZ + d - 1)
    parts = [cmsg[z].astype(F32)] + [crecv[at_z(-d)].astype(F32) for d in range(1, NZ)]
    lses = [p[64:72] + pltpu.roll(p[64:72], HD - 8, 1) + pltpu.roll(p[64:72], HD - 16, 1) for p in parts]
    top = functools.reduce(jnp.maximum, lses)
    weights = [jnp.exp2(x - top) for x in lses]
    weight_sum = functools.reduce(jnp.add, weights)
    weights = [x / weight_sum for x in weights]
    merged = []
    for h in range(HEADS):
        merged.append(functools.reduce(
            jnp.add, [x[:, h:h + 1] * p[h * 8:h * 8 + 8] for x, p in zip(weights, parts)]
        ))
    merged = jnp.concatenate(
        [jnp.concatenate(merged[0:4], axis=1), jnp.concatenate(merged[4:8], axis=1)], axis=0
    )
    abuf[c, z] = merged.astype(BF)

    for d in ZORDER:
        send(abuf.at[c, z], abuf.at[c, z], S_TZ + d - 1, dev(c, at_z(d), t))

    def pass_on(k):
        zz = at_z(-k)
        if k:
            recv(abuf.at[c, zz], S_TZ + k - 1)
        for d in YORDER:
            send(abuf.at[c, zz], abuf.at[c, zz], S_TY + 3 * k + d - 1, next_to(d))

    pass_on(0)
    for d in range(1, NZ):
        recv(akv.at[c, at_z(-d)], S_AC + d - 1)
    data = pl.ds(0, SL)
    for d in YORDER:
        send(akv.at[c, :, data], akv.at[c, :, data], S_AD + d - 1, next_to(d))

    for k in ZORDER:
        pass_on(k)

    def anchor_step(i):
        cols = pl.ds(pl.multiple_of(lax.rem(i, HEADS) * HD, HD), HD)
        rows = pl.ds(pl.multiple_of(i // HEADS * TILE, TILE), TILE)
        sa = lax.dot_general(cqv[rows, cols], akk[...], NT, preferred_element_type=F32)
        old = mo[i]
        top = jnp.maximum(jnp.max(sa, axis=1, keepdims=True) * SCALE, old)
        acc = jnp.dot(jnp.exp2(sa * SCALE - top[:, 0:1]).astype(BF), ava[...], preferred_element_type=F32)
        keep = jnp.exp2(old - top)
        acc = acc + acco[i] * jnp.concatenate([keep, keep], axis=1)
        obuf[rows, cols] = (acc[:, :HD] / acc[:, HD:]).astype(BF)

    stores = [
        pltpu.make_async_copy(obuf.at[pl.ds(rb * TILE, TILE)], out.at[pl.ds(rb * TILE, TILE)], ls.at[rb])
        for rb in range(NRB)
    ]

    def anchor_steps(start, steps):
        @pl.loop(0, 2)
        def _(i):
            for u in range(steps // 2):
                anchor_step(start + i * (steps // 2) + u)

    for d in range(1, NY):
        recv(akv.at[at_c(-d), :, data], S_AD + d - 1)
    alen = akv[c, z, SL:SL + 16, :].astype(F32)
    alive_to = jnp.where(ctx == 0, 0.0, alen[0:1] * 128.0 + alen[8:9])
    anchor_k, anchor_v = (
        jnp.concatenate([akv[(p + 2) % 4, n:n + 4, 0:SL, :].reshape(4 * SL, HD) for p in range(4)], axis=0)
        for n in (0, 4)
    )
    for a in range(3):
        part = slice(a * THIRD, (a + 1) * THIRD)
        live_keys(
            (row_of + a * THIRD).astype(F32) < alive_to, anchor_k[part], anchor_k[0:1], anchor_v[part],
            akk, ava, part,
        )

    anchor_steps(0, 4)
    load_w.wait()
    for k in range(NZ):
        for d in range(1, NY):
            recv(abuf.at[at_c(-d), lax.rem(z_from(d) - k + NZ, NZ)], S_TY + 3 * k + d - 1)

    rows = jnp.concatenate([abuf[(yy + 2 * zz) % NY, zz] for yy in range(NY) for zz in range(NZ)], axis=0)
    upper = jnp.dot(rows, wv[0:4 * HD], preferred_element_type=F32).reshape(NY * NZ, 16, -1)
    lower = jnp.dot(rows, wv[4 * HD:], preferred_element_type=F32).reshape(NY * NZ, 16, -1)
    partial = (upper[:, 0:8] + lower[:, 8:16]).reshape(pown.shape)
    pown[...] = partial
    psend[...] = partial.astype(BF)
    for d in range(1, TP):
        send(psend.at[at_t(d)], prec.at[t], S_RX + d - 1, dev(c, z, at_t(d)))
    anchor_steps(4, 12)
    stores[0].start()
    stores[1].start()
    for d in range(1, TP):
        recv(prec.at[at_t(-d)], S_RX + d - 1)
    answer = pown[t]
    for d in range(1, TP):
        answer = answer + prec[at_t(-d)].astype(F32)
    ansb[t] = answer.astype(BF)
    for d in range(1, TP):
        send(ansb.at[t], ansb.at[t], S_GX + d - 1, dev(c, z, at_t(d)))
    anchor_steps(16, 8)
    stores[2].start()
    for d in range(1, TP):
        recv(ansb.at[at_t(-d)], S_GX + d - 1)
    ans[...] = ansb[...].reshape(ans.shape)

    for copy in sends:
        copy.wait_send()

    @pl.when(z == source_z)
    def _():
        for d in range(1, NZ):
            to_z = at_z(d)
            remote(rst.at[to_z], akv.at[c, to_z], S_AA + d - 1, S_AA, dev(c, to_z, t)).wait_send()

    for copy in stores:
        copy.wait()


def finish(block, answer, block_out, answer_out, held, held_answer, sem):
    rows = ROWS // COPIES
    pieces = [(block, held, block_out, pl.ds(i * rows, rows)) for i in range(COPIES)]
    pieces.append((answer, held_answer, answer_out, pl.ds(0, answer.shape[0])))
    loads = [
        pltpu.make_async_copy(src.at[at], here.at[at], sem.at[2 * i]) for i, (src, here, _, at) in enumerate(pieces)
    ]
    stores = [
        pltpu.make_async_copy(here.at[at], dst.at[at], sem.at[2 * i + 1])
        for i, (_, here, dst, at) in enumerate(pieces)
    ]
    for copy in loads:
        copy.start()
    for load, store in zip(loads, stores):
        load.wait()
        store.start()
    for copy in stores:
        copy.wait()


def body(cq, ck, cv, blen, qq, qk, qv, qpos, w):
    hbm = pl.BlockSpec(memory_space=pl.ANY)
    vmem = pl.BlockSpec(memory_space=pltpu.VMEM)
    smem = pl.BlockSpec(memory_space=pltpu.SMEM)
    columns = w.shape[1]
    v = pltpu.VMEM
    results = pl.pallas_call(
        kernel,
        out_shape=(
            jax.ShapeDtypeStruct(cq.shape, BF),
            jax.ShapeDtypeStruct((NY * NZ * QROWS, columns), BF),
        ),
        in_specs=[hbm, hbm, hbm, smem, hbm, hbm, hbm, smem, hbm],
        out_specs=(hbm, vmem),
        scratch_shapes=[
            v(qq.shape, BF),
            v(qk.shape, BF),
            v(qv.shape, BF),
            v(cq.shape, BF),
            v(w.shape, BF),
            v((NY, 2, ROWS, HD), BF),
            v((ROWS, HD), BF),
            v((ROWS, 2 * HD), BF),
            v((ROWS, HD), BF),
            v((ROWS, 2 * HD), BF),
            v((TILE, TILE), F32),
            v((NRB * HEADS, TILE, HD), F32),
            v((NRB * HEADS, TILE, 2 * HD), F32),
            v(cq.shape, BF),
            v((NZ, 80, HD), BF),
            v((NY + 1, 48, HD), BF),
            v((NZ, SL + 16, HD), BF),
            v((4, NZ, SL + 16, HD), BF),
            v((2 * ROWS, HD), BF),
            v((2 * ROWS, 2 * HD), BF),
            v((NZ * 64, HD), F32),
            v((NZ * 64, 2 * HD), F32),
            v((NZ, 80, HD), BF),
            v((NZ, 80, HD), BF),
            v((NY, NZ, 16, 4 * HD), BF),
            v((TP, NY * NZ, columns), F32),
            v((TP, NY * NZ, columns), BF),
            v((TP, NY * NZ, columns), BF),
            v((TP, NY * NZ, columns), BF),
            pltpu.SemaphoreType.DMA((N_SEM,)),
            pltpu.SemaphoreType.DMA((N_SEM,)),
            pltpu.SemaphoreType.DMA((12,)),
        ],
        compiler_params=pltpu.CompilerParams(
            collective_id=1, has_side_effects=True, vmem_limit_bytes=63 * 2**20
        ),
        name="star_attention",
    )(cq, ck, cv, blen, qq, qk, qv, qpos, w)
    return pl.pallas_call(
        finish,
        out_shape=tuple(jax.ShapeDtypeStruct(x.shape, x.dtype) for x in results),
        in_specs=[hbm, hbm],
        out_specs=(hbm, hbm),
        scratch_shapes=[v(x.shape, x.dtype) for x in results] + [pltpu.SemaphoreType.DMA((2 * COPIES + 2,))],
        compiler_params=pltpu.CompilerParams(vmem_limit_bytes=62 * 2**20),
        name="results",
    )(*results)


def solution(mesh):
    in_specs = (
        P("ctx", "tp"),
        P("ctx", "tp"),
        P("ctx", "tp"),
        P("ctx"),
        P("ctx", "tp"),
        P("ctx", "tp"),
        P("ctx", "tp"),
        P("ctx"),
        P("tp", "ctx"),
    )
    out_specs = (P("ctx", "tp"), P(None, "ctx"))
    return jax.shard_map(body, mesh=mesh, in_specs=in_specs, out_specs=out_specs, check_vma=False)
```

```python
import functools
import math

import jax
import jax.numpy as jnp
from jax import lax
from jax.experimental import pallas as pl
from jax.experimental.pallas import tpu as pltpu
from jax.sharding import PartitionSpec as P

MESH = pl.DeviceIdType.MESH
NT = (((1,), (1,)), ((), ()))
BF = jnp.bfloat16
F32 = jnp.float32
NEG = -1e30
HD = 128
HEADS = 8
NY, NZ, TP = 4, 8, 8
ROWS = 768
QROWS = 8
TILE = 256
NRB = ROWS // TILE
SL = ROWS * 2 // (NY * NZ)
THIRD = ROWS // 3
SCALE = math.log2(math.e) / math.sqrt(HD)
LOG2E = math.log2(math.e)
ZORDER = (3, 5, 4, 1, 7, 2, 6)
TORDER = (4, 3, 5, 2, 6, 1, 7)
ARRIVAL = (2, 6, 1, 7, 4, 3, 5)
YORDER = (1, 3, 2)
COPIES = 4
HG = 4

S_Q, S_SM, S_KV, S_AA, S_AC, S_AD = 0, 7, 11, 27, 34, 41
S_PZ, S_TZ, S_TY, S_RX, S_GX = 44, 51, 58, 82, 89
N_SEM = 96


def kernel(
    cq, ck, cv, blen, qq_hbm, qk_hbm, qv_hbm, qpos, w,
    out, ans,
    qq, qk, qv, cqv, wv, kvb, kk, va, akk, ava, bias,
    mo, acco, obuf,
    qbuf, sml, rst, akv,
    p2kk, p2va, m2, acc2,
    cmsg, crecv, abuf, pown, psend, prec, ansb,
    ss, rs, ls,
):
    ctx = lax.axis_index("ctx")
    t = lax.axis_index("tp")
    z = lax.rem(ctx, NZ)
    c = lax.rem(ctx // NZ + 2 * z, NY)

    def at_z(d):
        return lax.rem(z + d + NZ, NZ)

    def at_c(d):
        return lax.rem(c + d + NY, NY)

    def at_t(d):
        return lax.rem(t + d + TP, TP)

    def dev(cc, zz, tt):
        return (lax.rem(cc + 2 * zz, NY) * NZ + zz, tt)

    def z_to(d):
        return at_z(-1) if d == 2 else z

    def z_from(d):
        return at_z(1) if d == 2 else z

    def next_to(d):
        return dev(at_c(d), z_to(d), t)

    def remote(src, dst, si, ri, device):
        return pltpu.make_async_remote_copy(
            src_ref=src, dst_ref=dst, send_sem=ss.at[si], recv_sem=rs.at[ri],
            device_id=device, device_id_type=MESH,
        )

    def recv(dst, ri):
        remote(dst, dst, ri, ri, next_to(1)).wait_recv()

    sends = []

    def send(src, dst, si, device):
        copy = remote(src, dst, si, si, device)
        copy.start()
        sends.append(copy)

    barrier = pltpu.get_barrier_semaphore()
    peers = (
        [dev(c, at_z(d), t) for d in range(1, NZ)]
        + [dev(at_c(1), z, t), dev(at_c(3), z, t), dev(at_c(2), at_z(1), t), dev(at_c(2), at_z(-1), t)]
        + [dev(c, z, at_t(d)) for d in range(1, TP)]
    )
    for peer in peers:
        pl.semaphore_signal(barrier, inc=1, device_id=peer, device_id_type=MESH)
    small_loads = [
        pltpu.make_async_copy(src, dst, ls.at[n])
        for n, (src, dst) in enumerate(((qq_hbm, qq), (qk_hbm, qk), (qv_hbm, qv)))
    ]
    loads = [
        pltpu.make_async_copy(src, kvb.at[c, n], ls.at[3 + n]) for n, src in enumerate((ck, cv))
    ]
    load_q = pltpu.make_async_copy(cq, cqv, ls.at[5])
    load_w = pltpu.make_async_copy(w, wv, ls.at[6])
    for copy in small_loads + loads + [load_q, load_w]:
        copy.start()
    pl.semaphore_wait(barrier, len(peers))

    def key_parts(part):
        at, length = (0, 2 * THIRD) if part == 0 else (2 * THIRD, THIRD)
        whole, half = pl.ds(at, length), length // 2
        return (
            (whole, dev(at_c(1), z, t), at_c(-1)),
            (whole, dev(at_c(3), z, t), at_c(-3)),
            (pl.ds(at, half), dev(at_c(2), at_z(-1), t), at_c(2)),
            (pl.ds(at + half, half), dev(at_c(2), at_z(1), t), at_c(2)),
        )

    def send_keys(part):
        for n, src in enumerate((ck, cv)):
            for k, (rows, peer, _) in enumerate(key_parts(part)):
                send(src.at[rows], kvb.at[c, n, rows], S_KV + 8 * part + 4 * n + k, peer)

    send_keys(0)
    for copy in small_loads:
        copy.wait()

    row8 = lax.broadcasted_iota(jnp.int32, (8, HD), 0)
    lane8 = lax.broadcasted_iota(jnp.int32, (8, HD), 1)
    qf = qq[...].astype(F32)
    qbuf[z, 0:64, :] = jnp.concatenate([qf[:, h * HD:(h + 1) * HD] for h in range(HEADS)], axis=0).astype(BF)
    pos = jnp.zeros((8, HD), jnp.int32)
    key_pos = jnp.full((8, HD), 512, jnp.int32)
    for r in range(QROWS):
        pos = jnp.where(row8 == r, qpos[r], pos)
        key_pos = jnp.where(lane8 == c * QROWS + r, qpos[r], key_pos)
    pos = pos.astype(F32)
    key_pos = key_pos.astype(F32)
    qbuf[z, 64:80, :] = jnp.concatenate([pos, pos], axis=0).astype(BF)
    length = jnp.zeros((8, HD), jnp.int32) + blen[0]
    info = jnp.concatenate([length // 128, lax.rem(length, 128)], axis=0).astype(F32).astype(BF)
    sml[c, 0:16, :] = jnp.concatenate([qk[...].astype(F32), qv[...].astype(F32)], axis=0).astype(BF)
    sml[c, 16:32, :] = jnp.concatenate([key_pos, key_pos], axis=0).astype(BF)
    sml[c, 32:48, :] = info

    for d in ZORDER:
        send(qbuf.at[z], qbuf.at[z], S_Q + d - 1, dev(c, at_z(d), t))
    for d in YORDER:
        send(sml.at[c], sml.at[c], S_SM + d - 1, next_to(d))
    send(sml.at[c], sml.at[NY], S_SM + 3, dev(at_c(2), at_z(1), t))
    for copy in loads:
        copy.wait()

    row_of = lax.broadcasted_iota(jnp.int32, (THIRD, HD), 0)

    def live_keys(live, keys, other, values, to_kk, to_va, rows):
        to_kk[rows, :] = jnp.where(live, keys, other)
        to_va[rows, :HD] = jnp.where(live, values, jnp.zeros_like(values))
        to_va[rows, HD:] = jnp.where(live, 1.0, 0.0).astype(BF)

    for a in range(3):
        live_keys(
            row_of + a * THIRD < blen[0], kvb[c, 0, a * THIRD:(a + 1) * THIRD], kvb[c, 0, 0:1],
            kvb[c, 1, a * THIRD:(a + 1) * THIRD], kk, va, slice(a * THIRD, (a + 1) * THIRD),
        )
    rr = lax.broadcasted_iota(jnp.int32, (TILE, TILE), 0)
    cc = lax.broadcasted_iota(jnp.int32, (TILE, TILE), 1)
    bias[...] = jnp.where(cc <= rr, 0.0, NEG)
    load_q.wait()

    def own_step(rb, h):
        qt = cqv[rb * TILE:(rb + 1) * TILE, pl.ds(pl.multiple_of(h * HD, HD), HD)]
        diagonal = slice(rb * TILE, (rb + 1) * TILE)
        sd = lax.dot_general(qt, kk[diagonal], NT, preferred_element_type=F32) + bias[...]
        top = jnp.max(sd, axis=1, keepdims=True)
        if rb:
            so = lax.dot_general(qt, kk[0:rb * TILE], NT, preferred_element_type=F32)
            top = jnp.maximum(top, jnp.max(so, axis=1, keepdims=True))
        top_s = top * SCALE
        pd = jnp.exp2(sd * SCALE - top_s).astype(BF)
        acc = jnp.dot(pd, va[diagonal], preferred_element_type=F32)
        if rb:
            po = jnp.exp2(so * SCALE - top_s).astype(BF)
            acc = acc + jnp.dot(po, va[0:rb * TILE], preferred_element_type=F32)
        acco[rb * HEADS + h] = acc
        mo[rb * HEADS + h] = jnp.broadcast_to(top_s, (TILE, HD))

    def own_steps(rb):
        @pl.loop(0, HEADS // HG)
        def _(i):
            for u in range(HG):
                own_step(rb, i * HG + u)

    own_steps(0)

    own_steps(1)
    send_keys(1)
    own_steps(2)

    for d in range(1, NZ):
        recv(qbuf.at[at_z(-d)], S_Q + d - 1)
    for d in range(1, NY):
        recv(sml.at[at_c(-d)], S_SM + d - 1)
    recv(sml.at[NY], S_SM + 3)
    half = NZ // 2 * 64

    def asked(i):
        return jnp.concatenate([qbuf[i * 4 + j, 0:64, :] for j in range(4)], axis=0)

    small = [sml[j].astype(F32) for j in range(NY)]
    zero96 = jnp.zeros((HD - NY * QROWS, HD), F32)
    ext_k = jnp.concatenate([s[0:8] for s in small] + [zero96], axis=0).astype(BF)
    ext_v = jnp.concatenate([s[8:16] for s in small] + [zero96], axis=0).astype(BF)
    ext_va = jnp.concatenate([ext_v, jnp.ones((HD, HD), BF)], axis=1)
    ext_pos = functools.reduce(jnp.minimum, [s[16:17] for s in small])

    for i in range(2):
        qt = asked(i)
        rows_pos = jnp.concatenate(
            [p for j in range(4) for p in [qbuf[i * 4 + j, 64:80, :].astype(F32)[0:8]] * HEADS], axis=0
        )
        se = lax.dot_general(qt, ext_k, NT, preferred_element_type=F32)
        se = jnp.where(ext_pos <= rows_pos, se, NEG)
        sa = lax.dot_general(qt, kk[...], NT, preferred_element_type=F32)
        top = jnp.maximum(jnp.max(se, axis=1, keepdims=True), jnp.max(sa, axis=1, keepdims=True)) * SCALE
        acc = jnp.dot(jnp.exp2(sa * SCALE - top).astype(BF), va[...], preferred_element_type=F32)
        acc = acc + jnp.dot(jnp.exp2(se * SCALE - top).astype(BF), ext_va, preferred_element_type=F32)
        m2[i * half:(i + 1) * half] = jnp.broadcast_to(top, (half, HD))
        acc2[i * half:(i + 1) * half] = acc

    def length_of(slot):
        length = sml[slot, 32:48, :].astype(F32)
        return length[0:1] * 128.0 + length[8:9]

    def phase_two(thirds):
        at = 0
        below = length_of(NY)
        for d in range(1, NY):
            slot = at_c(-d)
            above = length_of(slot)
            for a in thirds:
                live_to = above
                if d == 2 and a:
                    live_to = jnp.where(row_of < THIRD // 2, above, below) if a == 2 else below
                live_keys(
                    (row_of + a * THIRD).astype(F32) < live_to, kvb[slot, 0, a * THIRD:(a + 1) * THIRD],
                    kvb[slot, 0, 0:1], kvb[slot, 1, a * THIRD:(a + 1) * THIRD], p2kk, p2va, slice(at, at + THIRD),
                )
                at += THIRD
        for i in range(2):
            part = slice(i * half, (i + 1) * half)
            sa = lax.dot_general(asked(i), p2kk[0:at], NT, preferred_element_type=F32)
            old = m2[part]
            top = jnp.maximum(jnp.max(sa, axis=1, keepdims=True) * SCALE, old)
            acc = jnp.dot(jnp.exp2(sa * SCALE - top[:, 0:1]).astype(BF), p2va[0:at], preferred_element_type=F32)
            keep = jnp.exp2(old - top)
            acc2[part] = acc + acc2[part] * jnp.concatenate([keep, keep], axis=1)
            m2[part] = top

    def recv_keys(part):
        for n in range(2):
            for k, (rows, _, slot) in enumerate(key_parts(part)):
                recv(kvb.at[slot, n, rows], S_KV + 8 * part + 4 * n + k)

    recv_keys(0)
    phase_two((0, 1))
    recv_keys(1)

    source_z = jnp.where(c == 2, NZ - 1, 0)

    @pl.when(z == source_z)
    def _():
        for j in range(NZ):
            row = pl.multiple_of(at_c(2) * (ROWS // 4) + j % 4 * SL, 16)
            rst[j, 0:SL, :] = kvb[0, j // 4, pl.ds(row, SL), :]
            rst[j, SL:SL + 16, :] = sml[0, 32:48, :]
        akv[c, z] = rst[z]
        for d in range(1, NZ):
            to_z = at_z(d)
            remote(rst.at[to_z], akv.at[c, to_z], S_AA + d - 1, S_AA, dev(c, to_z, t)).start()

    phase_two((2,))

    total = acc2[:, HD:]
    lse = m2[...] + jnp.log(total) * LOG2E
    part_out = acc2[:, :HD] / total
    for j in range(NZ):
        compact = jnp.zeros((8, HD), F32)
        for h in range(HEADS):
            compact = jnp.where(lane8 == h, lse[j * 64 + h * 8:j * 64 + h * 8 + 8], compact)
        high = compact.astype(BF).astype(F32)
        middle = (compact - high).astype(BF).astype(F32)
        low = compact - high - middle
        cmsg[j, 0:64, :] = part_out[j * 64:(j + 1) * 64].astype(BF)
        pieces = high + pltpu.roll(middle, 8, 1) + pltpu.roll(low, 16, 1)
        cmsg[j, 64:80, :] = jnp.concatenate([pieces, pieces], axis=0).astype(BF)
    for d in ZORDER:
        send(cmsg.at[at_z(d)], crecv.at[z], S_PZ + d - 1, dev(c, at_z(d), t))

    @pl.when(z != source_z)
    def _():
        recv(akv.at[c, z], S_AA)

    for d in ZORDER:
        send(akv.at[c, z], akv.at[c, z], S_AC + d - 1, dev(c, at_z(d), t))


    for d in range(1, NZ):
        recv(crecv.at[at_z(-d)], S_PZ + d - 1)
    parts = [cmsg[z].astype(F32)] + [crecv[at_z(-d)].astype(F32) for d in range(1, NZ)]
    lses = [p[64:72] + pltpu.roll(p[64:72], HD - 8, 1) + pltpu.roll(p[64:72], HD - 16, 1) for p in parts]
    top = functools.reduce(jnp.maximum, lses)
    weights = [jnp.exp2(x - top) for x in lses]
    weight_sum = functools.reduce(jnp.add, weights)
    weights = [x / weight_sum for x in weights]
    merged = []
    for h in range(HEADS):
        merged.append(functools.reduce(
            jnp.add, [x[:, h:h + 1] * p[h * 8:h * 8 + 8] for x, p in zip(weights, parts)]
        ))
    merged = jnp.concatenate(
        [jnp.concatenate(merged[0:4], axis=1), jnp.concatenate(merged[4:8], axis=1)], axis=0
    )
    abuf[c, z] = merged.astype(BF)

    for d in ZORDER:
        send(abuf.at[c, z], abuf.at[c, z], S_TZ + d - 1, dev(c, at_z(d), t))

    def pass_on(k):
        zz = at_z(-k)
        if k:
            recv(abuf.at[c, zz], S_TZ + k - 1)
        for d in YORDER:
            send(abuf.at[c, zz], abuf.at[c, zz], S_TY + 3 * k + d - 1, next_to(d))

    pass_on(0)
    for d in range(1, NZ):
        recv(akv.at[c, at_z(-d)], S_AC + d - 1)
    data = pl.ds(0, SL)
    for d in YORDER:
        send(akv.at[c, :, data], akv.at[c, :, data], S_AD + d - 1, next_to(d))

    for k in ARRIVAL:
        pass_on(k)

    def anchor_step(i):
        cols = pl.ds(pl.multiple_of(lax.rem(i, HEADS) * HD, HD), HD)
        rows = pl.ds(pl.multiple_of(i // HEADS * TILE, TILE), TILE)
        sa = lax.dot_general(cqv[rows, cols], akk[...], NT, preferred_element_type=F32)
        old = mo[i]
        top = jnp.maximum(jnp.max(sa, axis=1, keepdims=True) * SCALE, old)
        acc = jnp.dot(jnp.exp2(sa * SCALE - top[:, 0:1]).astype(BF), ava[...], preferred_element_type=F32)
        keep = jnp.exp2(old - top)
        acc = acc + acco[i] * jnp.concatenate([keep, keep], axis=1)
        obuf[rows, cols] = (acc[:, :HD] / acc[:, HD:]).astype(BF)

    stores = [
        pltpu.make_async_copy(obuf.at[pl.ds(rb * TILE, TILE)], out.at[pl.ds(rb * TILE, TILE)], ls.at[rb])
        for rb in range(NRB)
    ]

    def anchor_steps(start, steps):
        @pl.loop(0, 2)
        def _(i):
            for u in range(steps // 2):
                anchor_step(start + i * (steps // 2) + u)

    for d in range(1, NY):
        recv(akv.at[at_c(-d), :, data], S_AD + d - 1)
    alen = akv[c, z, SL:SL + 16, :].astype(F32)
    alive_to = jnp.where(ctx == 0, 0.0, alen[0:1] * 128.0 + alen[8:9])
    anchor_k, anchor_v = (
        jnp.concatenate([akv[(p + 2) % 4, n:n + 4, 0:SL, :].reshape(4 * SL, HD) for p in range(4)], axis=0)
        for n in (0, 4)
    )
    for a in range(3):
        part = slice(a * THIRD, (a + 1) * THIRD)
        live_keys(
            (row_of + a * THIRD).astype(F32) < alive_to, anchor_k[part], anchor_k[0:1], anchor_v[part],
            akk, ava, part,
        )

    anchor_steps(0, 4)
    load_w.wait()
    for k in range(NZ):
        for d in range(1, NY):
            recv(abuf.at[at_c(-d), lax.rem(z_from(d) - k + NZ, NZ)], S_TY + 3 * k + d - 1)

    rows = jnp.concatenate([abuf[(yy + 2 * zz) % NY, zz] for yy in range(NY) for zz in range(NZ)], axis=0)
    upper = jnp.dot(rows, wv[0:4 * HD], preferred_element_type=F32).reshape(NY * NZ, 16, -1)
    lower = jnp.dot(rows, wv[4 * HD:], preferred_element_type=F32).reshape(NY * NZ, 16, -1)
    partial = (upper[:, 0:8] + lower[:, 8:16]).reshape(pown.shape)
    pown[...] = partial
    psend[...] = partial.astype(BF)
    for d in TORDER:
        send(psend.at[at_t(d)], prec.at[t], S_RX + d - 1, dev(c, z, at_t(d)))
    anchor_steps(4, 12)
    stores[0].start()
    stores[1].start()
    for d in range(1, TP):
        recv(prec.at[at_t(-d)], S_RX + d - 1)
    answer = pown[t]
    for d in range(1, TP):
        answer = answer + prec[at_t(-d)].astype(F32)
    ansb[t] = answer.astype(BF)
    for d in TORDER:
        send(ansb.at[t], ansb.at[t], S_GX + d - 1, dev(c, z, at_t(d)))
    anchor_steps(16, 8)
    stores[2].start()
    for d in range(1, TP):
        recv(ansb.at[at_t(-d)], S_GX + d - 1)
    ans[...] = ansb[...].reshape(ans.shape)

    for copy in sends:
        copy.wait_send()

    @pl.when(z == source_z)
    def _():
        for d in range(1, NZ):
            to_z = at_z(d)
            remote(rst.at[to_z], akv.at[c, to_z], S_AA + d - 1, S_AA, dev(c, to_z, t)).wait_send()

    for copy in stores:
        copy.wait()


def finish(block, answer, block_out, answer_out, held, held_answer, sem):
    rows = ROWS // COPIES
    pieces = [(block, held, block_out, pl.ds(i * rows, rows)) for i in range(COPIES)]
    pieces.append((answer, held_answer, answer_out, pl.ds(0, answer.shape[0])))
    loads = [
        pltpu.make_async_copy(src.at[at], here.at[at], sem.at[2 * i]) for i, (src, here, _, at) in enumerate(pieces)
    ]
    stores = [
        pltpu.make_async_copy(here.at[at], dst.at[at], sem.at[2 * i + 1])
        for i, (_, here, dst, at) in enumerate(pieces)
    ]
    for copy in loads:
        copy.start()
    for load, store in zip(loads, stores):
        load.wait()
        store.start()
    for copy in stores:
        copy.wait()


def body(cq, ck, cv, blen, qq, qk, qv, qpos, w):
    hbm = pl.BlockSpec(memory_space=pl.ANY)
    vmem = pl.BlockSpec(memory_space=pltpu.VMEM)
    smem = pl.BlockSpec(memory_space=pltpu.SMEM)
    columns = w.shape[1]
    v = pltpu.VMEM
    results = pl.pallas_call(
        kernel,
        out_shape=(
            jax.ShapeDtypeStruct(cq.shape, BF),
            jax.ShapeDtypeStruct((NY * NZ * QROWS, columns), BF),
        ),
        in_specs=[hbm, hbm, hbm, smem, hbm, hbm, hbm, smem, hbm],
        out_specs=(hbm, vmem),
        scratch_shapes=[
            v(qq.shape, BF),
            v(qk.shape, BF),
            v(qv.shape, BF),
            v(cq.shape, BF),
            v(w.shape, BF),
            v((NY, 2, ROWS, HD), BF),
            v((ROWS, HD), BF),
            v((ROWS, 2 * HD), BF),
            v((ROWS, HD), BF),
            v((ROWS, 2 * HD), BF),
            v((TILE, TILE), F32),
            v((NRB * HEADS, TILE, HD), F32),
            v((NRB * HEADS, TILE, 2 * HD), F32),
            v(cq.shape, BF),
            v((NZ, 80, HD), BF),
            v((NY + 1, 48, HD), BF),
            v((NZ, SL + 16, HD), BF),
            v((4, NZ, SL + 16, HD), BF),
            v((2 * ROWS, HD), BF),
            v((2 * ROWS, 2 * HD), BF),
            v((NZ * 64, HD), F32),
            v((NZ * 64, 2 * HD), F32),
            v((NZ, 80, HD), BF),
            v((NZ, 80, HD), BF),
            v((NY, NZ, 16, 4 * HD), BF),
            v((TP, NY * NZ, columns), F32),
            v((TP, NY * NZ, columns), BF),
            v((TP, NY * NZ, columns), BF),
            v((TP, NY * NZ, columns), BF),
            pltpu.SemaphoreType.DMA((N_SEM,)),
            pltpu.SemaphoreType.DMA((N_SEM,)),
            pltpu.SemaphoreType.DMA((12,)),
        ],
        compiler_params=pltpu.CompilerParams(
            collective_id=1, has_side_effects=True, vmem_limit_bytes=63 * 2**20
        ),
        name="star_attention",
    )(cq, ck, cv, blen, qq, qk, qv, qpos, w)
    return pl.pallas_call(
        finish,
        out_shape=tuple(jax.ShapeDtypeStruct(x.shape, x.dtype) for x in results),
        in_specs=[hbm, hbm],
        out_specs=(hbm, hbm),
        scratch_shapes=[v(x.shape, x.dtype) for x in results] + [pltpu.SemaphoreType.DMA((2 * COPIES + 2,))],
        compiler_params=pltpu.CompilerParams(vmem_limit_bytes=62 * 2**20),
        name="results",
    )(*results)


def solution(mesh):
    in_specs = (
        P("ctx", "tp"),
        P("ctx", "tp"),
        P("ctx", "tp"),
        P("ctx"),
        P("ctx", "tp"),
        P("ctx", "tp"),
        P("ctx", "tp"),
        P("ctx"),
        P("tp", "ctx"),
    )
    out_specs = (P("ctx", "tp"), P(None, "ctx"))
    return jax.shard_map(body, mesh=mesh, in_specs=in_specs, out_specs=out_specs, check_vma=False)
```

```python
import functools
import math

import jax
import jax.numpy as jnp
from jax import lax
from jax.experimental import pallas as pl
from jax.experimental.pallas import tpu as pltpu
from jax.sharding import PartitionSpec as P

MESH = pl.DeviceIdType.MESH
NT = (((1,), (1,)), ((), ()))
BF = jnp.bfloat16
F32 = jnp.float32
NEG = -1e30
HD = 128
HEADS = 8
NY, NZ, TP = 4, 8, 8
ROWS = 768
QROWS = 8
TILE = 256
NRB = ROWS // TILE
SL = ROWS * 2 // (NY * NZ)
THIRD = ROWS // 3
SCALE = math.log2(math.e) / math.sqrt(HD)
LOG2E = math.log2(math.e)
ZORDER = (3, 5, 4, 1, 7, 2, 6)
TORDER = (4, 3, 5, 2, 6, 1, 7)
ARRIVAL = (2, 6, 1, 7, 4, 3, 5)
YORDER = (1, 3, 2)
COPIES = 4
HG = 4

S_Q, S_SM, S_KV, S_AA, S_AC, S_AD = 0, 7, 11, 27, 34, 41
S_PZ, S_TZ, S_TY, S_RX, S_GX = 44, 51, 58, 82, 89
N_SEM = 96


def kernel(
    cq, ck, cv, blen, qq_hbm, qk_hbm, qv_hbm, qpos, w,
    out, ans,
    qq, qk, qv, cqv, wv, kvb, kk, va, akk, ava, bias,
    mo, acco, obuf,
    qbuf, sml, rst, akv,
    p2kk, p2va, m2, acc2,
    cmsg, crecv, abuf, pown, psend, prec, ansb,
    ss, rs, ls,
):
    ctx = lax.axis_index("ctx")
    t = lax.axis_index("tp")
    z = lax.rem(ctx, NZ)
    c = lax.rem(ctx // NZ + 2 * z, NY)

    def at_z(d):
        return lax.rem(z + d + NZ, NZ)

    def at_c(d):
        return lax.rem(c + d + NY, NY)

    def at_t(d):
        return lax.rem(t + d + TP, TP)

    def dev(cc, zz, tt):
        return (lax.rem(cc + 2 * zz, NY) * NZ + zz, tt)

    def z_to(d):
        return at_z(-1) if d == 2 else z

    def z_from(d):
        return at_z(1) if d == 2 else z

    def next_to(d):
        return dev(at_c(d), z_to(d), t)

    def remote(src, dst, si, ri, device):
        return pltpu.make_async_remote_copy(
            src_ref=src, dst_ref=dst, send_sem=ss.at[si], recv_sem=rs.at[ri],
            device_id=device, device_id_type=MESH,
        )

    def recv(dst, ri):
        remote(dst, dst, ri, ri, next_to(1)).wait_recv()

    sends = []

    def send(src, dst, si, device):
        copy = remote(src, dst, si, si, device)
        copy.start()
        sends.append(copy)

    barrier = pltpu.get_barrier_semaphore()
    peers = (
        [dev(c, at_z(d), t) for d in range(1, NZ)]
        + [dev(at_c(1), z, t), dev(at_c(3), z, t), dev(at_c(2), at_z(1), t), dev(at_c(2), at_z(-1), t)]
        + [dev(c, z, at_t(d)) for d in range(1, TP)]
    )
    for peer in peers:
        pl.semaphore_signal(barrier, inc=1, device_id=peer, device_id_type=MESH)
    small_loads = [
        pltpu.make_async_copy(src, dst, ls.at[n])
        for n, (src, dst) in enumerate(((qq_hbm, qq), (qk_hbm, qk), (qv_hbm, qv)))
    ]
    loads = [
        pltpu.make_async_copy(src, kvb.at[c, n], ls.at[3 + n]) for n, src in enumerate((ck, cv))
    ]
    load_q = pltpu.make_async_copy(cq, cqv, ls.at[5])
    load_w = pltpu.make_async_copy(w, wv, ls.at[6])
    for copy in small_loads + loads + [load_q, load_w]:
        copy.start()
    pl.semaphore_wait(barrier, len(peers))

    def key_parts(part):
        at, length = (0, 2 * THIRD) if part == 0 else (2 * THIRD, THIRD)
        whole, half = pl.ds(at, length), length // 2
        return (
            (whole, dev(at_c(1), z, t), at_c(-1)),
            (whole, dev(at_c(3), z, t), at_c(-3)),
            (pl.ds(at, half), dev(at_c(2), at_z(-1), t), at_c(2)),
            (pl.ds(at + half, half), dev(at_c(2), at_z(1), t), at_c(2)),
        )

    def send_keys(part):
        for n, src in enumerate((ck, cv)):
            for k, (rows, peer, _) in enumerate(key_parts(part)):
                send(src.at[rows], kvb.at[c, n, rows], S_KV + 8 * part + 4 * n + k, peer)

    send_keys(0)
    for copy in small_loads:
        copy.wait()

    row8 = lax.broadcasted_iota(jnp.int32, (8, HD), 0)
    lane8 = lax.broadcasted_iota(jnp.int32, (8, HD), 1)
    qf = qq[...].astype(F32)
    qbuf[z, 0:64, :] = jnp.concatenate([qf[:, h * HD:(h + 1) * HD] for h in range(HEADS)], axis=0).astype(BF)
    pos = jnp.zeros((8, HD), jnp.int32)
    key_pos = jnp.full((8, HD), 512, jnp.int32)
    for r in range(QROWS):
        pos = jnp.where(row8 == r, qpos[r], pos)
        key_pos = jnp.where(lane8 == c * QROWS + r, qpos[r], key_pos)
    pos = pos.astype(F32)
    key_pos = key_pos.astype(F32)
    qbuf[z, 64:80, :] = jnp.concatenate([pos, pos], axis=0).astype(BF)
    length = jnp.zeros((8, HD), jnp.int32) + blen[0]
    info = jnp.concatenate([length // 128, lax.rem(length, 128)], axis=0).astype(F32).astype(BF)
    sml[c, 0:16, :] = jnp.concatenate([qk[...].astype(F32), qv[...].astype(F32)], axis=0).astype(BF)
    sml[c, 16:32, :] = jnp.concatenate([key_pos, key_pos], axis=0).astype(BF)
    sml[c, 32:48, :] = info

    for d in ZORDER:
        send(qbuf.at[z], qbuf.at[z], S_Q + d - 1, dev(c, at_z(d), t))
    for d in YORDER:
        send(sml.at[c], sml.at[c], S_SM + d - 1, next_to(d))
    send(sml.at[c], sml.at[NY], S_SM + 3, dev(at_c(2), at_z(1), t))
    for copy in loads:
        copy.wait()

    row_of = lax.broadcasted_iota(jnp.int32, (THIRD, HD), 0)

    def live_keys(live, keys, other, values, to_kk, to_va, rows):
        to_kk[rows, :] = jnp.where(live, keys, other)
        to_va[rows, :HD] = jnp.where(live, values, jnp.zeros_like(values))
        to_va[rows, HD:] = jnp.where(live, 1.0, 0.0).astype(BF)

    for a in range(3):
        live_keys(
            row_of + a * THIRD < blen[0], kvb[c, 0, a * THIRD:(a + 1) * THIRD], kvb[c, 0, 0:1],
            kvb[c, 1, a * THIRD:(a + 1) * THIRD], kk, va, slice(a * THIRD, (a + 1) * THIRD),
        )
    rr = lax.broadcasted_iota(jnp.int32, (TILE, TILE), 0)
    cc = lax.broadcasted_iota(jnp.int32, (TILE, TILE), 1)
    bias[...] = jnp.where(cc <= rr, 0.0, NEG)
    load_q.wait()

    def own_step(rb, h):
        qt = cqv[rb * TILE:(rb + 1) * TILE, pl.ds(pl.multiple_of(h * HD, HD), HD)]
        diagonal = slice(rb * TILE, (rb + 1) * TILE)
        sd = lax.dot_general(qt, kk[diagonal], NT, preferred_element_type=F32) + bias[...]
        top = jnp.max(sd, axis=1, keepdims=True)
        if rb:
            so = lax.dot_general(qt, kk[0:rb * TILE], NT, preferred_element_type=F32)
            top = jnp.maximum(top, jnp.max(so, axis=1, keepdims=True))
        top_s = top * SCALE
        pd = jnp.exp2(sd * SCALE - top_s).astype(BF)
        acc = jnp.dot(pd, va[diagonal], preferred_element_type=F32)
        if rb:
            po = jnp.exp2(so * SCALE - top_s).astype(BF)
            acc = acc + jnp.dot(po, va[0:rb * TILE], preferred_element_type=F32)
        acco[rb * HEADS + h] = acc
        mo[rb * HEADS + h] = jnp.broadcast_to(top_s, (TILE, HD))

    def own_steps(rb):
        @pl.loop(0, HEADS // HG)
        def _(i):
            for u in range(HG):
                own_step(rb, i * HG + u)

    own_steps(0)

    own_steps(1)
    send_keys(1)
    own_steps(2)

    for d in range(1, NZ):
        recv(qbuf.at[at_z(-d)], S_Q + d - 1)
    for d in range(1, NY):
        recv(sml.at[at_c(-d)], S_SM + d - 1)
    recv(sml.at[NY], S_SM + 3)
    half = NZ // 2 * 64

    def asked(i):
        return jnp.concatenate([qbuf[i * 4 + j, 0:64, :] for j in range(4)], axis=0)

    small = [sml[j].astype(F32) for j in range(NY)]
    zero96 = jnp.zeros((HD - NY * QROWS, HD), F32)
    ext_k = jnp.concatenate([s[0:8] for s in small] + [zero96], axis=0).astype(BF)
    ext_v = jnp.concatenate([s[8:16] for s in small] + [zero96], axis=0).astype(BF)
    ext_va = jnp.concatenate([ext_v, jnp.ones((HD, HD), BF)], axis=1)
    ext_pos = functools.reduce(jnp.minimum, [s[16:17] for s in small])

    for i in range(2):
        qt = asked(i)
        rows_pos = jnp.concatenate(
            [p for j in range(4) for p in [qbuf[i * 4 + j, 64:80, :].astype(F32)[0:8]] * HEADS], axis=0
        )
        se = lax.dot_general(qt, ext_k, NT, preferred_element_type=F32)
        se = jnp.where(ext_pos <= rows_pos, se, NEG)
        sa = lax.dot_general(qt, kk[...], NT, preferred_element_type=F32)
        top = jnp.maximum(jnp.max(se, axis=1, keepdims=True), jnp.max(sa, axis=1, keepdims=True)) * SCALE
        acc = jnp.dot(jnp.exp2(sa * SCALE - top).astype(BF), va[...], preferred_element_type=F32)
        acc = acc + jnp.dot(jnp.exp2(se * SCALE - top).astype(BF), ext_va, preferred_element_type=F32)
        m2[i * half:(i + 1) * half] = jnp.broadcast_to(top, (half, HD))
        acc2[i * half:(i + 1) * half] = acc

    def length_of(slot):
        length = sml[slot, 32:48, :].astype(F32)
        return length[0:1] * 128.0 + length[8:9]

    def phase_two(thirds):
        at = 0
        below = length_of(NY)
        for d in range(1, NY):
            slot = at_c(-d)
            above = length_of(slot)
            for a in thirds:
                live_to = above
                if d == 2 and a:
                    live_to = jnp.where(row_of < THIRD // 2, above, below) if a == 2 else below
                live_keys(
                    (row_of + a * THIRD).astype(F32) < live_to, kvb[slot, 0, a * THIRD:(a + 1) * THIRD],
                    kvb[slot, 0, 0:1], kvb[slot, 1, a * THIRD:(a + 1) * THIRD], p2kk, p2va, slice(at, at + THIRD),
                )
                at += THIRD
        for i in range(2):
            part = slice(i * half, (i + 1) * half)
            sa = lax.dot_general(asked(i), p2kk[0:at], NT, preferred_element_type=F32)
            old = m2[part]
            top = jnp.maximum(jnp.max(sa, axis=1, keepdims=True) * SCALE, old)
            acc = jnp.dot(jnp.exp2(sa * SCALE - top[:, 0:1]).astype(BF), p2va[0:at], preferred_element_type=F32)
            keep = jnp.exp2(old - top)
            acc2[part] = acc + acc2[part] * jnp.concatenate([keep, keep], axis=1)
            m2[part] = top

    def recv_keys(part):
        for n in range(2):
            for k, (rows, _, slot) in enumerate(key_parts(part)):
                recv(kvb.at[slot, n, rows], S_KV + 8 * part + 4 * n + k)

    recv_keys(0)
    phase_two((0, 1))
    recv_keys(1)

    source_z = jnp.where(c == 2, NZ - 1, 0)

    @pl.when(z == source_z)
    def _():
        for j in range(NZ):
            row = pl.multiple_of(at_c(2) * (ROWS // 4) + j % 4 * SL, 16)
            rst[j, 0:SL, :] = kvb[0, j // 4, pl.ds(row, SL), :]
            rst[j, SL:SL + 16, :] = sml[0, 32:48, :]
        akv[c, z] = rst[z]
        for d in range(1, NZ):
            to_z = at_z(d)
            remote(rst.at[to_z], akv.at[c, to_z], S_AA + d - 1, S_AA, dev(c, to_z, t)).start()

    phase_two((2,))

    def pack(j):
        at = pl.ds(pl.multiple_of(j * 64, 64), 64)
        acc = acc2[at, :]
        total = acc[:, HD:]
        lse = m2[at, :] + jnp.log(total) * LOG2E
        compact = jnp.zeros((8, HD), F32)
        for h in range(HEADS):
            compact = jnp.where(lane8 == h, lse[h * 8:h * 8 + 8], compact)
        high = compact.astype(BF).astype(F32)
        middle = (compact - high).astype(BF).astype(F32)
        low = compact - high - middle
        cmsg[j, 0:64, :] = (acc[:, :HD] / total).astype(BF)
        pieces = high + pltpu.roll(middle, 8, 1) + pltpu.roll(low, 16, 1)
        cmsg[j, 64:80, :] = jnp.concatenate([pieces, pieces], axis=0).astype(BF)

    for d in ZORDER:
        pack(at_z(d))
        send(cmsg.at[at_z(d)], crecv.at[z], S_PZ + d - 1, dev(c, at_z(d), t))
    pack(z)

    @pl.when(z != source_z)
    def _():
        recv(akv.at[c, z], S_AA)

    for d in ZORDER:
        send(akv.at[c, z], akv.at[c, z], S_AC + d - 1, dev(c, at_z(d), t))


    for d in range(1, NZ):
        recv(crecv.at[at_z(-d)], S_PZ + d - 1)
    parts = [cmsg[z].astype(F32)] + [crecv[at_z(-d)].astype(F32) for d in range(1, NZ)]
    lses = [p[64:72] + pltpu.roll(p[64:72], HD - 8, 1) + pltpu.roll(p[64:72], HD - 16, 1) for p in parts]
    top = functools.reduce(jnp.maximum, lses)
    weights = [jnp.exp2(x - top) for x in lses]
    weight_sum = functools.reduce(jnp.add, weights)
    weights = [x / weight_sum for x in weights]
    merged = []
    for h in range(HEADS):
        merged.append(functools.reduce(
            jnp.add, [x[:, h:h + 1] * p[h * 8:h * 8 + 8] for x, p in zip(weights, parts)]
        ))
    merged = jnp.concatenate(
        [jnp.concatenate(merged[0:4], axis=1), jnp.concatenate(merged[4:8], axis=1)], axis=0
    )
    abuf[c, z] = merged.astype(BF)

    for d in ZORDER:
        send(abuf.at[c, z], abuf.at[c, z], S_TZ + d - 1, dev(c, at_z(d), t))

    def pass_on(k):
        zz = at_z(-k)
        if k:
            recv(abuf.at[c, zz], S_TZ + k - 1)
        for d in YORDER:
            send(abuf.at[c, zz], abuf.at[c, zz], S_TY + 3 * k + d - 1, next_to(d))

    pass_on(0)
    for d in range(1, NZ):
        recv(akv.at[c, at_z(-d)], S_AC + d - 1)
    data = pl.ds(0, SL)
    for d in YORDER:
        send(akv.at[c, :, data], akv.at[c, :, data], S_AD + d - 1, next_to(d))

    for k in ARRIVAL:
        pass_on(k)

    def anchor_step(i):
        cols = pl.ds(pl.multiple_of(lax.rem(i, HEADS) * HD, HD), HD)
        rows = pl.ds(pl.multiple_of(i // HEADS * TILE, TILE), TILE)
        sa = lax.dot_general(cqv[rows, cols], akk[...], NT, preferred_element_type=F32)
        old = mo[i]
        top = jnp.maximum(jnp.max(sa, axis=1, keepdims=True) * SCALE, old)
        acc = jnp.dot(jnp.exp2(sa * SCALE - top[:, 0:1]).astype(BF), ava[...], preferred_element_type=F32)
        keep = jnp.exp2(old - top)
        acc = acc + acco[i] * jnp.concatenate([keep, keep], axis=1)
        obuf[rows, cols] = (acc[:, :HD] / acc[:, HD:]).astype(BF)

    stores = [
        pltpu.make_async_copy(obuf.at[pl.ds(rb * TILE, TILE)], out.at[pl.ds(rb * TILE, TILE)], ls.at[rb])
        for rb in range(NRB)
    ]

    def anchor_steps(start, steps):
        @pl.loop(0, 2)
        def _(i):
            for u in range(steps // 2):
                anchor_step(start + i * (steps // 2) + u)

    for d in range(1, NY):
        recv(akv.at[at_c(-d), :, data], S_AD + d - 1)
    alen = akv[c, z, SL:SL + 16, :].astype(F32)
    alive_to = jnp.where(ctx == 0, 0.0, alen[0:1] * 128.0 + alen[8:9])
    anchor_k, anchor_v = (
        jnp.concatenate([akv[(p + 2) % 4, n:n + 4, 0:SL, :].reshape(4 * SL, HD) for p in range(4)], axis=0)
        for n in (0, 4)
    )
    for a in range(3):
        part = slice(a * THIRD, (a + 1) * THIRD)
        live_keys(
            (row_of + a * THIRD).astype(F32) < alive_to, anchor_k[part], anchor_k[0:1], anchor_v[part],
            akk, ava, part,
        )

    anchor_steps(0, 4)
    load_w.wait()
    for k in range(NZ):
        for d in range(1, NY):
            recv(abuf.at[at_c(-d), lax.rem(z_from(d) - k + NZ, NZ)], S_TY + 3 * k + d - 1)

    rows = jnp.concatenate([abuf[(yy + 2 * zz) % NY, zz] for yy in range(NY) for zz in range(NZ)], axis=0)
    upper = jnp.dot(rows, wv[0:4 * HD], preferred_element_type=F32).reshape(NY * NZ, 16, -1)
    lower = jnp.dot(rows, wv[4 * HD:], preferred_element_type=F32).reshape(NY * NZ, 16, -1)
    partial = (upper[:, 0:8] + lower[:, 8:16]).reshape(pown.shape)
    pown[...] = partial
    psend[...] = partial.astype(BF)
    for d in TORDER:
        send(psend.at[at_t(d)], prec.at[t], S_RX + d - 1, dev(c, z, at_t(d)))
    anchor_steps(4, 12)
    stores[0].start()
    stores[1].start()
    for d in range(1, TP):
        recv(prec.at[at_t(-d)], S_RX + d - 1)
    answer = pown[t]
    for d in range(1, TP):
        answer = answer + prec[at_t(-d)].astype(F32)
    ansb[t] = answer.astype(BF)
    for d in TORDER:
        send(ansb.at[t], ansb.at[t], S_GX + d - 1, dev(c, z, at_t(d)))
    anchor_steps(16, 8)
    stores[2].start()
    for d in range(1, TP):
        recv(ansb.at[at_t(-d)], S_GX + d - 1)
    ans[...] = ansb[...].reshape(ans.shape)

    for copy in sends:
        copy.wait_send()

    @pl.when(z == source_z)
    def _():
        for d in range(1, NZ):
            to_z = at_z(d)
            remote(rst.at[to_z], akv.at[c, to_z], S_AA + d - 1, S_AA, dev(c, to_z, t)).wait_send()

    for copy in stores:
        copy.wait()


def finish(block, answer, block_out, answer_out, held, held_answer, sem):
    rows = ROWS // COPIES
    pieces = [(block, held, block_out, pl.ds(i * rows, rows)) for i in range(COPIES)]
    pieces.append((answer, held_answer, answer_out, pl.ds(0, answer.shape[0])))
    loads = [
        pltpu.make_async_copy(src.at[at], here.at[at], sem.at[2 * i]) for i, (src, here, _, at) in enumerate(pieces)
    ]
    stores = [
        pltpu.make_async_copy(here.at[at], dst.at[at], sem.at[2 * i + 1])
        for i, (_, here, dst, at) in enumerate(pieces)
    ]
    for copy in loads:
        copy.start()
    for load, store in zip(loads, stores):
        load.wait()
        store.start()
    for copy in stores:
        copy.wait()


def body(cq, ck, cv, blen, qq, qk, qv, qpos, w):
    hbm = pl.BlockSpec(memory_space=pl.ANY)
    vmem = pl.BlockSpec(memory_space=pltpu.VMEM)
    smem = pl.BlockSpec(memory_space=pltpu.SMEM)
    columns = w.shape[1]
    v = pltpu.VMEM
    results = pl.pallas_call(
        kernel,
        out_shape=(
            jax.ShapeDtypeStruct(cq.shape, BF),
            jax.ShapeDtypeStruct((NY * NZ * QROWS, columns), BF),
        ),
        in_specs=[hbm, hbm, hbm, smem, hbm, hbm, hbm, smem, hbm],
        out_specs=(hbm, vmem),
        scratch_shapes=[
            v(qq.shape, BF),
            v(qk.shape, BF),
            v(qv.shape, BF),
            v(cq.shape, BF),
            v(w.shape, BF),
            v((NY, 2, ROWS, HD), BF),
            v((ROWS, HD), BF),
            v((ROWS, 2 * HD), BF),
            v((ROWS, HD), BF),
            v((ROWS, 2 * HD), BF),
            v((TILE, TILE), F32),
            v((NRB * HEADS, TILE, HD), F32),
            v((NRB * HEADS, TILE, 2 * HD), F32),
            v(cq.shape, BF),
            v((NZ, 80, HD), BF),
            v((NY + 1, 48, HD), BF),
            v((NZ, SL + 16, HD), BF),
            v((4, NZ, SL + 16, HD), BF),
            v((2 * ROWS, HD), BF),
            v((2 * ROWS, 2 * HD), BF),
            v((NZ * 64, HD), F32),
            v((NZ * 64, 2 * HD), F32),
            v((NZ, 80, HD), BF),
            v((NZ, 80, HD), BF),
            v((NY, NZ, 16, 4 * HD), BF),
            v((TP, NY * NZ, columns), F32),
            v((TP, NY * NZ, columns), BF),
            v((TP, NY * NZ, columns), BF),
            v((TP, NY * NZ, columns), BF),
            pltpu.SemaphoreType.DMA((N_SEM,)),
            pltpu.SemaphoreType.DMA((N_SEM,)),
            pltpu.SemaphoreType.DMA((12,)),
        ],
        compiler_params=pltpu.CompilerParams(
            collective_id=1, has_side_effects=True, vmem_limit_bytes=63 * 2**20
        ),
        name="star_attention",
    )(cq, ck, cv, blen, qq, qk, qv, qpos, w)
    return pl.pallas_call(
        finish,
        out_shape=tuple(jax.ShapeDtypeStruct(x.shape, x.dtype) for x in results),
        in_specs=[hbm, hbm],
        out_specs=(hbm, hbm),
        scratch_shapes=[v(x.shape, x.dtype) for x in results] + [pltpu.SemaphoreType.DMA((2 * COPIES + 2,))],
        compiler_params=pltpu.CompilerParams(vmem_limit_bytes=62 * 2**20),
        name="results",
    )(*results)


def solution(mesh):
    in_specs = (
        P("ctx", "tp"),
        P("ctx", "tp"),
        P("ctx", "tp"),
        P("ctx"),
        P("ctx", "tp"),
        P("ctx", "tp"),
        P("ctx", "tp"),
        P("ctx"),
        P("tp", "ctx"),
    )
    out_specs = (P("ctx", "tp"), P(None, "ctx"))
    return jax.shard_map(body, mesh=mesh, in_specs=in_specs, out_specs=out_specs, check_vma=False)
```
